128 devices in a mesh: xy: 32 (over z, x, core), lev: 4 (over y).
Axes of the slice: x: 4, y: 4, z: 4, core: 2. Of those that a mesh axis runs over, the one named last changes fastest.
Arguments:
- euler_field: float32 [8, 128, 256, 256], P(None, 'lev', 'xy'), may hold values from 0.1 to 3
- parcel_mass: float32 [8, 524288], P(None, ('xy', 'lev')), may hold values from 0.05 to 2
- dest_device: int32 [524288, 1], P(('xy', 'lev')), may hold values from 0 to 31; in each aligned block of 4096 rows (0 to 4095, 4096 to 8191, ...) at most 256 rows name the same one
- dest_cell: int32 [524288], P(('xy', 'lev')), may hold values from 0 to 65535
- diffusivity: float32 [128, 256, 256], P('lev', 'xy'), may hold values from 0.02 to 0.12
- wind_speed: float32 [128, 256, 256], P('lev', 'xy'), may hold values from 0 to 0.3
- inverses: float32 [8, 8, 16, 16], P('lev'), may hold values from -0.15 to 1
- lower_coupling: float32 [8, 8], P('lev'), may hold values from 0.3 to 1.5
- upper_coupling: float32 [8, 8], P('lev'), may hold values from 0.3 to 1.5
Outputs:
- dust_field: float32 [8, 128, 256, 256], P(None, 'lev', 'xy')
The draws below stay inside these ranges and needn't reach their ends.
Inputs may be any that keep to these rules, and one draw needn't show every extreme that they name: `dest_device`: in the rows of one device no tile is named more than 256 times, a bound that some block reaches.
All inputs are finite; a program needn't handle non-finite values.
Results may differ from the reference program's by a relative error of at most 0.0003.
Values sent between devices are 32-bit elements; how exact they have to be, the bound alone decides.
A program may use at most 512 MiB of HBM per device.

```python
import math
import jax
import jax.numpy as jnp
import numpy as np
from jax import lax

BINS = 8
K = 16
GX = 8
GY = 256
PARC_DEV = 4096
LEV_DEV = 32
GROUPS = 8
LEVELS = 128
NX = 256
PARCELS = 524288
SEND_CAP = 256
N_XY = 32
N_LEV = 4


def draw_inverses(key, part):
    key = jax.random.fold_in(key, 7)
    key_diag, key_off, key_low, key_high = jax.random.split(key, 4)
    full_shape = (GROUPS, BINS, K, K)
    diagonal = jax.random.uniform(key_diag, (GROUPS, BINS, K), jnp.float32, 0.5, 1.0)
    offdiag = jax.random.uniform(key_off, full_shape, jnp.float32, -0.12, 0.12)
    low_corner = jax.random.uniform(key_low, (GROUPS, BINS), jnp.float32, 0.4, 1.0)
    high_corner = jax.random.uniform(key_high, (GROUPS, BINS), jnp.float32, 0.4, 1.0)
    row_ids = lax.broadcasted_iota(jnp.int32, (K, K), 0)
    col_ids = lax.broadcasted_iota(jnp.int32, (K, K), 1)
    matrix = jnp.where(row_ids == col_ids, diagonal[..., None], offdiag)
    matrix = jnp.where((row_ids == K - 1) & (col_ids == 0), low_corner[..., None, None], matrix)
    matrix = jnp.where((row_ids == 0) & (col_ids == K - 1), high_corner[..., None, None], matrix)
    return matrix


def place_ends(array, key, low, top_value):
    longest = array.shape.index(max(array.shape))
    spots = []
    for shift in (0, 1):
        where = [jax.random.randint(jax.random.fold_in(key, axis), (), 0, length) for axis, length in enumerate(array.shape)]
        where[longest] = (where[longest] + shift) % array.shape[longest]
        spots.append(tuple(where))
    return array.at[spots[0]].set(low).at[spots[1]].set(top_value)


def steps_of(stream_key, dims, pieces, least, top_value):
    def one(position, blocks):
        heights = jax.random.uniform(jax.random.fold_in(jax.random.fold_in(stream_key, 6), position), (blocks,), jnp.float32, least / len(pieces), top_value / len(pieces))
        return jnp.repeat(jnp.exp(heights), dims[position] // blocks).reshape((-1,) + (1,) * (len(dims) - position - 1))

    level = one(*pieces[0])
    for cut in pieces[1:]:
        level = level * one(*cut)
    return level


def shared_out(rng, own, number, rows, number_of, top, reach, lean):
    order = jax.random.permutation(rng, number_of)
    crowded, usual = portions_of(number_of, rows * top, reach, lean, True), portions_of(number_of, rows * top, reach, lean, False)
    places = jnp.arange(number_of)

    def named(lengths, rotation):
        used = int((lengths > 0).sum())
        fixed = max(1, used // 4)
        shifted = fixed + (places - fixed + rotation * (used - fixed)) % max(1, number_of - fixed)
        return jnp.zeros((number_of,), jnp.int32).at[order[jnp.where(places < fixed, places, shifted)]].set(jnp.asarray(lengths, jnp.int32))

    lengths = jnp.where(number % 4 == 0, named(crowded, number // 4), named(usual, number - number // 4 - 1))
    mixed = jax.random.permutation(jax.random.fold_in(own, 3), number_of)
    giver, receiver = mixed[0:number_of // 2 * 2:2], mixed[1:number_of // 2 * 2:2]
    margin = jnp.minimum(lengths[giver] - 1, reach - lengths[receiver]) // 2
    margin = jnp.where((giver == order[0]) | (receiver == order[0]) | (lengths[receiver] == 0), 0, jnp.maximum(margin, 0))
    shifted = jax.random.randint(jax.random.fold_in(own, 4), (number_of // 2,), 0, 1 << 20) % (margin + 1)
    lengths = lengths.at[giver].add(-shifted).at[receiver].add(shifted)
    items = jnp.searchsorted(jnp.cumsum(lengths), jnp.arange(rows * top), side="right").astype(jnp.int32)
    grid = items.reshape(top, rows).T
    grid = grid[jax.random.permutation(jax.random.fold_in(own, 1), rows)]
    rotation = jax.random.randint(jax.random.fold_in(own, 2), (rows, 1), 0, top)
    return jnp.take_along_axis(grid, (jnp.arange(top)[None, :] + rotation) % top, axis=1)


def portions_of(count, total, limit, skew, full):
    loads = [(1 << 20) // math.isqrt(standing ** skew) + 1 for standing in range(1, count + 1)]
    largest = limit if full else min(limit, max(-(-total // count), total * loads[0] // sum(loads)))
    least = 1 if total - largest >= count - 1 else 0
    holding, rest = [largest] + [least] * (count - 1), total - largest - least * (count - 1)
    while rest > 0:
        movable = [i for i in range(1, count) if holding[i] < largest] or [i for i in range(1, count) if holding[i] < limit]
        mass, left = sum([loads[i] for i in movable]), rest
        for i in movable:
            addition = min(limit - holding[i], max(1, left * loads[i] // mass), rest)
            holding[i] = holding[i] + addition
            rest = rest - addition
    return np.array(holding)


def setup_inputs(seed: int = 0) -> dict:
    key_of = jax.random.split(jax.random.key(seed), 10)
    euler_field = jnp.clip(jnp.exp(math.log(3.0) - 3.4011974 * jax.random.uniform(key_of[0], (BINS, LEVELS, NX, GY), jnp.float32) ** steps_of(key_of[0], (BINS, LEVELS, NX, GY), ((1, 4), (2, 32)), -0.2, 0.2)), 0.1, 3.0)
    parcel_mass = jnp.clip(jnp.exp(math.log(2.0) - 3.6888794 * jax.random.uniform(key_of[1], (BINS, PARCELS), jnp.float32) ** steps_of(key_of[1], (BINS, PARCELS), ((1, 128),), -0.2, 0.2)), 0.05, 2.0)
    dest_device_keys = jax.random.split(jax.random.fold_in(key_of[2], 1), PARCELS // PARC_DEV)
    dest_device_turns = jax.random.permutation(jax.random.fold_in(key_of[2], 3), PARCELS // PARC_DEV)
    dest_device = jax.vmap(lambda own, number: shared_out(jax.random.fold_in(key_of[2], 2), own, number, PARC_DEV, N_XY, 1, SEND_CAP, 2))(dest_device_keys, dest_device_turns).reshape((PARCELS, 1))
    dest_cell = place_ends(jax.random.randint(key_of[3], (PARCELS,), 0, LEV_DEV * GX * GY), jax.random.fold_in(key_of[3], 1), 0, (LEV_DEV * GX * GY) - 1).astype(jnp.int32)
    diffusivity = jnp.clip(0.02 + 0.09999999776482582 * jax.random.uniform(key_of[4], (LEVELS, NX, GY), jnp.float32) ** steps_of(key_of[4], (LEVELS, NX, GY), ((0, 4), (1, 32)), -0.2, 0.2), 0.02, 0.12)
    wind_speed = jnp.clip(0.3 * jax.random.uniform(key_of[5], (LEVELS, NX, GY), jnp.float32) ** steps_of(key_of[5], (LEVELS, NX, GY), ((0, 4), (1, 32)), -0.2, 0.2), 0.0, 0.3)
    inverses = draw_inverses(jax.random.fold_in(key_of[9], 71), 0)
    lower_coupling = jnp.clip(jnp.exp(math.log(1.5) - 1.60943787 * jax.random.uniform(key_of[7], (GROUPS, BINS), jnp.float32) ** steps_of(key_of[7], (GROUPS, BINS), ((0, 4),), -0.2, 0.2)), 0.3, 1.5)
    upper_coupling = jnp.clip(jnp.exp(math.log(1.5) - 1.60943787 * jax.random.uniform(key_of[8], (GROUPS, BINS), jnp.float32) ** steps_of(key_of[8], (GROUPS, BINS), ((0, 4),), -0.2, 0.2)), 0.3, 1.5)
    return {"euler_field": euler_field, "parcel_mass": parcel_mass, "dest_device": dest_device, "dest_cell": dest_cell, "diffusivity": diffusivity, "wind_speed": wind_speed, "inverses": inverses, "lower_coupling": lower_coupling, "upper_coupling": upper_coupling}


PRECISE = lax.Precision.HIGHEST


def horizontal(grid_field, diffusivity, wind_speed):
    padded = jnp.pad(grid_field, ((0, 0), (0, 0), (1, 1), (1, 1)))
    centre = padded[:, :, 1:-1, 1:-1]
    lower_row = padded[:, :, :-2, 1:-1]
    laplace = padded[:, :, 2:, 1:-1] + lower_row + padded[:, :, 1:-1, 2:] + padded[:, :, 1:-1, :-2] - 4.0 * centre
    return centre + diffusivity * laplace - wind_speed * (centre - lower_row)


def vertical(grid_field, inverses, lower_coupling, upper_coupling):
    extent = grid_field.shape
    groups = inverses.shape[0]
    block_size = inverses.shape[2]
    columns = extent[2] * extent[3]
    values = grid_field.reshape(extent[0], groups, block_size, columns)
    carried = jnp.zeros((extent[0], columns), jnp.float32)
    downward = []
    for group_id in range(groups):
        matrix = inverses[group_id]
        current = jnp.einsum("bkj,bjh->bkh", matrix, values[:, group_id], precision=PRECISE)
        current = current + (lower_coupling[group_id][:, None, None] * matrix[:, :, 0][:, :, None]) * carried[:, None, :]
        downward.append(current)
        carried = current[:, block_size - 1]
    carried = jnp.zeros((extent[0], columns), jnp.float32)
    upward = list(downward)
    for group_id in range(groups - 1, -1, -1):
        matrix = inverses[group_id]
        current = downward[group_id] + (upper_coupling[group_id][:, None, None] * matrix[:, :, block_size - 1][:, :, None]) * carried[:, None, :]
        upward[group_id] = current
        carried = current[:, 0]
    return jnp.stack(upward, axis=1).reshape(extent)


def reference(euler_field, parcel_mass, dest_device, dest_cell, diffusivity, wind_speed, inverses, lower_coupling, upper_coupling):
    first_step = horizontal(euler_field, diffusivity, wind_speed)
    plane_size = GX * GY
    rows_all = jnp.arange(PARCELS, dtype=jnp.int32)
    level_block = (rows_all // PARC_DEV) % N_LEV
    local_level = dest_cell // plane_size
    within = dest_cell % plane_size
    flat_index = ((level_block * LEV_DEV + local_level) * NX + dest_device[:, 0] * GX + within // GY) * GY + within % GY
    cells_all = LEVELS * NX * GY
    deposit = jnp.zeros((BINS, cells_all), jnp.float32).at[:, flat_index].add(parcel_mass)
    deposit = deposit.reshape(BINS, LEVELS, NX, GY)
    counts = jnp.zeros((cells_all,), jnp.float32).at[flat_index].add(1.0).reshape(LEVELS, NX, GY)
    weight_share = counts / (counts + 2.0)
    blended = (1.0 - weight_share) * first_step + weight_share * deposit
    after_first = vertical(blended, inverses, lower_coupling, upper_coupling)
    second_step = horizontal(after_first, diffusivity, wind_speed)
    return vertical(second_step, inverses, lower_coupling, upper_coupling)
```

```python
import functools

import jax
import jax.numpy as jnp
from jax import lax
from jax.experimental import pallas as pl
from jax.experimental.pallas import tpu as pltpu
from jax.sharding import PartitionSpec as P

F32, BF16, I32 = jnp.float32, jnp.bfloat16, jnp.int32
MESH = pl.DeviceIdType.MESH
N_XY, N_LEV, BINS, LEV, GX, GY = 32, 4, 8, 32, 8, 256
ROWS = BINS * LEV
PARC, CAP, BLK = 4096, 256, 256
BUCKETS = 16
NT = (((1,), (1,)), ((), ()))
LIMIT = 50 << 20


def iota(shape, dim, dtype=F32):
    return lax.broadcasted_iota(I32, shape, dim).astype(dtype)


def ranks(keys, count, lower):
    n = keys.shape[0]
    masks = [jnp.where(keys == k, 1.0, 0.0) for k in range(count)]
    stack = jnp.concatenate(masks, axis=0).astype(BF16)
    before = (iota((BLK, BLK), 0) < iota((BLK, BLK), 1)).astype(BF16)
    inside = jnp.dot(stack, before, preferred_element_type=F32)
    totals = jnp.dot(stack, jnp.ones((BLK, 128), BF16), preferred_element_type=F32)
    base = jnp.dot(lower, totals.astype(BF16), preferred_element_type=F32)
    wide = jnp.concatenate([base, base], axis=1)
    whole = inside + wide
    position = jnp.zeros(keys.shape, F32)
    for k in range(count):
        position += masks[k] * whole[k * n : (k + 1) * n]
    return position, base


def sort_block(values16, high_low, column, target, slot, out_rows, out_codes):
    chosen = jnp.broadcast_to(target, (16, BLK)).astype(BF16)
    zero = jnp.zeros((16, BLK), BF16)
    parts = [jnp.where(chosen == jnp.array(d, BF16), values16, zero) for d in range(32)]
    weighted = jnp.concatenate(parts, axis=0)
    mine = iota((32, BLK), 0) == target
    codes = jnp.concatenate(
        [jnp.where(mine, high_low, 0.0), jnp.where(mine, column, 0.0)], axis=0
    ).astype(BF16)
    spot = one_hot(slot)
    out_rows[...] += lax.dot_general(weighted, spot, NT, preferred_element_type=F32)
    out_codes[...] += lax.dot_general(codes, spot, NT, preferred_element_type=F32)


def one_hot(row):
    wide = jnp.broadcast_to(row, (BLK, BLK)).astype(BF16)
    ids = iota((BLK, BLK), 0, BF16)
    return jnp.where(ids == wide, jnp.ones((BLK, BLK), BF16), jnp.zeros((BLK, BLK), BF16))


def two_parts(values):
    high = values.astype(BF16).astype(F32)
    return jnp.concatenate([high, values - high], axis=0).astype(BF16)


def stencil(centre, before, after, diffusivity, wind):
    shape = (BINS, LEV, GY)
    lane = lax.broadcasted_iota(I32, (ROWS, GY), 1)
    left = jnp.where(lane == 0, 0.0, pltpu.roll(centre, 1, 1))
    right = jnp.where(lane == GY - 1, 0.0, pltpu.roll(centre, GY - 1, 1))
    laplace = (after + before + right + left - 4.0 * centre).reshape(shape)
    drift = (centre - before).reshape(shape)
    result = centre.reshape(shape) + diffusivity[None] * laplace - wind[None] * drift
    return result.reshape(ROWS, GY)


def plane_copies(source, target, sems, at=0):
    return [pltpu.make_async_copy(source.at[:, x, :], target.at[at + x], sems.at[x]) for x in range(GX)]


def remote(src, dst, send, recv, device):
    return pltpu.make_async_remote_copy(
        src_ref=src, dst_ref=dst, send_sem=send, recv_sem=recv, device_id=device, device_id_type=MESH
    )


def compose(inv, low, up, hi_ref, lo_ref, p_ref, e_ref):
    lane16 = lax.broadcasted_iota(I32, (16, ROWS), 1) % LEV
    row16 = lax.broadcasted_iota(I32, (16, ROWS), 0)
    own = lax.broadcasted_iota(I32, (BINS, 16, ROWS), 0) == (
        lax.broadcasted_iota(I32, (BINS, 16, ROWS), 2) // LEV
    )

    def spread(group):
        place = (lane16 == row16 + 16 * group).astype(F32)
        flat = inv[group].reshape(BINS * 16, 16)
        full = jnp.dot(flat, place, precision=lax.Precision.HIGHEST, preferred_element_type=F32)
        return jnp.where(own, full.reshape(BINS, 16, ROWS), 0.0)

    def per_bin(ref, group):
        wide = jnp.broadcast_to(ref[group : group + 1, :].reshape(1, 1, BINS), (BINS, 1, BINS))
        same = lax.broadcasted_iota(I32, (BINS, 1, BINS), 0) == lax.broadcasted_iota(
            I32, (BINS, 1, BINS), 2
        )
        return jnp.sum(jnp.where(same, wide, 0.0), axis=2, keepdims=True)

    t0, t1 = spread(0), spread(1)
    l0, l1, u0, u1 = per_bin(low, 0), per_bin(low, 1), per_bin(up, 0), per_bin(up, 1)
    m0, m1 = inv[0], inv[1]
    m0_first, m0_last = m0[:, :, 0:1], m0[:, :, 15:16]
    m1_first, m1_last = m1[:, :, 0:1], m1[:, :, 15:16]
    tail0 = t0[:, 15:16, :]
    link = (l1 * m1[:, 0:1, 0:1]) * tail0 + t1[:, 0:1, :]
    p0 = t0 + (u0 * m0_last) * link
    p1 = t1 + (l1 * m1_first) * tail0
    full = jnp.concatenate([p0, p1], axis=1).reshape(ROWS, ROWS)
    high = full.astype(BF16)
    hi_ref[...] = high
    lo_ref[...] = (full - high.astype(F32)).astype(BF16)
    passed = l1 * l0 * m0[:, 15:16, 0:1]
    c0 = l0 * m0_first + (u0 * m0_last) * (passed * m1[:, 0:1, 0:1])
    c1 = passed * m1_first
    d0 = (u0 * u1 * m1[:, 0:1, 15:16]) * m0_last
    d1 = u1 * m1_last
    p_ref[...] = jnp.broadcast_to(jnp.concatenate([c0, c1], axis=1), (BINS, LEV, 128)).reshape(ROWS, 128)
    e_ref[...] = jnp.broadcast_to(jnp.concatenate([d0, d1], axis=1), (BINS, LEV, 128)).reshape(ROWS, 128)


def carry_factors(level, all_ref, out_ref):
    alpha = [all_ref[f, 0] for f in range(N_LEV)]
    beta = [all_ref[f, 1] for f in range(N_LEV)]
    gamma = [all_ref[f, 2] for f in range(N_LEV)]
    zero, one = jnp.zeros((BINS, 128), F32), jnp.ones((BINS, 128), F32)
    for f in range(N_LEV):
        down, product = zero, one
        for i in range(f + 1, N_LEV):
            down = jnp.where(level == i, product, down)
            product = product * alpha[i]
        upward, product = zero, one
        for i in range(f - 1, -1, -1):
            upward = jnp.where(level == i, product, upward)
            product = product * beta[i]
        out_ref[f] = down
        out_ref[N_LEV + f] = upward
    sigma = [zero] * N_LEV
    for f in range(N_LEV - 1, 0, -1):
        sigma[f - 1] = gamma[f] + beta[f] * alpha[f] * sigma[f]

    def own(values):
        result = values[0]
        for f in range(1, N_LEV):
            result = jnp.where(level == f, values[f], result)
        return result

    out_ref[8] = own(sigma)
    out_ref[9] = own([sigma[f] * alpha[f] for f in range(N_LEV)])
    out_ref[10] = own([sigma[f] * beta[f] for f in range(N_LEV)])


def route_kernel(
    euler, mass, dest, cell, diffusivity, wind, inv, low, up,
    first, got_mass, got_code, p_high, p_low, p_col, e_col, factors,
    ext, diff_s, wind_s, rows_acc, codes_acc, send_mass, send_code, dest_s, slot_s, hl_s, col_s, links,
    load_sem, halo_send, halo_recv, mass_send, mass_recv, code_send, code_recv, link_send, link_recv,
):
    me, level = lax.axis_index("xy"), lax.axis_index("lev")
    barrier = pltpu.get_barrier_semaphore()

    def greet(k, unused):
        pl.semaphore_signal(
            barrier, inc=1, device_id={"xy": lax.rem(me + k, N_XY), "lev": level}, device_id_type=MESH
        )
        return unused

    lax.fori_loop(1, N_XY, greet, 0)
    for k in range(1, N_LEV):
        pl.semaphore_signal(
            barrier, inc=1, device_id={"xy": me, "lev": lax.rem(level + k, N_LEV)}, device_id_type=MESH
        )

    loads = plane_copies(euler, ext, load_sem.at[0], 1)
    loads += plane_copies(diffusivity, diff_s, load_sem.at[1]) + plane_copies(wind, wind_s, load_sem.at[2])
    for copy in loads:
        copy.start()

    def wide(ref):
        return jnp.concatenate([ref[pl.ds(0, 16, stride=2), :], ref[pl.ds(1, 16, stride=2), :]], axis=1)

    target = wide(dest).astype(F32)
    cells = wide(cell)
    levels = cells // (GX * GY)
    xs = (cells // GY) % GX
    bucket = xs * 2 + levels // 16
    dest_s[...] = target
    hl_s[...] = (bucket * 16 + levels % 16 + 1).astype(F32)
    col_s[...] = (cells % GY).astype(F32)
    r, c = (lax.broadcasted_iota(I32, (512, 512), d) for d in (0, 1))
    lower = jnp.where((c < r) & (c // 16 == r // 16), 1.0, 0.0).astype(BF16)
    slot, unused_base = ranks(target, N_XY, lower)
    slot_s[...] = slot

    for copy in loads:
        copy.wait()
    pl.semaphore_wait(barrier, N_XY - 1 + N_LEV - 1)
    above, below = lax.rem(me + 1, N_XY), lax.rem(me + N_XY - 1, N_XY)
    up_copy = remote(ext.at[GX], ext.at[0], halo_send.at[0], halo_recv.at[0], {"xy": above, "lev": level})
    down_copy = remote(ext.at[1], ext.at[GX + 1], halo_send.at[1], halo_recv.at[1], {"xy": below, "lev": level})
    up_copy.start()
    down_copy.start()

    rows_acc[...] = jnp.zeros_like(rows_acc)
    codes_acc[...] = jnp.zeros_like(codes_acc)

    def one_block(i, unused):
        lanes = pl.ds(pl.multiple_of(i * BLK, BLK), BLK)
        row = pl.ds(i, 1)
        sort_block(
            two_parts(mass[:, lanes]), hl_s[row, :], col_s[row, :], dest_s[row, :], slot_s[row, :],
            rows_acc, codes_acc,
        )
        return unused

    lax.fori_loop(0, PARC // BLK, one_block, 0)
    table = rows_acc[...].reshape(N_XY, 16, CAP)
    send_mass[...] = table[:, :8] + table[:, 8:]
    send_code[...] = codes_acc[0:32] * 256.0 + codes_acc[32:64]

    def copies(other, slot_id):
        device = {"xy": other, "lev": level}
        return (
            remote(send_mass.at[other], got_mass.at[slot_id], mass_send.at[other], mass_recv.at[slot_id], device),
            remote(
                send_code.at[pl.ds(other, 1)], got_code.at[pl.ds(slot_id, 1)],
                code_send.at[other], code_recv.at[slot_id], device,
            ),
        )

    def send(k, unused):
        for copy in copies(lax.rem(me + k, N_XY), me):
            copy.start()
        return unused

    lax.fori_loop(1, N_XY, send, 0)
    got_mass[me] = send_mass[me]
    got_code[pl.ds(me, 1), :] = send_code[pl.ds(me, 1), :]

    compose(inv, low, up, p_high, p_low, p_col, e_col)
    links[level, 0] = p_col[pl.ds(LEV - 1, BINS, stride=LEV), :]
    links[level, 1] = e_col[pl.ds(0, BINS, stride=LEV), :]
    links[level, 2] = p_col[pl.ds(0, BINS, stride=LEV), :]

    def link_copy(k, owner):
        peer = lax.rem(level + k, N_LEV)
        return remote(
            links.at[owner], links.at[owner], link_send.at[k], link_recv.at[k], {"xy": me, "lev": peer}
        )

    for k in range(1, N_LEV):
        link_copy(k, level).start()

    up_copy.wait()
    down_copy.wait()

    @pl.when(me == 0)
    def _():
        ext[0] = jnp.zeros((ROWS, GY), F32)

    @pl.when(me == N_XY - 1)
    def _():
        ext[GX + 1] = jnp.zeros((ROWS, GY), F32)

    def step(x, unused):
        first[x] = stencil(ext[x + 1], ext[x], ext[x + 2], diff_s[x], wind_s[x])
        return unused

    lax.fori_loop(0, GX, step, 0)

    for k in range(1, N_LEV):
        link_copy(k, lax.rem(level + N_LEV - k, N_LEV)).wait()
    carry_factors(level, links, factors)

    def finish(k, unused):
        for copy in copies(lax.rem(me + k, N_XY), me):
            copy.wait_send()
        for copy in copies(me, lax.rem(me + k, N_XY)):
            copy.wait_recv()
        return unused

    lax.fori_loop(1, N_XY, finish, 0)


def deposit_kernel(
    got_mass, got_code, first, blended,
    rows_acc, codes_acc, key_s, hp_s, lp_s, hl_s, col_s, total, starts_v, starts_s, sem,
):
    code = got_code[...].astype(I32)
    hl = code // 256
    col = code % 256
    valid = hl > 0
    key = jnp.where(valid, (hl - 1) // 16, -1).astype(F32)
    hl_s[...] = hl.astype(F32)
    col_s[...] = col.astype(F32)
    r, c = (lax.broadcasted_iota(I32, (512, 512), d) for d in (0, 1))
    lower = jnp.where(c < r, 1.0, 0.0).astype(BF16)
    position, base = ranks(key, BUCKETS, lower)
    place = position.astype(I32)
    hp_s[...] = jnp.where(valid, place // BLK, -1).astype(F32)
    lp_s[...] = (place % BLK).astype(F32)
    for k in range(BUCKETS):
        starts_v[k : k + 1, :] = base[32 * k : 32 * k + 1, :].astype(I32)
    count = jnp.sum(jnp.where(valid, 1.0, 0.0)).astype(I32)
    starts_v[BUCKETS:, :] = jnp.full((8, 128), count, I32)
    to_scalars = pltpu.make_async_copy(starts_v, starts_s, sem)
    to_scalars.start()

    rows_acc[...] = jnp.zeros_like(rows_acc)
    codes_acc[...] = jnp.zeros_like(codes_acc)
    total[...] = jnp.zeros_like(total)

    def one_block(i, unused):
        row = pl.ds(i, 1)
        sort_block(
            two_parts(got_mass[i]), hl_s[row, :], col_s[row, :], hp_s[row, :], lp_s[row, :],
            rows_acc, codes_acc,
        )
        return unused

    lax.fori_loop(0, N_XY, one_block, 0)
    to_scalars.wait()

    def one_bucket(k, unused):
        begin, end = starts_s[k, 0], starts_s[k + 1, 0]
        first_code = (k * 16 + 1).astype(F32)
        x, half = k // 2, k % 2

        def one_pair(j, unused):
            rows = rows_acc[pl.ds(pl.multiple_of(j * 16, 16), 16), :]
            hl_row = codes_acc[pl.ds(j, 1), :]
            col_row = codes_acc[pl.ds(j + 32, 1), :]
            mine = jnp.broadcast_to(hl_row, (16, BLK)) == iota((16, BLK), 0) + first_code
            spread = [
                jnp.where(mine, jnp.broadcast_to(rows[q : q + 1, :], (16, BLK)), 0.0) for q in range(16)
            ]
            high = jnp.concatenate(spread[:8] + [jnp.where(mine, 1.0, 0.0)], axis=0).astype(BF16)
            low = jnp.concatenate(spread[8:], axis=0).astype(BF16)
            spot = one_hot(col_row)
            big = lax.dot_general(high, spot, NT, preferred_element_type=F32).reshape(9, 16, GY)
            small = lax.dot_general(low, spot, NT, preferred_element_type=F32).reshape(8, 16, GY)
            levels = pl.ds(pl.multiple_of(half * 16, 16), 16)
            total[x, 0:8, levels, :] += big[0:8] + small
            total[x, 8, levels, :] += big[8]
            return unused

        @pl.when(end > begin)
        def _():
            lax.fori_loop(begin // BLK, (end + BLK - 1) // BLK, one_pair, 0)

        return unused

    lax.fori_loop(0, BUCKETS, one_bucket, 0)

    def blend(x, unused):
        counts = total[x, 8]
        share = counts / (counts + 2.0)
        old = first[x].reshape(BINS, LEV, GY)
        mixed = (1.0 - share)[None] * old + share[None] * total[x, 0:8]
        blended[x] = mixed.reshape(ROWS, GY)
        return unused

    lax.fori_loop(0, GX, blend, 0)


def solve_kernel(
    blended, diffusivity, wind, p_high, p_low, p_col, e_col, factors,
    out,
    ext, diff_s, wind_s, second, edge, seen, edge2, seen2,
    load_sem, store_sem, lev_send, lev_recv, diag_send, diag_recv, halo_send, halo_recv, lev2_send, lev2_recv,
):
    me, level = lax.axis_index("xy"), lax.axis_index("lev")
    above, below = lax.rem(me + 1, N_XY), lax.rem(me + N_XY - 1, N_XY)
    barrier = pltpu.get_barrier_semaphore()
    for k in range(N_LEV):
        peer = lax.rem(level + k, N_LEV)
        for where in ([me] if k else []) + [above, below]:
            pl.semaphore_signal(barrier, inc=1, device_id={"xy": where, "lev": peer}, device_id_type=MESH)

    loads = plane_copies(diffusivity, diff_s, load_sem.at[0]) + plane_copies(wind, wind_s, load_sem.at[1])
    for copy in loads:
        copy.start()

    def product(values):
        high = values.astype(BF16)
        low = (values - high.astype(F32)).astype(BF16)
        return (
            jnp.dot(p_high[...], high, preferred_element_type=F32)
            + jnp.dot(p_high[...], low, preferred_element_type=F32)
            + jnp.dot(p_low[...], high, preferred_element_type=F32)
        )

    def both(ref, i):
        return jnp.concatenate([ref[i], ref[i]], axis=1)

    def edges(values, target, x):
        blocks = values.reshape(BINS, LEV, GY)
        last, start = blocks[:, LEV - 1, :], blocks[:, 0, :]
        target[0, x] = last
        target[1, x] = start + both(factors, 10) * last

    def corrected(values, at, seen_ref):
        down = jnp.zeros((BINS, GY), F32)
        upward = jnp.zeros((BINS, GY), F32)
        for f in range(N_LEV):
            here = jnp.where(level == f, 0.0, seen_ref[f, at])
            down += both(factors, f) * here
            upward += both(factors, N_LEV + f) * here
        tail = values.reshape(BINS, LEV, GY)[:, LEV - 1, :]
        upward += both(factors, 8) * tail + both(factors, 9) * down
        shape = (BINS, LEV, GY)
        p_wide = jnp.concatenate([p_col[...], p_col[...]], axis=1).reshape(shape)
        e_wide = jnp.concatenate([e_col[...], e_col[...]], axis=1).reshape(shape)
        result = values.reshape(shape) + p_wide * down[:, None, :] + e_wide * upward[:, None, :]
        return result.reshape(ROWS, GY)

    def solve_plane(x, unused):
        solved = product(blended[x])
        ext[x + 1] = solved
        edges(solved, edge, x)
        return unused

    lax.fori_loop(0, 2, lambda i, u: solve_plane(i * (GX - 1), u), 0)
    pl.semaphore_wait(barrier, 3 * N_LEV - 1)
    up_copy = remote(ext.at[GX], ext.at[0], halo_send.at[0], halo_recv.at[0], {"xy": above, "lev": level})
    down_copy = remote(ext.at[1], ext.at[GX + 1], halo_send.at[1], halo_recv.at[1], {"xy": below, "lev": level})
    up_copy.start()
    down_copy.start()
    lax.fori_loop(1, GX - 1, solve_plane, 0)

    def lev_copies(k, owner, first_round):
        peer = lax.rem(level + k, N_LEV)
        kind = jnp.where(peer > level, 0, 1)
        if not first_round:
            return [
                remote(edge2.at[kind], seen2.at[owner], lev2_send.at[k], lev2_recv.at[k], {"xy": me, "lev": peer})
            ]
        return [
            remote(
                edge.at[kind], seen.at[owner, pl.ds(1, GX)], lev_send.at[k], lev_recv.at[k], {"xy": me, "lev": peer}
            ),
            remote(
                edge.at[kind, GX - 1], seen.at[owner, 0], diag_send.at[0, k], diag_recv.at[0, k],
                {"xy": above, "lev": peer},
            ),
            remote(
                edge.at[kind, 0], seen.at[owner, GX + 1], diag_send.at[1, k], diag_recv.at[1, k],
                {"xy": below, "lev": peer},
            ),
        ]

    for k in range(1, N_LEV):
        for copy in lev_copies(k, level, True):
            copy.start()
    for k in range(1, N_LEV):
        for copy in lev_copies(k, lax.rem(level + N_LEV - k, N_LEV), True):
            copy.wait()

    def correct_plane(at, unused):
        ext[at] = corrected(ext[at], at, seen)
        return unused

    up_copy.wait()
    down_copy.wait()
    lax.fori_loop(0, GX + 2, correct_plane, 0)

    @pl.when(me == 0)
    def _():
        ext[0] = jnp.zeros((ROWS, GY), F32)

    @pl.when(me == N_XY - 1)
    def _():
        ext[GX + 1] = jnp.zeros((ROWS, GY), F32)

    def second_plane(x, unused):
        stepped = stencil(ext[x + 1], ext[x], ext[x + 2], diff_s[x], wind_s[x])
        solved = product(stepped)
        second[x] = solved
        edges(solved, edge2, x)
        return unused

    for copy in loads:
        copy.wait()
    lax.fori_loop(0, GX, second_plane, 0)
    for k in range(1, N_LEV):
        for copy in lev_copies(k, level, False):
            copy.start()
    for k in range(1, N_LEV):
        for copy in lev_copies(k, lax.rem(level + N_LEV - k, N_LEV), False):
            copy.wait()

    def last_plane(x, unused):
        second[x] = corrected(second[x], x, seen2)
        pltpu.make_async_copy(second.at[x], out.at[:, x, :], store_sem.at[x]).start()
        return unused

    lax.fori_loop(0, GX, last_plane, 0)
    for x in range(GX):
        pltpu.make_async_copy(second.at[x], out.at[:, x, :], store_sem.at[x]).wait()


def vmem(*shape, dtype=F32):
    return pltpu.VMEM(shape, dtype)


def whole(count):
    return [pl.BlockSpec(memory_space=pltpu.VMEM)] * count


def somewhere(count):
    return [pl.BlockSpec(memory_space=pl.ANY)] * count


def shaped(*shape, dtype=F32):
    return jax.ShapeDtypeStruct(shape, dtype)


def shards(
    euler_field, parcel_mass, dest_device, dest_cell, diffusivity, wind_speed, inverses, lower_coupling, upper_coupling
):
    dma = pltpu.SemaphoreType.DMA
    routed = pl.pallas_call(
        route_kernel,
        name="route",
        out_shape=[
            shaped(GX, ROWS, GY), shaped(N_XY, BINS, CAP), shaped(N_XY, CAP),
            shaped(ROWS, ROWS, dtype=BF16), shaped(ROWS, ROWS, dtype=BF16),
            shaped(ROWS, 128), shaped(ROWS, 128), shaped(11, BINS, 128),
        ],
        in_specs=somewhere(1) + whole(3) + somewhere(2) + whole(3),
        out_specs=whole(8),
        scratch_shapes=[
            vmem(GX + 2, ROWS, GY), vmem(GX, LEV, GY), vmem(GX, LEV, GY), vmem(512, CAP), vmem(64, CAP),
            vmem(N_XY, BINS, CAP), vmem(N_XY, CAP),
            vmem(16, BLK), vmem(16, BLK), vmem(16, BLK), vmem(16, BLK), vmem(N_LEV, 3, BINS, 128),
            dma((3, GX)), dma((2,)), dma((2,)), dma((N_XY,)), dma((N_XY,)), dma((N_XY,)), dma((N_XY,)),
            dma((N_LEV,)), dma((N_LEV,)),
        ],
        compiler_params=pltpu.CompilerParams(collective_id=0, has_side_effects=True, vmem_limit_bytes=LIMIT),
    )(
        euler_field.reshape(ROWS, GX, GY), parcel_mass, dest_device.reshape(32, 128), dest_cell.reshape(32, 128),
        diffusivity, wind_speed, inverses, lower_coupling, upper_coupling,
    )
    first, got_mass, got_code, p_high, p_low, p_col, e_col, factors = routed
    blended = pl.pallas_call(
        deposit_kernel,
        name="deposit",
        out_shape=shaped(GX, ROWS, GY),
        in_specs=whole(3),
        out_specs=pl.BlockSpec(memory_space=pltpu.VMEM),
        scratch_shapes=[
            vmem(512, BLK), vmem(64, BLK),
            vmem(N_XY, BLK), vmem(N_XY, BLK), vmem(N_XY, BLK), vmem(N_XY, BLK), vmem(N_XY, BLK),
            vmem(GX, BINS + 1, LEV, GY), vmem(BUCKETS + 8, 128, dtype=I32),
            pltpu.SMEM((BUCKETS + 8, 128), I32), dma,
        ],
        compiler_params=pltpu.CompilerParams(vmem_limit_bytes=LIMIT),
    )(got_mass, got_code, first)
    result = pl.pallas_call(
        solve_kernel,
        name="solve",
        out_shape=shaped(ROWS, GX, GY),
        in_specs=whole(1) + somewhere(2) + whole(5),
        out_specs=pl.BlockSpec(memory_space=pl.ANY),
        scratch_shapes=[
            vmem(GX + 2, ROWS, GY), vmem(GX, LEV, GY), vmem(GX, LEV, GY), vmem(GX, ROWS, GY),
            vmem(2, GX, BINS, GY), vmem(N_LEV, GX + 2, BINS, GY),
            vmem(2, GX, BINS, GY), vmem(N_LEV, GX, BINS, GY),
            dma((2, GX)), dma((GX,)), dma((N_LEV,)), dma((N_LEV,)), dma((2, N_LEV)), dma((2, N_LEV)), dma((2,)), dma((2,)),
            dma((N_LEV,)), dma((N_LEV,)),
        ],
        compiler_params=pltpu.CompilerParams(collective_id=1, has_side_effects=True, vmem_limit_bytes=LIMIT),
    )(blended, diffusivity, wind_speed, p_high, p_low, p_col, e_col, factors)
    return result.reshape(BINS, LEV, GX, GY)


def solution(mesh):
    placed = (
        P(None, "lev", "xy", None),
        P(None, ("xy", "lev")),
        P(("xy", "lev"), None),
        P(("xy", "lev")),
        P("lev", "xy", None),
        P("lev", "xy", None),
        P("lev", None, None, None),
        P("lev", None),
        P("lev", None),
    )
    return jax.shard_map(
        shards, mesh=mesh, in_specs=placed, out_specs=P(None, "lev", "xy", None), check_vma=False
    )
```

```python
import functools

import jax
import jax.numpy as jnp
from jax import lax
from jax.experimental import pallas as pl
from jax.experimental.pallas import tpu as pltpu
from jax.sharding import PartitionSpec as P

F32, BF16, I32 = jnp.float32, jnp.bfloat16, jnp.int32
MESH = pl.DeviceIdType.MESH
N_XY, N_LEV, BINS, LEV, GX, GY = 32, 4, 8, 32, 8, 256
ROWS = BINS * LEV
PARC, CAP, BLK = 4096, 256, 256
BUCKETS = 16
NT = (((1,), (1,)), ((), ()))
LIMIT = 24 << 20
SETS = 2
SRC = N_XY // SETS
SPAN = SRC * CAP
UNITS = SPAN // 128
WIN = 4


def iota(shape, dim, dtype=F32):
    return lax.broadcasted_iota(I32, shape, dim).astype(dtype)


def ranks(keys, count, lower):
    n = keys.shape[0]
    masks = [jnp.where(keys == k, 1.0, 0.0) for k in range(count)]
    stack = jnp.concatenate(masks, axis=0).astype(BF16)
    before = (iota((BLK, BLK), 0) < iota((BLK, BLK), 1)).astype(BF16)
    inside = jnp.dot(stack, before, preferred_element_type=F32)
    totals = jnp.dot(stack, jnp.ones((BLK, 128), BF16), preferred_element_type=F32)
    base = jnp.dot(lower, totals.astype(BF16), preferred_element_type=F32)
    wide = jnp.concatenate([base, base], axis=1)
    whole = inside + wide[: inside.shape[0]]
    position = jnp.zeros(keys.shape, F32)
    for k in range(count):
        position += masks[k] * whole[k * n : (k + 1) * n]
    return position, base


def lanes(pieces):
    return jnp.concatenate(pieces, axis=1)


def one_hot(row):
    width = row.shape[1]
    wide = jnp.broadcast_to(row, (BLK, width)).astype(BF16)
    ids = iota((BLK, width), 0, BF16)
    return jnp.where(ids == wide, jnp.ones((BLK, width), BF16), jnp.zeros((BLK, width), BF16))


def sort_slots(values16, high_low, column, target, slot, count):
    width = target.shape[1]
    chosen = jnp.broadcast_to(target, (16, width)).astype(BF16)
    zero = jnp.zeros((16, width), BF16)
    parts = [jnp.where(chosen == jnp.array(d, BF16), values16, zero) for d in range(count)]
    mine = iota((count, width), 0) == target
    codes = jnp.concatenate([jnp.where(mine, high_low, 0.0), jnp.where(mine, column, 0.0)], axis=0)
    weighted = jnp.concatenate(parts + [codes.astype(BF16)], axis=0)
    return lax.dot_general(weighted, one_hot(slot), NT, preferred_element_type=F32)


def two_parts(values):
    high = values.astype(BF16).astype(F32)
    return jnp.concatenate([high, values - high], axis=0).astype(BF16)


def stencil(centre, before, after, diffusivity, wind):
    shape = (BINS, LEV, GY)
    lane = lax.broadcasted_iota(I32, (ROWS, GY), 1)
    left = jnp.where(lane == 0, 0.0, pltpu.roll(centre, 1, 1))
    right = jnp.where(lane == GY - 1, 0.0, pltpu.roll(centre, GY - 1, 1))
    laplace = (after + before + right + left - 4.0 * centre).reshape(shape)
    drift = (centre - before).reshape(shape)
    result = centre.reshape(shape) + diffusivity[None] * laplace - wind[None] * drift
    return result.reshape(ROWS, GY)


def plane_copies(source, target, sems, at=0):
    return [pltpu.make_async_copy(source.at[:, x, :], target.at[at + x], sems.at[x]) for x in range(GX)]


def remote(src, dst, send, recv, device):
    return pltpu.make_async_remote_copy(
        src_ref=src, dst_ref=dst, send_sem=send, recv_sem=recv, device_id=device, device_id_type=MESH
    )


def compose(inv, low, up, hi_ref, lo_ref, p_ref, e_ref):
    lane16 = lax.broadcasted_iota(I32, (16, ROWS), 1) % LEV
    row16 = lax.broadcasted_iota(I32, (16, ROWS), 0)
    own = lax.broadcasted_iota(I32, (BINS, 16, ROWS), 0) == (
        lax.broadcasted_iota(I32, (BINS, 16, ROWS), 2) // LEV
    )

    def spread(group):
        place = (lane16 == row16 + 16 * group).astype(F32)
        flat = inv[group].reshape(BINS * 16, 16)
        full = jnp.dot(flat, place, precision=lax.Precision.HIGHEST, preferred_element_type=F32)
        return jnp.where(own, full.reshape(BINS, 16, ROWS), 0.0)

    def per_bin(ref, group):
        wide = jnp.broadcast_to(ref[group : group + 1, :].reshape(1, 1, BINS), (BINS, 1, BINS))
        same = lax.broadcasted_iota(I32, (BINS, 1, BINS), 0) == lax.broadcasted_iota(
            I32, (BINS, 1, BINS), 2
        )
        return jnp.sum(jnp.where(same, wide, 0.0), axis=2, keepdims=True)

    t0, t1 = spread(0), spread(1)
    l0, l1, u0, u1 = per_bin(low, 0), per_bin(low, 1), per_bin(up, 0), per_bin(up, 1)
    m0, m1 = inv[0], inv[1]
    m0_first, m0_last = m0[:, :, 0:1], m0[:, :, 15:16]
    m1_first, m1_last = m1[:, :, 0:1], m1[:, :, 15:16]
    tail0 = t0[:, 15:16, :]
    link = (l1 * m1[:, 0:1, 0:1]) * tail0 + t1[:, 0:1, :]
    p0 = t0 + (u0 * m0_last) * link
    p1 = t1 + (l1 * m1_first) * tail0
    full = jnp.concatenate([p0, p1], axis=1).reshape(ROWS, ROWS)
    high = full.astype(BF16)
    hi_ref[...] = high
    lo_ref[...] = (full - high.astype(F32)).astype(BF16)
    passed = l1 * l0 * m0[:, 15:16, 0:1]
    c0 = l0 * m0_first + (u0 * m0_last) * (passed * m1[:, 0:1, 0:1])
    c1 = passed * m1_first
    d0 = (u0 * u1 * m1[:, 0:1, 15:16]) * m0_last
    d1 = u1 * m1_last
    p_ref[...] = jnp.broadcast_to(jnp.concatenate([c0, c1], axis=1), (BINS, LEV, 128)).reshape(ROWS, 128)
    e_ref[...] = jnp.broadcast_to(jnp.concatenate([d0, d1], axis=1), (BINS, LEV, 128)).reshape(ROWS, 128)


def carry_factors(level, all_ref, out_ref):
    alpha = [all_ref[f, 0] for f in range(N_LEV)]
    beta = [all_ref[f, 1] for f in range(N_LEV)]
    gamma = [all_ref[f, 2] for f in range(N_LEV)]
    zero, one = jnp.zeros((BINS, 128), F32), jnp.ones((BINS, 128), F32)
    for f in range(N_LEV):
        down, product = zero, one
        for i in range(f + 1, N_LEV):
            down = jnp.where(level == i, product, down)
            product = product * alpha[i]
        upward, product = zero, one
        for i in range(f - 1, -1, -1):
            upward = jnp.where(level == i, product, upward)
            product = product * beta[i]
        out_ref[f] = down
        out_ref[N_LEV + f] = upward
    sigma = [zero] * N_LEV
    for f in range(N_LEV - 1, 0, -1):
        sigma[f - 1] = gamma[f] + beta[f] * alpha[f] * sigma[f]

    def own(values):
        result = values[0]
        for f in range(1, N_LEV):
            result = jnp.where(level == f, values[f], result)
        return result

    out_ref[8] = own(sigma)
    out_ref[9] = own([sigma[f] * alpha[f] for f in range(N_LEV)])
    out_ref[10] = own([sigma[f] * beta[f] for f in range(N_LEV)])


def route_kernel(
    euler, mass, dest, cell, diffusivity, wind, inv, low, up,
    first, got_mass, got_code, p_high, p_low, p_col, e_col, factors,
    ext, diff_s, wind_s, mass_s, dest_in, cell_in, inv_s, low_s, up_s, table_s,
    send_mass, send_code, dest_s, slot_s, hl_s, col_s, links,
    load_sem, small_sem, halo_send, halo_recv, mass_send, mass_recv, code_send, code_recv, link_send, link_recv,
):
    me, level = lax.axis_index("xy"), lax.axis_index("lev")
    barrier = pltpu.get_barrier_semaphore()

    def greet(k, unused):
        pl.semaphore_signal(
            barrier, inc=1, device_id={"xy": lax.rem(me + k, N_XY), "lev": level}, device_id_type=MESH
        )
        return unused

    lax.fori_loop(1, N_XY, greet, 0)
    for k in range(1, N_LEV):
        pl.semaphore_signal(
            barrier, inc=1, device_id={"xy": me, "lev": lax.rem(level + k, N_LEV)}, device_id_type=MESH
        )

    small = [
        pltpu.make_async_copy(source, target, small_sem.at[i])
        for i, (source, target) in enumerate(
            [(dest, dest_in), (cell, cell_in), (mass, mass_s), (inv, inv_s), (low, low_s), (up, up_s)]
        )
    ]
    field = plane_copies(euler, ext, load_sem.at[0], 1)
    coefficients = plane_copies(diffusivity, diff_s, load_sem.at[1]) + plane_copies(wind, wind_s, load_sem.at[2])
    for copy in small + field + coefficients:
        copy.start()

    def wide(ref):
        return jnp.concatenate([ref[pl.ds(0, 16, stride=2), :], ref[pl.ds(1, 16, stride=2), :]], axis=1)

    for copy in small[:2]:
        copy.wait()
    target = wide(dest_in).astype(F32)
    cells = wide(cell_in)
    levels = cells // (GX * GY)
    xs = (cells // GY) % GX
    bucket = xs * 2 + levels // 16
    dest_s[...] = target
    hl_s[...] = (bucket * 16 + levels % 16 + 1).astype(F32)
    col_s[...] = (cells % GY).astype(F32)
    r, c = (lax.broadcasted_iota(I32, (512, 512), d) for d in (0, 1))
    lower = jnp.where((c < r) & (c // 16 == r // 16), 1.0, 0.0).astype(BF16)
    slot, unused_base = ranks(target, N_XY, lower)
    slot_s[...] = slot

    for copy in field:
        copy.wait()
    pl.semaphore_wait(barrier, N_XY - 1 + N_LEV - 1)
    above, below = lax.rem(me + 1, N_XY), lax.rem(me + N_XY - 1, N_XY)
    up_copy = remote(ext.at[GX], ext.at[0], halo_send.at[0], halo_recv.at[0], {"xy": above, "lev": level})
    down_copy = remote(ext.at[1], ext.at[GX + 1], halo_send.at[1], halo_recv.at[1], {"xy": below, "lev": level})
    up_copy.start()
    down_copy.start()

    small[2].wait()
    table_s[...] = jnp.zeros_like(table_s)

    def some_blocks(i, unused):
        block = pl.ds(pl.multiple_of(i * (PARC // 2), PARC // 2), PARC // 2)
        take = lambda ref: lanes([ref[pl.ds(i * 8 + j, 1), :] for j in range(8)])
        table_s[...] += sort_slots(
            two_parts(mass_s[:, block]), take(hl_s), take(col_s), take(dest_s), take(slot_s), N_XY
        )
        return unused

    lax.fori_loop(0, 2, some_blocks, 0)
    table = table_s[0 : 16 * N_XY].reshape(N_XY, 16, CAP)
    send_mass[...] = table[:, :8] + table[:, 8:]
    send_code[...] = table_s[16 * N_XY : 17 * N_XY] * 256.0 + table_s[17 * N_XY :]

    def copies(other, slot_id):
        device = {"xy": other, "lev": level}
        return (
            remote(send_mass.at[other], got_mass.at[slot_id], mass_send.at[other], mass_recv.at[slot_id], device),
            remote(
                send_code.at[pl.ds(other, 1)], got_code.at[pl.ds(slot_id, 1)],
                code_send.at[other], code_recv.at[slot_id], device,
            ),
        )

    def send(k, unused):
        for copy in copies(lax.rem(me + k, N_XY), me):
            copy.start()
        return unused

    lax.fori_loop(1, N_XY, send, 0)
    got_mass[me] = send_mass[me]
    got_code[pl.ds(me, 1), :] = send_code[pl.ds(me, 1), :]

    for copy in small[3:]:
        copy.wait()
    compose(inv_s, low_s, up_s, p_high, p_low, p_col, e_col)
    links[level, 0] = p_col[pl.ds(LEV - 1, BINS, stride=LEV), :]
    links[level, 1] = e_col[pl.ds(0, BINS, stride=LEV), :]
    links[level, 2] = p_col[pl.ds(0, BINS, stride=LEV), :]

    def link_copy(k, owner):
        peer = lax.rem(level + k, N_LEV)
        return remote(
            links.at[owner], links.at[owner], link_send.at[k], link_recv.at[k], {"xy": me, "lev": peer}
        )

    for k in range(1, N_LEV):
        link_copy(k, level).start()

    for copy in coefficients:
        copy.wait()
    up_copy.wait()
    down_copy.wait()

    @pl.when(me == 0)
    def _():
        ext[0] = jnp.zeros((ROWS, GY), F32)

    @pl.when(me == N_XY - 1)
    def _():
        ext[GX + 1] = jnp.zeros((ROWS, GY), F32)

    def step(x, unused):
        first[x] = stencil(ext[x + 1], ext[x], ext[x + 2], diff_s[x], wind_s[x])
        return unused

    lax.fori_loop(0, GX, step, 0)

    for k in range(1, N_LEV):
        link_copy(k, lax.rem(level + N_LEV - k, N_LEV)).wait()
    carry_factors(level, links, factors)

    def finish(k, unused):
        for copy in copies(lax.rem(me + k, N_XY), me):
            copy.wait_send()
        for copy in copies(me, lax.rem(me + k, N_XY)):
            copy.wait_recv()
        return unused

    lax.fori_loop(1, N_XY, finish, 0)


def deposit_kernel(
    got_mass, got_code, first, blended,
    rows_u, hl_u, col_u, hp_s, lp_s, hl_s, col_s, total, starts_v, starts_s, sem,
):
    code = got_code[...].astype(I32)
    hl = code // 256
    col = code % 256
    valid = hl > 0
    key = jnp.where(valid, (hl - 1) // 16, -1).astype(F32)
    hl_s[...] = hl.astype(F32)
    col_s[...] = col.astype(F32)
    r, c = (lax.broadcasted_iota(I32, (N_XY * (BUCKETS + 1), 512), d) for d in (0, 1))
    lower = jnp.where((c < r) & ((c % N_XY) // SRC == (r % N_XY) // SRC), 1.0, 0.0).astype(BF16)
    position, base = ranks(key, BUCKETS, lower)
    place = position.astype(I32)
    hp_s[...] = jnp.where(valid, place // BLK, -1).astype(F32)
    lp_s[...] = (place % BLK).astype(F32)
    lane = lax.broadcasted_iota(I32, (1, 128), 1)
    longest = jnp.zeros((1, 128), I32)
    before = None
    for k in range(BUCKETS + 1):
        start = jnp.zeros((1, 128), F32)
        for g in range(SETS):
            at = N_XY * k + SRC * g
            start = jnp.where(lane == g, base[at : at + 1, :], start)
        start = start.astype(I32)
        starts_v[k : k + 1, :] = start
        if k:
            longest = jnp.maximum(longest, start - before // 128 * 128)
        before = start
    starts_v[BUCKETS + 1 : BUCKETS + 2, :] = longest
    to_scalars = pltpu.make_async_copy(starts_v, starts_s, sem)
    to_scalars.start()

    def one_set(g, unused):
        take = lambda ref: lanes([ref[pl.ds(g * SRC + i, 1), :] for i in range(SRC)])
        values = lanes([two_parts(got_mass[g * SRC + i]) for i in range(SRC)])
        table = sort_slots(values, take(hl_s), take(col_s), take(hp_s), take(lp_s), SRC)
        for half in range(2):
            side = slice(128 * half, 128 * half + 128)
            for d in range(SRC):
                rows_u[g, 2 * d + half] = table[16 * d : 16 * d + 16, side]
            hl_u[g, pl.ds(half, SRC, stride=2), :] = table[16 * SRC : 17 * SRC, side]
            col_u[g, pl.ds(half, SRC, stride=2), :] = table[17 * SRC : 18 * SRC, side]
        rows_u[g, UNITS:] = jnp.zeros((WIN, 16, 128), F32)
        hl_u[g, UNITS:, :] = jnp.zeros((8, 128), F32)
        col_u[g, UNITS:, :] = jnp.zeros((8, 128), F32)
        return unused

    lax.fori_loop(0, SETS, one_set, 0)
    to_scalars.wait()

    def place_of(k):
        return k // 2, pl.ds(pl.multiple_of((k % 2) * 16, 16), 16)

    def window(k, t):
        first_code = (k * 16 + 1).astype(F32)
        at = [jnp.minimum(starts_s[k, g] // 128 + WIN * t, UNITS) for g in range(SETS)]
        units = [(g, at[g] + i) for g in range(SETS) for i in range(WIN)]
        hl_row = lanes([hl_u[g, pl.ds(u, 1), :] for g, u in units])
        col_row = lanes([col_u[g, pl.ds(u, 1), :] for g, u in units])
        rows = lanes([rows_u[g, u] for g, u in units])
        width = 128 * WIN * SETS
        mine = jnp.broadcast_to(hl_row, (16, width)) == iota((16, width), 0) + first_code
        spread = [jnp.where(mine, jnp.broadcast_to(rows[q : q + 1, :], (16, width)), 0.0) for q in range(16)]
        spread.insert(8, jnp.where(mine, 1.0, 0.0))
        weighted = jnp.concatenate(spread, axis=0).astype(BF16)
        table = lax.dot_general(weighted, one_hot(col_row), NT, preferred_element_type=F32)
        table = table.reshape(17, 16, GY)
        return jnp.concatenate([table[:8] + table[9:], table[8:9]], axis=0)

    def one_bucket(k, unused):
        x, levels = place_of(k)
        total[x, :, levels, :] = window(k, 0)
        return unused

    lax.fori_loop(0, BUCKETS, one_bucket, 0, unroll=4)

    def rest(k, unused):
        x, levels = place_of(k)
        rounds = jnp.int32(1)
        for g in range(SETS):
            span = starts_s[k + 1, g] - starts_s[k, g] // 128 * 128
            rounds = jnp.maximum(rounds, (span + 128 * WIN - 1) // (128 * WIN))

        def again(t, unused):
            total[x, :, levels, :] += window(k, t)
            return unused

        lax.fori_loop(1, rounds, again, 0)
        return unused

    most = starts_s[BUCKETS + 1, 0]
    for g in range(1, SETS):
        most = jnp.maximum(most, starts_s[BUCKETS + 1, g])

    @pl.when(most > 128 * WIN)
    def _():
        lax.fori_loop(0, BUCKETS, rest, 0)

    def blend(x, unused):
        counts = total[x, 8]
        share = counts / (counts + 2.0)
        old = first[x].reshape(BINS, LEV, GY)
        mixed = (1.0 - share)[None] * old + share[None] * total[x, 0:8]
        blended[x] = mixed.reshape(ROWS, GY)
        return unused

    lax.fori_loop(0, GX, blend, 0)


def correction(values, down, upward, p_col, e_col):
    shape = (BINS, LEV, GY)
    p_wide = lanes([p_col[...], p_col[...]]).reshape(shape)
    e_wide = lanes([e_col[...], e_col[...]]).reshape(shape)
    result = values.reshape(shape) + p_wide * down[:, None, :] + e_wide * upward[:, None, :]
    return result.reshape(ROWS, GY)


def solve_kernel(
    blended, diffusivity, wind, p_high, p_low, p_col, e_col, factors,
    second, down_out, up_out,
    ext, fixed, triple, diff_s, wind_s, edge, seen, edge2, seen2,
    load_sem, lev_send, lev_recv, diag_send, diag_recv, halo_send, halo_recv, lev2_send, lev2_recv,
):
    me, level = lax.axis_index("xy"), lax.axis_index("lev")
    above, below = lax.rem(me + 1, N_XY), lax.rem(me + N_XY - 1, N_XY)
    barrier = pltpu.get_barrier_semaphore()
    for k in range(N_LEV):
        peer = lax.rem(level + k, N_LEV)
        for where in ([me] if k else []) + [above, below]:
            pl.semaphore_signal(barrier, inc=1, device_id={"xy": where, "lev": peer}, device_id_type=MESH)
    loads = plane_copies(diffusivity, diff_s, load_sem.at[0]) + plane_copies(wind, wind_s, load_sem.at[1])
    for copy in loads:
        copy.start()
    triple[:, 0:ROWS] = p_high[...]
    triple[:, ROWS : 2 * ROWS] = p_high[...]
    triple[:, 2 * ROWS :] = p_low[...]

    def product(values):
        high = values.astype(BF16)
        low = (values - high.astype(F32)).astype(BF16)
        return jnp.dot(triple[...], jnp.concatenate([high, low, high], axis=0), preferred_element_type=F32)

    def both(i):
        return lanes([factors[i], factors[i]])

    def edges(values, target, at):
        blocks = values.reshape(BINS, LEV, GY)
        last, start = blocks[:, LEV - 1, :], blocks[:, 0, :]
        target[0, at] = last
        target[1, at] = start + both(10) * last

    def carries(values, at, seen_ref):
        down = jnp.zeros((BINS, GY), F32)
        upward = jnp.zeros((BINS, GY), F32)
        for f in range(N_LEV):
            here = jnp.where(level == f, 0.0, seen_ref[f, at])
            down += both(f) * here
            upward += both(N_LEV + f) * here
        tail = values.reshape(BINS, LEV, GY)[:, LEV - 1, :]
        return down, upward + both(8) * tail + both(9) * down

    def solve_plane(x, unused):
        solved = product(blended[x])
        ext[x + 1] = solved
        edges(solved, edge, x)
        return unused

    lax.fori_loop(0, 2, lambda i, u: solve_plane(i * (GX - 1), u), 0, unroll=2)
    pl.semaphore_wait(barrier, 3 * N_LEV - 1)
    up_copy = remote(ext.at[GX], ext.at[0], halo_send.at[0], halo_recv.at[0], {"xy": above, "lev": level})
    down_copy = remote(ext.at[1], ext.at[GX + 1], halo_send.at[1], halo_recv.at[1], {"xy": below, "lev": level})
    up_copy.start()
    down_copy.start()
    lax.fori_loop(1, GX - 1, solve_plane, 0, unroll=3)

    def lev_copies(k, owner):
        peer = lax.rem(level + k, N_LEV)
        kind = jnp.where(peer > level, 0, 1)
        return [
            remote(
                edge.at[kind], seen.at[owner, pl.ds(1, GX)], lev_send.at[k], lev_recv.at[k], {"xy": me, "lev": peer}
            ),
            remote(
                edge.at[kind, GX - 1], seen.at[owner, 0], diag_send.at[0, k], diag_recv.at[0, k],
                {"xy": above, "lev": peer},
            ),
            remote(
                edge.at[kind, 0], seen.at[owner, GX + 1], diag_send.at[1, k], diag_recv.at[1, k],
                {"xy": below, "lev": peer},
            ),
        ]

    def back(k):
        return lax.rem(level + N_LEV - k, N_LEV)

    out_going = [lev_copies(k, level) for k in range(1, N_LEV)]
    in_coming = [lev_copies(k, back(k)) for k in range(1, N_LEV)]
    for i in range(3):
        for group in out_going:
            group[i].start()
    for group in in_coming:
        group[0].wait()

    def correct_plane(at, unused):
        down, upward = carries(ext[at], at, seen)
        fixed[at] = correction(ext[at], down, upward, p_col, e_col)
        return unused

    lax.fori_loop(1, GX + 1, correct_plane, 0, unroll=2)

    def second_plane(x, at):
        stepped = stencil(fixed[x + 1], fixed[x], fixed[x + 2], diff_s[x], wind_s[x])
        solved = product(stepped)
        second[x] = solved
        edges(solved, edge2, at)

    for copy in loads:
        copy.wait()

    parts = ((0, 3), (3, 3), (6, 2))

    def lev2_copies(part, k, owner):
        peer = lax.rem(level + k, N_LEV)
        kind = jnp.where(peer > level, 0, 1)
        begin, size = parts[part]
        return remote(
            edge2.at[kind, pl.ds(begin, size)], seen2.at[owner, pl.ds(begin, size)],
            lev2_send.at[part, k], lev2_recv.at[part, k], {"xy": me, "lev": peer},
        )

    def inner(at, unused):
        second_plane(at + 1, at)
        return unused

    for part in range(2):
        begin, size = parts[part]
        lax.fori_loop(begin, begin + size, inner, 0)
        for k in range(1, N_LEV):
            lev2_copies(part, k, level).start()

    up_copy.wait()
    down_copy.wait()
    for group in in_coming:
        for copy in group[1:]:
            copy.wait()
    correct_plane(0, 0)
    correct_plane(GX + 1, 0)

    @pl.when(me == 0)
    def _():
        fixed[0] = jnp.zeros((ROWS, GY), F32)

    @pl.when(me == N_XY - 1)
    def _():
        fixed[GX + 1] = jnp.zeros((ROWS, GY), F32)

    def outer(i, unused):
        second_plane(i * (GX - 1), i + 6)
        return unused

    lax.fori_loop(0, 2, outer, 0)
    for k in range(1, N_LEV):
        lev2_copies(2, k, level).start()
    for part in range(3):
        for k in range(1, N_LEV):
            lev2_copies(part, k, back(k)).wait()

    def last_carries(at, unused):
        x = jnp.where(at < 6, at + 1, (at - 6) * (GX - 1))
        down, upward = carries(second[x], at, seen2)
        down_out[x] = down
        up_out[x] = upward
        return unused

    lax.fori_loop(0, GX, last_carries, 0, unroll=2)


def finish_kernel(second, down, upward, p_col, e_col, out, planes, sem):
    def copy(x):
        return pltpu.make_async_copy(planes.at[x], out.at[:, x, :], sem.at[x])

    def one(x, unused):
        planes[x] = correction(second[x], down[x], upward[x], p_col, e_col)
        copy(x).start()
        return unused

    lax.fori_loop(0, GX, one, 0)
    for x in range(GX):
        copy(x).wait()


def vmem(*shape, dtype=F32):
    return pltpu.VMEM(shape, dtype)


def whole(count):
    return [pl.BlockSpec(memory_space=pltpu.VMEM)] * count


def somewhere(count):
    return [pl.BlockSpec(memory_space=pltpu.HBM)] * count


def shaped(*shape, dtype=F32):
    return jax.ShapeDtypeStruct(shape, dtype)


def shards(
    euler_field, parcel_mass, dest_device, dest_cell, diffusivity, wind_speed, inverses, lower_coupling, upper_coupling
):
    dma = pltpu.SemaphoreType.DMA
    euler, mass, dest, cell, diffusivity, wind, inv, low, up = [
        pltpu.with_memory_space_constraint(array, pltpu.HBM)
        for array in (
            euler_field.reshape(ROWS, GX, GY), parcel_mass, dest_device.reshape(32, 128), dest_cell.reshape(32, 128),
            diffusivity, wind_speed, inverses, lower_coupling, upper_coupling,
        )
    ]
    routed = pl.pallas_call(
        route_kernel,
        name="route",
        out_shape=[
            shaped(GX, ROWS, GY), shaped(N_XY, BINS, CAP), shaped(N_XY, CAP),
            shaped(ROWS, ROWS, dtype=BF16), shaped(ROWS, ROWS, dtype=BF16),
            shaped(ROWS, 128), shaped(ROWS, 128), shaped(11, BINS, 128),
        ],
        in_specs=somewhere(9),
        out_specs=whole(8),
        scratch_shapes=[
            vmem(GX + 2, ROWS, GY), vmem(GX, LEV, GY), vmem(GX, LEV, GY),
            vmem(BINS, PARC), vmem(32, 128, dtype=I32), vmem(32, 128, dtype=I32),
            vmem(2, BINS, 16, 16), vmem(2, BINS), vmem(2, BINS), vmem(18 * N_XY, CAP),
            vmem(N_XY, BINS, CAP), vmem(N_XY, CAP),
            vmem(16, BLK), vmem(16, BLK), vmem(16, BLK), vmem(16, BLK), vmem(N_LEV, 3, BINS, 128),
            dma((3, GX)), dma((6,)), dma((2,)), dma((2,)), dma((N_XY,)), dma((N_XY,)), dma((N_XY,)), dma((N_XY,)),
            dma((N_LEV,)), dma((N_LEV,)),
        ],
        compiler_params=pltpu.CompilerParams(collective_id=0, has_side_effects=True, vmem_limit_bytes=LIMIT),
    )(euler, mass, dest, cell, diffusivity, wind, inv, low, up)
    first, got_mass, got_code, p_high, p_low, p_col, e_col, factors = routed
    blended = pl.pallas_call(
        deposit_kernel,
        name="deposit",
        out_shape=shaped(GX, ROWS, GY),
        in_specs=whole(3),
        out_specs=pl.BlockSpec(memory_space=pltpu.VMEM),
        scratch_shapes=[
            vmem(SETS, UNITS + WIN, 16, 128), vmem(SETS, UNITS + 8, 128), vmem(SETS, UNITS + 8, 128),
            vmem(N_XY, BLK), vmem(N_XY, BLK), vmem(N_XY, BLK), vmem(N_XY, BLK),
            vmem(GX, BINS + 1, LEV, GY), vmem(BUCKETS + 8, 128, dtype=I32),
            pltpu.SMEM((BUCKETS + 8, 128), I32), dma,
        ],
        compiler_params=pltpu.CompilerParams(vmem_limit_bytes=LIMIT),
    )(got_mass, got_code, first)
    second, down, upward = pl.pallas_call(
        solve_kernel,
        name="solve",
        out_shape=[shaped(GX, ROWS, GY), shaped(GX, BINS, GY), shaped(GX, BINS, GY)],
        in_specs=whole(1) + somewhere(2) + whole(5),
        out_specs=whole(3),
        scratch_shapes=[
            vmem(GX + 2, ROWS, GY), vmem(GX + 2, ROWS, GY), vmem(ROWS, 3 * ROWS, dtype=BF16), vmem(GX, LEV, GY), vmem(GX, LEV, GY),
            vmem(2, GX, BINS, GY), vmem(N_LEV, GX + 2, BINS, GY),
            vmem(2, GX, BINS, GY), vmem(N_LEV, GX, BINS, GY),
            dma((2, GX)), dma((N_LEV,)), dma((N_LEV,)), dma((2, N_LEV)), dma((2, N_LEV)), dma((2,)), dma((2,)),
            dma((3, N_LEV)), dma((3, N_LEV)),
        ],
        compiler_params=pltpu.CompilerParams(collective_id=1, has_side_effects=True, vmem_limit_bytes=LIMIT),
    )(blended, diffusivity, wind, p_high, p_low, p_col, e_col, factors)
    result = pl.pallas_call(
        finish_kernel,
        name="finish",
        out_shape=shaped(ROWS, GX, GY),
        in_specs=whole(5),
        out_specs=pl.BlockSpec(memory_space=pltpu.HBM),
        scratch_shapes=[vmem(GX, ROWS, GY), dma((GX,))],
        compiler_params=pltpu.CompilerParams(vmem_limit_bytes=LIMIT),
    )(second, down, upward, p_col, e_col)
    return result.reshape(BINS, LEV, GX, GY)


def solution(mesh):
    placed = (
        P(None, "lev", "xy", None),
        P(None, ("xy", "lev")),
        P(("xy", "lev"), None),
        P(("xy", "lev")),
        P("lev", "xy", None),
        P("lev", "xy", None),
        P("lev", None, None, None),
        P("lev", None),
        P("lev", None),
    )
    return jax.shard_map(
        shards, mesh=mesh, in_specs=placed, out_specs=P(None, "lev", "xy", None), check_vma=False
    )
```

```python
import functools

import jax
import jax.numpy as jnp
from jax import lax
from jax.experimental import pallas as pl
from jax.experimental.pallas import tpu as pltpu
from jax.sharding import PartitionSpec as P

F32, BF16, I32 = jnp.float32, jnp.bfloat16, jnp.int32
MESH = pl.DeviceIdType.MESH
N_XY, N_LEV, BINS, LEV, GX, GY = 32, 4, 8, 32, 8, 256
ROWS = BINS * LEV
PARC, CAP, BLK = 4096, 256, 256
BUCKETS = 16
NT = (((1,), (1,)), ((), ()))
LIMIT = 24 << 20
SETS = 2
SRC = N_XY // SETS
SPAN = SRC * CAP
UNITS = SPAN // 128
WIN = 4


def iota(shape, dim, dtype=F32):
    return lax.broadcasted_iota(I32, shape, dim).astype(dtype)


def ranks(keys, count, lower):
    n = keys.shape[0]
    masks = [jnp.where(keys == k, 1.0, 0.0) for k in range(count)]
    stack = jnp.concatenate(masks, axis=0).astype(BF16)
    before = (iota((BLK, BLK), 0) < iota((BLK, BLK), 1)).astype(BF16)
    inside = jnp.dot(stack, before, preferred_element_type=F32)
    totals = jnp.dot(stack, jnp.ones((BLK, 128), BF16), preferred_element_type=F32)
    base = jnp.dot(lower, totals.astype(BF16), preferred_element_type=F32)
    wide = jnp.concatenate([base, base], axis=1)
    whole = inside + wide[: inside.shape[0]]
    position = jnp.zeros(keys.shape, F32)
    for k in range(count):
        position += masks[k] * whole[k * n : (k + 1) * n]
    return position, base


def lanes(pieces):
    return jnp.concatenate(pieces, axis=1)


def one_hot(row):
    width = row.shape[1]
    wide = jnp.broadcast_to(row, (BLK, width)).astype(BF16)
    ids = iota((BLK, width), 0, BF16)
    return jnp.where(ids == wide, jnp.ones((BLK, width), BF16), jnp.zeros((BLK, width), BF16))


def sort_slots(values16, high_low, column, target, spot, first, count):
    width = target.shape[1]
    chosen = jnp.broadcast_to(target, (16, width)).astype(BF16)
    zero = jnp.zeros((16, width), BF16)
    parts = [jnp.where(chosen == jnp.array(first + d, BF16), values16, zero) for d in range(count)]
    mine = iota((count, width), 0) + float(first) == target
    codes = jnp.concatenate([jnp.where(mine, high_low, 0.0), jnp.where(mine, column, 0.0)], axis=0)
    weighted = jnp.concatenate(parts + [codes.astype(BF16)], axis=0)
    return lax.dot_general(weighted, spot, NT, preferred_element_type=F32)


def two_parts(values):
    high = values.astype(BF16).astype(F32)
    return jnp.concatenate([high, values - high], axis=0).astype(BF16)


def stencil(centre, before, after, diffusivity, wind):
    shape = (BINS, LEV, GY)
    lane = lax.broadcasted_iota(I32, (ROWS, GY), 1)
    left = jnp.where(lane == 0, 0.0, pltpu.roll(centre, 1, 1))
    right = jnp.where(lane == GY - 1, 0.0, pltpu.roll(centre, GY - 1, 1))
    laplace = (after + before + right + left - 4.0 * centre).reshape(shape)
    drift = (centre - before).reshape(shape)
    result = centre.reshape(shape) + diffusivity[None] * laplace - wind[None] * drift
    return result.reshape(ROWS, GY)


def plane_copies(source, target, sems, at=0):
    return [pltpu.make_async_copy(source.at[:, x, :], target.at[at + x], sems.at[x]) for x in range(GX)]


def remote(src, dst, send, recv, device):
    return pltpu.make_async_remote_copy(
        src_ref=src, dst_ref=dst, send_sem=send, recv_sem=recv, device_id=device, device_id_type=MESH
    )


def compose(inv, low, up, hi_ref, lo_ref, p_ref, e_ref):
    lane16 = lax.broadcasted_iota(I32, (16, ROWS), 1) % LEV
    row16 = lax.broadcasted_iota(I32, (16, ROWS), 0)
    own = lax.broadcasted_iota(I32, (BINS, 16, ROWS), 0) == (
        lax.broadcasted_iota(I32, (BINS, 16, ROWS), 2) // LEV
    )

    def spread(group):
        place = (lane16 == row16 + 16 * group).astype(F32)
        flat = inv[group].reshape(BINS * 16, 16)
        full = jnp.dot(flat, place, precision=lax.Precision.HIGHEST, preferred_element_type=F32)
        return jnp.where(own, full.reshape(BINS, 16, ROWS), 0.0)

    def per_bin(ref, group):
        wide = jnp.broadcast_to(ref[group : group + 1, :].reshape(1, 1, BINS), (BINS, 1, BINS))
        same = lax.broadcasted_iota(I32, (BINS, 1, BINS), 0) == lax.broadcasted_iota(
            I32, (BINS, 1, BINS), 2
        )
        return jnp.sum(jnp.where(same, wide, 0.0), axis=2, keepdims=True)

    t0, t1 = spread(0), spread(1)
    l0, l1, u0, u1 = per_bin(low, 0), per_bin(low, 1), per_bin(up, 0), per_bin(up, 1)
    m0, m1 = inv[0], inv[1]
    m0_first, m0_last = m0[:, :, 0:1], m0[:, :, 15:16]
    m1_first, m1_last = m1[:, :, 0:1], m1[:, :, 15:16]
    tail0 = t0[:, 15:16, :]
    link = (l1 * m1[:, 0:1, 0:1]) * tail0 + t1[:, 0:1, :]
    p0 = t0 + (u0 * m0_last) * link
    p1 = t1 + (l1 * m1_first) * tail0
    full = jnp.concatenate([p0, p1], axis=1).reshape(ROWS, ROWS)
    high = full.astype(BF16)
    hi_ref[...] = high
    lo_ref[...] = (full - high.astype(F32)).astype(BF16)
    passed = l1 * l0 * m0[:, 15:16, 0:1]
    c0 = l0 * m0_first + (u0 * m0_last) * (passed * m1[:, 0:1, 0:1])
    c1 = passed * m1_first
    d0 = (u0 * u1 * m1[:, 0:1, 15:16]) * m0_last
    d1 = u1 * m1_last
    p_ref[...] = jnp.broadcast_to(jnp.concatenate([c0, c1], axis=1), (BINS, LEV, 128)).reshape(ROWS, 128)
    e_ref[...] = jnp.broadcast_to(jnp.concatenate([d0, d1], axis=1), (BINS, LEV, 128)).reshape(ROWS, 128)


def carry_factors(level, all_ref, out_ref):
    alpha = [all_ref[f, 0] for f in range(N_LEV)]
    beta = [all_ref[f, 1] for f in range(N_LEV)]
    gamma = [all_ref[f, 2] for f in range(N_LEV)]
    zero, one = jnp.zeros((BINS, 128), F32), jnp.ones((BINS, 128), F32)
    for f in range(N_LEV):
        down, product = zero, one
        for i in range(f + 1, N_LEV):
            down = jnp.where(level == i, product, down)
            product = product * alpha[i]
        upward, product = zero, one
        for i in range(f - 1, -1, -1):
            upward = jnp.where(level == i, product, upward)
            product = product * beta[i]
        out_ref[f] = down
        out_ref[N_LEV + f] = upward
    sigma = [zero] * N_LEV
    for f in range(N_LEV - 1, 0, -1):
        sigma[f - 1] = gamma[f] + beta[f] * alpha[f] * sigma[f]

    def own(values):
        result = values[0]
        for f in range(1, N_LEV):
            result = jnp.where(level == f, values[f], result)
        return result

    out_ref[8] = own(sigma)
    out_ref[9] = own([sigma[f] * alpha[f] for f in range(N_LEV)])
    out_ref[10] = own([sigma[f] * beta[f] for f in range(N_LEV)])


def route_kernel(
    euler, mass, dest, cell, diffusivity, wind, inv, low, up,
    first, got_mass, got_code, p_high, p_low, p_col, e_col, factors,
    ext, diff_s, wind_s, mass_s, dest_in, cell_in, inv_s, low_s, up_s,
    send_mass, send_code, spot_s, links,
    load_sem, small_sem, halo_send, halo_recv, mass_send, mass_recv, code_send, code_recv, link_send, link_recv,
):
    me, level = lax.axis_index("xy"), lax.axis_index("lev")
    barrier = pltpu.get_barrier_semaphore()

    def greet(k, unused):
        pl.semaphore_signal(
            barrier, inc=1, device_id={"xy": lax.rem(me + k, N_XY), "lev": level}, device_id_type=MESH
        )
        return unused

    lax.fori_loop(1, N_XY, greet, 0)
    for k in range(1, N_LEV):
        pl.semaphore_signal(
            barrier, inc=1, device_id={"xy": me, "lev": lax.rem(level + k, N_LEV)}, device_id_type=MESH
        )

    small = [
        pltpu.make_async_copy(source, target, small_sem.at[i])
        for i, (source, target) in enumerate(
            [(dest, dest_in), (cell, cell_in), (mass, mass_s), (inv, inv_s), (low, low_s), (up, up_s)]
        )
    ]
    field = plane_copies(euler, ext, load_sem.at[0], 1)
    coefficients = plane_copies(diffusivity, diff_s, load_sem.at[1]) + plane_copies(wind, wind_s, load_sem.at[2])
    for copy in small + field + coefficients:
        copy.start()

    above, below = lax.rem(me + 1, N_XY), lax.rem(me + N_XY - 1, N_XY)
    up_copy = remote(ext.at[GX], ext.at[0], halo_send.at[0], halo_recv.at[0], {"xy": above, "lev": level})
    down_copy = remote(ext.at[1], ext.at[GX + 1], halo_send.at[1], halo_recv.at[1], {"xy": below, "lev": level})
    field[0].wait()
    field[GX - 1].wait()
    pl.semaphore_wait(barrier, N_XY - 1 + N_LEV - 1)
    up_copy.start()
    down_copy.start()

    def wide(ref):
        return lanes([ref[pl.ds(0, 16, stride=2), :], ref[pl.ds(1, 16, stride=2), :]])

    def flat(rows):
        return lanes([rows[i : i + 1] for i in range(16)])

    for copy in small[:3]:
        copy.wait()
    target = wide(dest_in).astype(F32)
    cells = wide(cell_in)
    levels = cells // (GX * GY)
    bucket = (cells // GY) % GX * 2 + levels // 16
    high_low = flat((bucket * 16 + levels % 16 + 1).astype(F32))
    column = flat((cells % GY).astype(F32))
    r, c = (lax.broadcasted_iota(I32, (512, 512), d) for d in (0, 1))
    lower = jnp.where((c < r) & (c // 16 == r // 16), 1.0, 0.0).astype(BF16)
    slot, unused_base = ranks(target, N_XY, lower)
    spot_s[...] = one_hot(flat(slot))
    values = two_parts(mass_s[...])
    flat_target = flat(target)

    def copies(other, slot_id):
        device = {"xy": other, "lev": level}
        return (
            remote(send_mass.at[other], got_mass.at[slot_id], mass_send.at[other], mass_recv.at[slot_id], device),
            remote(
                send_code.at[pl.ds(other, 1)], got_code.at[pl.ds(slot_id, 1)],
                code_send.at[other], code_recv.at[slot_id], device,
            ),
        )

    half = N_XY // 2
    for begin in (0, half):
        table = sort_slots(values, high_low, column, flat_target, spot_s[...], begin, half)
        masses = table[: 16 * half].reshape(half, 16, CAP)
        send_mass[begin : begin + half] = masses[:, :8] + masses[:, 8:]
        send_code[begin : begin + half] = table[16 * half : 17 * half] * 256.0 + table[17 * half :]

        def send(k, unused):
            other = begin + lax.rem(me + k, half)

            @pl.when(other != me)
            def _():
                for copy in copies(other, me):
                    copy.start()

            return unused

        lax.fori_loop(0, half, send, 0)
    got_mass[me] = send_mass[me]
    got_code[pl.ds(me, 1), :] = send_code[pl.ds(me, 1), :]

    for copy in small[3:]:
        copy.wait()
    compose(inv_s, low_s, up_s, p_high, p_low, p_col, e_col)
    links[level, 0] = p_col[pl.ds(LEV - 1, BINS, stride=LEV), :]
    links[level, 1] = e_col[pl.ds(0, BINS, stride=LEV), :]
    links[level, 2] = p_col[pl.ds(0, BINS, stride=LEV), :]

    def link_copy(k, owner):
        peer = lax.rem(level + k, N_LEV)
        return remote(
            links.at[owner], links.at[owner], link_send.at[k], link_recv.at[k], {"xy": me, "lev": peer}
        )

    for k in range(1, N_LEV):
        link_copy(k, level).start()

    for copy in field[1 : GX - 1] + coefficients:
        copy.wait()

    def step(x, unused):
        first[x] = stencil(ext[x + 1], ext[x], ext[x + 2], diff_s[x], wind_s[x])
        return unused

    lax.fori_loop(1, GX - 1, step, 0)
    up_copy.wait()
    down_copy.wait()

    @pl.when(me == 0)
    def _():
        ext[0] = jnp.zeros((ROWS, GY), F32)

    @pl.when(me == N_XY - 1)
    def _():
        ext[GX + 1] = jnp.zeros((ROWS, GY), F32)

    lax.fori_loop(0, 2, lambda i, u: step(i * (GX - 1), u), 0)

    for k in range(1, N_LEV):
        link_copy(k, lax.rem(level + N_LEV - k, N_LEV)).wait()
    carry_factors(level, links, factors)

    def finish(k, unused):
        for copy in copies(lax.rem(me + k, N_XY), me):
            copy.wait_send()
        for copy in copies(me, lax.rem(me + k, N_XY)):
            copy.wait_recv()
        return unused

    lax.fori_loop(1, N_XY, finish, 0)


def deposit_kernel(
    got_mass, got_code, first, blended,
    rows_u, hl_u, col_u, hp_s, lp_s, hl_s, col_s, total, starts_v, starts_s, sem,
):
    code = got_code[...].astype(I32)
    hl = code // 256
    col = code % 256
    valid = hl > 0
    key = jnp.where(valid, (hl - 1) // 16, -1).astype(F32)
    hl_s[...] = hl.astype(F32)
    col_s[...] = col.astype(F32)
    r, c = (lax.broadcasted_iota(I32, (N_XY * (BUCKETS + 1), 512), d) for d in (0, 1))
    lower = jnp.where((c < r) & ((c % N_XY) // SRC == (r % N_XY) // SRC), 1.0, 0.0).astype(BF16)
    position, base = ranks(key, BUCKETS, lower)
    place = position.astype(I32)
    hp_s[...] = jnp.where(valid, place // BLK, -1).astype(F32)
    lp_s[...] = (place % BLK).astype(F32)
    lane = lax.broadcasted_iota(I32, (1, 128), 1)
    longest = jnp.zeros((1, 128), I32)
    before = None
    for k in range(BUCKETS + 1):
        start = jnp.zeros((1, 128), F32)
        for g in range(SETS):
            at = N_XY * k + SRC * g
            start = jnp.where(lane == g, base[at : at + 1, :], start)
        start = start.astype(I32)
        starts_v[k : k + 1, :] = start
        if k:
            longest = jnp.maximum(longest, start - before // 128 * 128)
        before = start
    starts_v[BUCKETS + 1 : BUCKETS + 2, :] = longest
    to_scalars = pltpu.make_async_copy(starts_v, starts_s, sem)
    to_scalars.start()

    def one_set(g, unused):
        take = lambda ref: lanes([ref[pl.ds(g * SRC + i, 1), :] for i in range(SRC)])
        values = lanes([two_parts(got_mass[g * SRC + i]) for i in range(SRC)])
        table = sort_slots(values, take(hl_s), take(col_s), take(hp_s), one_hot(take(lp_s)), 0, SRC)
        for half in range(2):
            side = slice(128 * half, 128 * half + 128)
            for d in range(SRC):
                rows_u[g, 2 * d + half] = table[16 * d : 16 * d + 16, side]
            hl_u[g, pl.ds(half, SRC, stride=2), :] = table[16 * SRC : 17 * SRC, side]
            col_u[g, pl.ds(half, SRC, stride=2), :] = table[17 * SRC : 18 * SRC, side]
        rows_u[g, UNITS:] = jnp.zeros((WIN, 16, 128), F32)
        hl_u[g, UNITS:, :] = jnp.zeros((8, 128), F32)
        col_u[g, UNITS:, :] = jnp.zeros((8, 128), F32)
        return unused

    lax.fori_loop(0, SETS, one_set, 0)
    to_scalars.wait()

    def place_of(k):
        return k // 2, pl.ds(pl.multiple_of((k % 2) * 16, 16), 16)

    def window(k, t):
        first_code = (k * 16 + 1).astype(F32)
        at = [jnp.minimum(starts_s[k, g] // 128 + WIN * t, UNITS) for g in range(SETS)]
        units = [(g, at[g] + i) for g in range(SETS) for i in range(WIN)]
        hl_row = lanes([hl_u[g, pl.ds(u, 1), :] for g, u in units])
        col_row = lanes([col_u[g, pl.ds(u, 1), :] for g, u in units])
        rows = lanes([rows_u[g, u] for g, u in units])
        width = 128 * WIN * SETS
        mine = jnp.broadcast_to(hl_row, (16, width)) == iota((16, width), 0) + first_code
        spread = [jnp.where(mine, jnp.broadcast_to(rows[q : q + 1, :], (16, width)), 0.0) for q in range(16)]
        spread.insert(8, jnp.where(mine, 1.0, 0.0))
        weighted = jnp.concatenate(spread, axis=0).astype(BF16)
        table = lax.dot_general(weighted, one_hot(col_row), NT, preferred_element_type=F32)
        table = table.reshape(17, 16, GY)
        return jnp.concatenate([table[:8] + table[9:], table[8:9]], axis=0)

    def one_bucket(k, unused):
        x, levels = place_of(k)
        total[x, :, levels, :] = window(k, 0)
        return unused

    lax.fori_loop(0, BUCKETS, one_bucket, 0, unroll=16)

    def rest(k, unused):
        x, levels = place_of(k)
        rounds = jnp.int32(1)
        for g in range(SETS):
            span = starts_s[k + 1, g] - starts_s[k, g] // 128 * 128
            rounds = jnp.maximum(rounds, (span + 128 * WIN - 1) // (128 * WIN))

        def again(t, unused):
            total[x, :, levels, :] += window(k, t)
            return unused

        lax.fori_loop(1, rounds, again, 0)
        return unused

    most = starts_s[BUCKETS + 1, 0]
    for g in range(1, SETS):
        most = jnp.maximum(most, starts_s[BUCKETS + 1, g])

    @pl.when(most > 128 * WIN)
    def _():
        lax.fori_loop(0, BUCKETS, rest, 0)

    def blend(x, unused):
        counts = total[x, 8]
        share = counts / (counts + 2.0)
        old = first[x].reshape(BINS, LEV, GY)
        mixed = (1.0 - share)[None] * old + share[None] * total[x, 0:8]
        blended[x] = mixed.reshape(ROWS, GY)
        return unused

    lax.fori_loop(0, GX, blend, 0)


def correction(values, down, upward, p_col, e_col):
    shape = (BINS, LEV, GY)
    p_wide = lanes([p_col[...], p_col[...]]).reshape(shape)
    e_wide = lanes([e_col[...], e_col[...]]).reshape(shape)
    result = values.reshape(shape) + p_wide * down[:, None, :] + e_wide * upward[:, None, :]
    return result.reshape(ROWS, GY)


PARTS = ((0, 2), (2, 3), (5, 3))


def solve_kernel(
    blended, diffusivity, wind, p_high, p_low, p_col, e_col, factors,
    second, down_out, up_out,
    ext, fixed, triple, diff_s, wind_s, edge, seen, seen_halo, edge2, seen2,
    load_sem, lev_send, lev_recv, diag_send, diag_recv, halo_send, halo_recv,
):
    me, level = lax.axis_index("xy"), lax.axis_index("lev")
    above, below = lax.rem(me + 1, N_XY), lax.rem(me + N_XY - 1, N_XY)
    barrier = pltpu.get_barrier_semaphore()
    for k in range(N_LEV):
        peer = lax.rem(level + k, N_LEV)
        for where in ([me] if k else []) + [above, below]:
            pl.semaphore_signal(barrier, inc=1, device_id={"xy": where, "lev": peer}, device_id_type=MESH)
    loads = plane_copies(diffusivity, diff_s, load_sem.at[0]) + plane_copies(wind, wind_s, load_sem.at[1])
    for copy in loads:
        copy.start()
    triple[:, 0:ROWS] = p_high[...]
    triple[:, ROWS : 2 * ROWS] = p_high[...]
    triple[:, 2 * ROWS :] = p_low[...]

    def product(values):
        high = values.astype(BF16)
        low = (values - high.astype(F32)).astype(BF16)
        return jnp.dot(triple[...], jnp.concatenate([high, low, high], axis=0), preferred_element_type=F32)

    def both(i):
        return lanes([factors[i], factors[i]])

    def edges(values, target, place):
        blocks = values.reshape(BINS, LEV, GY)
        last, start = blocks[:, LEV - 1, :], blocks[:, 0, :]
        target[0, place] = last
        target[1, place] = start + both(10) * last

    def carries(values, seen_at):
        down = jnp.zeros((BINS, GY), F32)
        upward = jnp.zeros((BINS, GY), F32)
        for f in range(N_LEV):
            here = jnp.where(level == f, 0.0, seen_at(f))
            down += both(f) * here
            upward += both(N_LEV + f) * here
        tail = values.reshape(BINS, LEV, GY)[:, LEV - 1, :]
        return down, upward + both(8) * tail + both(9) * down

    def peer_of(k):
        return lax.rem(level + k, N_LEV)

    def back(k):
        return lax.rem(level + N_LEV - k, N_LEV)

    def kind(k):
        return jnp.where(peer_of(k) > level, 0, 1)

    def lev_copies(turn, part, own):
        source, target = ((edge, seen), (edge2, seen2))[turn]
        span = pl.ds(*PARTS[part])
        return [
            remote(
                source.at[kind(k), span], target.at[level if own else back(k), span],
                lev_send.at[turn, part, k], lev_recv.at[turn, part, k], {"xy": me, "lev": peer_of(k)},
            )
            for k in range(1, N_LEV)
        ]

    def diag_copies(own):
        return [
            remote(
                edge.at[kind(k), 1 - side], seen_halo.at[side, level if own else back(k)],
                diag_send.at[side, k], diag_recv.at[side, k], {"xy": where, "lev": peer_of(k)},
            )
            for side, where in enumerate((above, below))
            for k in range(1, N_LEV)
        ]

    def start(copies):
        for copy in copies:
            copy.start()

    def wait(copies):
        for copy in copies:
            copy.wait()

    def solve_plane(x, place):
        solved = product(blended[x])
        ext[x + 1] = solved
        edges(solved, edge, place)

    def some(function, begin, count, shift):
        def one(i, unused):
            function(i, i + shift)
            return unused

        lax.fori_loop(begin, begin + count, one, 0, unroll=count)

    solve_plane(0, 0)
    solve_plane(GX - 1, 1)
    pl.semaphore_wait(barrier, 3 * N_LEV - 1)
    halos = [
        remote(ext.at[GX], ext.at[0], halo_send.at[0], halo_recv.at[0], {"xy": above, "lev": level}),
        remote(ext.at[1], ext.at[GX + 1], halo_send.at[1], halo_recv.at[1], {"xy": below, "lev": level}),
    ]
    start(diag_copies(True) + lev_copies(0, 0, True) + halos)
    some(solve_plane, 1, 3, 1)
    start(lev_copies(0, 1, True))
    some(solve_plane, 4, 3, 1)
    start(lev_copies(0, 2, True))

    def correct_plane(x, place):
        down, upward = carries(ext[x + 1], lambda f: seen[f, place])
        fixed[x + 1] = correction(ext[x + 1], down, upward, p_col, e_col)

    def correct_halo(at, side):
        down, upward = carries(ext[at], lambda f: seen_halo[side, f])
        fixed[at] = correction(ext[at], down, upward, p_col, e_col)

    def second_plane(x, place):
        stepped = stencil(fixed[x + 1], fixed[x], fixed[x + 2], diff_s[x], wind_s[x])
        solved = product(stepped)
        second[x] = solved
        edges(solved, edge2, place)

    def last_plane(x, place):
        down, upward = carries(second[x], lambda f: seen2[f, place])
        second[x] = correction(second[x], down, upward, p_col, e_col)

    wait(loads)
    wait(lev_copies(0, 0, False) + lev_copies(0, 1, False))
    correct_plane(0, 0)
    correct_plane(GX - 1, 1)
    some(correct_plane, 1, 3, 1)
    some(second_plane, 1, 2, 1)
    wait(lev_copies(0, 2, False))
    some(correct_plane, 4, 3, 1)
    second_plane(3, 4)
    start(lev_copies(1, 1, True))
    some(second_plane, 4, 3, 1)
    start(lev_copies(1, 2, True))
    wait(halos + diag_copies(False))
    correct_halo(0, 0)
    correct_halo(GX + 1, 1)

    @pl.when(me == 0)
    def _():
        fixed[0] = jnp.zeros((ROWS, GY), F32)

    @pl.when(me == N_XY - 1)
    def _():
        fixed[GX + 1] = jnp.zeros((ROWS, GY), F32)

    second_plane(0, 0)
    second_plane(GX - 1, 1)
    start(lev_copies(1, 0, True))
    for part in (1, 2):
        wait(lev_copies(1, part, False))
        some(last_plane, 3 * part - 2, 3, 1)
    wait(lev_copies(1, 0, False))
    for side in range(2):
        down, upward = carries(second[side * (GX - 1)], lambda f: seen2[f, side])
        down_out[side] = down
        up_out[side] = upward


def finish_kernel(second, down, upward, p_col, e_col, out, outer, sem):
    inner = [pltpu.make_async_copy(second.at[x], out.at[:, x, :], sem.at[x]) for x in range(1, GX - 1)]
    for copy in inner:
        copy.start()
    last = []
    for side in range(2):
        x = side * (GX - 1)
        outer[side] = correction(second[x], down[side], upward[side], p_col, e_col)
        last.append(pltpu.make_async_copy(outer.at[side], out.at[:, x, :], sem.at[x]))
        last[side].start()
    for copy in inner + last:
        copy.wait()


def vmem(*shape, dtype=F32):
    return pltpu.VMEM(shape, dtype)


def whole(count):
    return [pl.BlockSpec(memory_space=pltpu.VMEM)] * count


def somewhere(count):
    return [pl.BlockSpec(memory_space=pltpu.HBM)] * count


def shaped(*shape, dtype=F32):
    return jax.ShapeDtypeStruct(shape, dtype)


def shards(
    euler_field, parcel_mass, dest_device, dest_cell, diffusivity, wind_speed, inverses, lower_coupling, upper_coupling
):
    dma = pltpu.SemaphoreType.DMA
    euler, mass, dest, cell, diffusivity, wind, inv, low, up = [
        pltpu.with_memory_space_constraint(array, pltpu.HBM)
        for array in (
            euler_field.reshape(ROWS, GX, GY), parcel_mass, dest_device.reshape(32, 128), dest_cell.reshape(32, 128),
            diffusivity, wind_speed, inverses, lower_coupling, upper_coupling,
        )
    ]
    routed = pl.pallas_call(
        route_kernel,
        name="route",
        out_shape=[
            shaped(GX, ROWS, GY), shaped(N_XY, BINS, CAP), shaped(N_XY, CAP),
            shaped(ROWS, ROWS, dtype=BF16), shaped(ROWS, ROWS, dtype=BF16),
            shaped(ROWS, 128), shaped(ROWS, 128), shaped(11, BINS, 128),
        ],
        in_specs=somewhere(9),
        out_specs=whole(8),
        scratch_shapes=[
            vmem(GX + 2, ROWS, GY), vmem(GX, LEV, GY), vmem(GX, LEV, GY),
            vmem(BINS, PARC), vmem(32, 128, dtype=I32), vmem(32, 128, dtype=I32),
            vmem(2, BINS, 16, 16), vmem(2, BINS), vmem(2, BINS),
            vmem(N_XY, BINS, CAP), vmem(N_XY, CAP), vmem(CAP, PARC, dtype=BF16), vmem(N_LEV, 3, BINS, 128),
            dma((3, GX)), dma((6,)), dma((2,)), dma((2,)), dma((N_XY,)), dma((N_XY,)), dma((N_XY,)), dma((N_XY,)),
            dma((N_LEV,)), dma((N_LEV,)),
        ],
        compiler_params=pltpu.CompilerParams(collective_id=0, has_side_effects=True, vmem_limit_bytes=LIMIT),
    )(euler, mass, dest, cell, diffusivity, wind, inv, low, up)
    first, got_mass, got_code, p_high, p_low, p_col, e_col, factors = routed
    blended = pl.pallas_call(
        deposit_kernel,
        name="deposit",
        out_shape=shaped(GX, ROWS, GY),
        in_specs=whole(3),
        out_specs=pl.BlockSpec(memory_space=pltpu.VMEM),
        scratch_shapes=[
            vmem(SETS, UNITS + WIN, 16, 128), vmem(SETS, UNITS + 8, 128), vmem(SETS, UNITS + 8, 128),
            vmem(N_XY, BLK), vmem(N_XY, BLK), vmem(N_XY, BLK), vmem(N_XY, BLK),
            vmem(GX, BINS + 1, LEV, GY), vmem(BUCKETS + 8, 128, dtype=I32),
            pltpu.SMEM((BUCKETS + 8, 128), I32), dma,
        ],
        compiler_params=pltpu.CompilerParams(vmem_limit_bytes=LIMIT),
    )(got_mass, got_code, first)
    second, down, upward = pl.pallas_call(
        solve_kernel,
        name="solve",
        out_shape=[shaped(GX, ROWS, GY), shaped(2, BINS, GY), shaped(2, BINS, GY)],
        in_specs=whole(1) + somewhere(2) + whole(5),
        out_specs=whole(3),
        scratch_shapes=[
            vmem(GX + 2, ROWS, GY), vmem(GX + 2, ROWS, GY), vmem(ROWS, 3 * ROWS, dtype=BF16),
            vmem(GX, LEV, GY), vmem(GX, LEV, GY),
            vmem(2, GX, BINS, GY), vmem(N_LEV, GX, BINS, GY), vmem(2, N_LEV, BINS, GY),
            vmem(2, GX, BINS, GY), vmem(N_LEV, GX, BINS, GY),
            dma((2, GX)), dma((2, 3, N_LEV)), dma((2, 3, N_LEV)), dma((2, N_LEV)), dma((2, N_LEV)), dma((2,)), dma((2,)),
        ],
        compiler_params=pltpu.CompilerParams(collective_id=1, has_side_effects=True, vmem_limit_bytes=LIMIT),
    )(blended, diffusivity, wind, p_high, p_low, p_col, e_col, factors)
    result = pl.pallas_call(
        finish_kernel,
        name="finish",
        out_shape=shaped(ROWS, GX, GY),
        in_specs=whole(5),
        out_specs=pl.BlockSpec(memory_space=pltpu.HBM),
        scratch_shapes=[vmem(2, ROWS, GY), dma((GX,))],
        compiler_params=pltpu.CompilerParams(vmem_limit_bytes=LIMIT),
    )(second, down, upward, p_col, e_col)
    return result.reshape(BINS, LEV, GX, GY)


def solution(mesh):
    placed = (
        P(None, "lev", "xy", None),
        P(None, ("xy", "lev")),
        P(("xy", "lev"), None),
        P(("xy", "lev")),
        P("lev", "xy", None),
        P("lev", "xy", None),
        P("lev", None, None, None),
        P("lev", None),
        P("lev", None),
    )
    return jax.shard_map(
        shards, mesh=mesh, in_specs=placed, out_specs=P(None, "lev", "xy", None), check_vma=False
    )
```

```python
import functools

import jax
import jax.numpy as jnp
from jax import lax
from jax.experimental import pallas as pl
from jax.experimental.pallas import tpu as pltpu
from jax.sharding import PartitionSpec as P

F32, BF16, I32 = jnp.float32, jnp.bfloat16, jnp.int32
MESH = pl.DeviceIdType.MESH
N_XY, N_LEV, BINS, LEV, GX, GY = 32, 4, 8, 32, 8, 256
ROWS = BINS * LEV
PARC, CAP, BLK = 4096, 256, 256
BUCKETS = 16
NT = (((1,), (1,)), ((), ()))
LIMIT = 24 << 20
SETS = 2
SRC = N_XY // SETS
SPAN = SRC * CAP
UNITS = SPAN // 128
WIN = 4


def iota(shape, dim, dtype=F32):
    return lax.broadcasted_iota(I32, shape, dim).astype(dtype)


def ranks(keys, count, lower):
    n = keys.shape[0]
    masks = [jnp.where(keys == k, 1.0, 0.0) for k in range(count)]
    stack = jnp.concatenate(masks, axis=0).astype(BF16)
    before = (iota((BLK, BLK), 0) < iota((BLK, BLK), 1)).astype(BF16)
    inside = jnp.dot(stack, before, preferred_element_type=F32)
    totals = jnp.dot(stack, jnp.ones((BLK, 128), BF16), preferred_element_type=F32)
    base = jnp.dot(lower, totals.astype(BF16), preferred_element_type=F32)
    wide = jnp.concatenate([base, base], axis=1)
    whole = inside + wide[: inside.shape[0]]
    position = jnp.zeros(keys.shape, F32)
    for k in range(count):
        position += masks[k] * whole[k * n : (k + 1) * n]
    return position, base


def lanes(pieces):
    return jnp.concatenate(pieces, axis=1)


def one_hot(row):
    width = row.shape[1]
    wide = jnp.broadcast_to(row, (BLK, width)).astype(BF16)
    ids = iota((BLK, width), 0, BF16)
    return jnp.where(ids == wide, jnp.ones((BLK, width), BF16), jnp.zeros((BLK, width), BF16))


def sort_slots(values16, high_low, column, target, spot, first, count):
    width = target.shape[1]
    chosen = jnp.broadcast_to(target, (16, width)).astype(BF16)
    zero = jnp.zeros((16, width), BF16)
    parts = [jnp.where(chosen == jnp.array(first + d, BF16), values16, zero) for d in range(count)]
    mine = iota((count, width), 0) + float(first) == target
    codes = jnp.concatenate([jnp.where(mine, high_low, 0.0), jnp.where(mine, column, 0.0)], axis=0)
    weighted = jnp.concatenate(parts + [codes.astype(BF16)], axis=0)
    return lax.dot_general(weighted, spot, NT, preferred_element_type=F32)


def two_parts(values):
    high = values.astype(BF16).astype(F32)
    return jnp.concatenate([high, values - high], axis=0).astype(BF16)


def stencil(centre, before, after, diffusivity, wind):
    shape = (BINS, LEV, GY)
    lane = lax.broadcasted_iota(I32, (ROWS, GY), 1)
    left = jnp.where(lane == 0, 0.0, pltpu.roll(centre, 1, 1))
    right = jnp.where(lane == GY - 1, 0.0, pltpu.roll(centre, GY - 1, 1))
    laplace = (after + before + right + left - 4.0 * centre).reshape(shape)
    drift = (centre - before).reshape(shape)
    result = centre.reshape(shape) + diffusivity[None] * laplace - wind[None] * drift
    return result.reshape(ROWS, GY)


def at_edges(me, upward, downward, action):
    @pl.when(me < N_XY - 1)
    def _():
        for copy in upward:
            copy.start() if action == "start" else copy.wait_send()
        for copy in downward if action == "wait" else []:
            copy.wait_recv()

    @pl.when(me > 0)
    def _():
        for copy in downward:
            copy.start() if action == "start" else copy.wait_send()
        for copy in upward if action == "wait" else []:
            copy.wait_recv()


def plane_copies(source, target, sems, at=0):
    return [pltpu.make_async_copy(source.at[:, x, :], target.at[at + x], sems.at[x]) for x in range(GX)]


def remote(src, dst, send, recv, device):
    return pltpu.make_async_remote_copy(
        src_ref=src, dst_ref=dst, send_sem=send, recv_sem=recv, device_id=device, device_id_type=MESH
    )


def compose(inv, low, up, triple, p_ref, e_ref):
    lane16 = lax.broadcasted_iota(I32, (16, ROWS), 1) % LEV
    row16 = lax.broadcasted_iota(I32, (16, ROWS), 0)
    own = lax.broadcasted_iota(I32, (BINS, 16, ROWS), 0) == (
        lax.broadcasted_iota(I32, (BINS, 16, ROWS), 2) // LEV
    )

    def spread(group):
        place = (lane16 == row16 + 16 * group).astype(F32)
        flat = inv[group].reshape(BINS * 16, 16)
        full = jnp.dot(flat, place, precision=lax.Precision.HIGHEST, preferred_element_type=F32)
        return jnp.where(own, full.reshape(BINS, 16, ROWS), 0.0)

    def per_bin(ref, group):
        wide = jnp.broadcast_to(ref[group : group + 1, :].reshape(1, 1, BINS), (BINS, 1, BINS))
        same = lax.broadcasted_iota(I32, (BINS, 1, BINS), 0) == lax.broadcasted_iota(
            I32, (BINS, 1, BINS), 2
        )
        return jnp.sum(jnp.where(same, wide, 0.0), axis=2, keepdims=True)

    t0, t1 = spread(0), spread(1)
    l0, l1, u0, u1 = per_bin(low, 0), per_bin(low, 1), per_bin(up, 0), per_bin(up, 1)
    m0, m1 = inv[0], inv[1]
    m0_first, m0_last = m0[:, :, 0:1], m0[:, :, 15:16]
    m1_first, m1_last = m1[:, :, 0:1], m1[:, :, 15:16]
    tail0 = t0[:, 15:16, :]
    link = (l1 * m1[:, 0:1, 0:1]) * tail0 + t1[:, 0:1, :]
    p0 = t0 + (u0 * m0_last) * link
    p1 = t1 + (l1 * m1_first) * tail0
    full = jnp.concatenate([p0, p1], axis=1).reshape(ROWS, ROWS)
    high = full.astype(BF16)
    triple[:, 0:ROWS] = high
    triple[:, ROWS : 2 * ROWS] = high
    triple[:, 2 * ROWS :] = (full - high.astype(F32)).astype(BF16)
    passed = l1 * l0 * m0[:, 15:16, 0:1]
    c0 = l0 * m0_first + (u0 * m0_last) * (passed * m1[:, 0:1, 0:1])
    c1 = passed * m1_first
    d0 = (u0 * u1 * m1[:, 0:1, 15:16]) * m0_last
    d1 = u1 * m1_last
    p_ref[...] = jnp.broadcast_to(jnp.concatenate([c0, c1], axis=1), (BINS, LEV, 128)).reshape(ROWS, 128)
    e_ref[...] = jnp.broadcast_to(jnp.concatenate([d0, d1], axis=1), (BINS, LEV, 128)).reshape(ROWS, 128)


def carry_factors(level, all_ref, out_ref):
    alpha = [all_ref[f, 0] for f in range(N_LEV)]
    beta = [all_ref[f, 1] for f in range(N_LEV)]
    gamma = [all_ref[f, 2] for f in range(N_LEV)]
    zero, one = jnp.zeros((BINS, 128), F32), jnp.ones((BINS, 128), F32)
    for f in range(N_LEV):
        down, product = zero, one
        for i in range(f + 1, N_LEV):
            down = jnp.where(level == i, product, down)
            product = product * alpha[i]
        upward, product = zero, one
        for i in range(f - 1, -1, -1):
            upward = jnp.where(level == i, product, upward)
            product = product * beta[i]
        out_ref[f] = down
        out_ref[N_LEV + f] = upward
    sigma = [zero] * N_LEV
    for f in range(N_LEV - 1, 0, -1):
        sigma[f - 1] = gamma[f] + beta[f] * alpha[f] * sigma[f]

    def own(values):
        result = values[0]
        for f in range(1, N_LEV):
            result = jnp.where(level == f, values[f], result)
        return result

    out_ref[8] = own(sigma)
    out_ref[9] = own([sigma[f] * alpha[f] for f in range(N_LEV)])
    out_ref[10] = own([sigma[f] * beta[f] for f in range(N_LEV)])


def route_kernel(
    euler, mass, dest, cell, diffusivity, wind, inv, low, up,
    first, got_mass, got_code, order, triple, p_col, e_col, factors,
    ext, diff_s, wind_s, mass_s, dest_in, cell_in, inv_s, low_s, up_s,
    send_mass, send_code, spot_s, links,
    load_sem, small_sem, halo_send, halo_recv, mass_send, mass_recv, code_send, code_recv, link_send, link_recv,
):
    me, level = lax.axis_index("xy"), lax.axis_index("lev")
    barrier = pltpu.get_barrier_semaphore()

    def greet(k, unused):
        pl.semaphore_signal(
            barrier, inc=1, device_id={"xy": lax.rem(me + k, N_XY), "lev": level}, device_id_type=MESH
        )
        return unused

    lax.fori_loop(1, N_XY, greet, 0)
    for k in range(1, N_LEV):
        pl.semaphore_signal(
            barrier, inc=1, device_id={"xy": me, "lev": lax.rem(level + k, N_LEV)}, device_id_type=MESH
        )

    small = [
        pltpu.make_async_copy(source, target, small_sem.at[i])
        for i, (source, target) in enumerate(
            [(dest, dest_in), (cell, cell_in), (mass, mass_s), (inv, inv_s), (low, low_s), (up, up_s)]
        )
    ]
    field = plane_copies(euler, ext, load_sem.at[0], 1)
    coefficients = plane_copies(diffusivity, diff_s, load_sem.at[1]) + plane_copies(wind, wind_s, load_sem.at[2])
    for copy in small[:3] + [field[0], field[GX - 1]]:
        copy.start()

    above, below = lax.rem(me + 1, N_XY), lax.rem(me + N_XY - 1, N_XY)
    up_copy = remote(ext.at[GX], ext.at[0], halo_send.at[0], halo_recv.at[0], {"xy": above, "lev": level})
    down_copy = remote(ext.at[1], ext.at[GX + 1], halo_send.at[1], halo_recv.at[1], {"xy": below, "lev": level})
    def wide(ref):
        return lanes([ref[pl.ds(0, 16, stride=2), :], ref[pl.ds(1, 16, stride=2), :]])

    def flat(rows):
        return lanes([rows[i : i + 1] for i in range(16)])

    for copy in small[:3]:
        copy.wait()
    target = wide(dest_in).astype(F32)
    cells = wide(cell_in)
    levels = cells // (GX * GY)
    bucket = (cells // GY) % GX * 2 + levels // 16
    high_low = flat((bucket * 16 + levels % 16 + 1).astype(F32))
    column = flat((cells % GY).astype(F32))
    r, c = (lax.broadcasted_iota(I32, (512, 512), d) for d in (0, 1))
    lower = jnp.where((c < r) & (c // 16 == r // 16), 1.0, 0.0).astype(BF16)
    slot, unused_base = ranks(target, N_XY, lower)
    for copy in small[3:] + field[1 : GX - 1] + coefficients:
        copy.start()
    field[0].wait()
    field[GX - 1].wait()
    pl.semaphore_wait(barrier, N_XY - 1 + N_LEV - 1)
    at_edges(me, [up_copy], [down_copy], "start")
    spot_s[...] = one_hot(flat(slot))
    values = two_parts(mass_s[...])
    flat_target = flat(target)

    def copies(other, slot_id):
        device = {"xy": other, "lev": level}
        return (
            remote(send_mass.at[other], got_mass.at[slot_id], mass_send.at[other], mass_recv.at[slot_id], device),
            remote(
                send_code.at[pl.ds(other, 1)], got_code.at[pl.ds(slot_id, 1)],
                code_send.at[other], code_recv.at[slot_id], device,
            ),
        )

    half = N_XY // 2
    for begin in (0, half):
        table = sort_slots(values, high_low, column, flat_target, spot_s[...], begin, half)
        masses = table[: 16 * half].reshape(half, 16, CAP)
        send_mass[begin : begin + half] = masses[:, :8] + masses[:, 8:]
        send_code[begin : begin + half] = table[16 * half : 17 * half] * 256.0 + table[17 * half :]

        def send(k, unused):
            other = begin + lax.rem(me + k, half)

            @pl.when(other != me)
            def _():
                for copy in copies(other, me):
                    copy.start()

            return unused

        lax.fori_loop(0, half, send, 0)
    got_mass[me] = send_mass[me]
    got_code[pl.ds(me, 1), :] = send_code[pl.ds(me, 1), :]

    for copy in small[3:]:
        copy.wait()
    compose(inv_s, low_s, up_s, triple, p_col, e_col)
    r, c = (lax.broadcasted_iota(I32, (N_XY * (BUCKETS + 1), N_XY * BUCKETS), d) for d in (0, 1))
    order[...] = jnp.where((c < r) & (c % N_XY // SRC == r % N_XY // SRC), 1.0, 0.0).astype(BF16)
    links[level, 0] = p_col[pl.ds(LEV - 1, BINS, stride=LEV), :]
    links[level, 1] = e_col[pl.ds(0, BINS, stride=LEV), :]
    links[level, 2] = p_col[pl.ds(0, BINS, stride=LEV), :]

    def link_copy(k, owner):
        peer = lax.rem(level + k, N_LEV)
        return remote(
            links.at[owner], links.at[owner], link_send.at[k], link_recv.at[k], {"xy": me, "lev": peer}
        )

    for k in range(1, N_LEV):
        link_copy(k, level).start()

    for copy in field[1 : GX - 1] + coefficients:
        copy.wait()

    def step(x, unused):
        first[x] = stencil(ext[x + 1], ext[x], ext[x + 2], diff_s[x], wind_s[x])
        return unused

    lax.fori_loop(1, GX - 1, step, 0)
    at_edges(me, [up_copy], [down_copy], "wait")

    @pl.when(me == 0)
    def _():
        ext[0] = jnp.zeros((ROWS, GY), F32)

    @pl.when(me == N_XY - 1)
    def _():
        ext[GX + 1] = jnp.zeros((ROWS, GY), F32)

    lax.fori_loop(0, 2, lambda i, u: step(i * (GX - 1), u), 0)

    for k in range(1, N_LEV):
        link_copy(k, lax.rem(level + N_LEV - k, N_LEV)).wait()
    carry_factors(level, links, factors)

    def finish(k, unused):
        for copy in copies(lax.rem(me + k, N_XY), me):
            copy.wait_send()
        for copy in copies(me, lax.rem(me + k, N_XY)):
            copy.wait_recv()
        return unused

    lax.fori_loop(1, N_XY, finish, 0)


def deposit_kernel(
    got_mass, got_code, order, total,
    rows_u, hl_u, col_u, hp_s, lp_s, hl_s, col_s, starts_v, starts_s, sem,
):
    code = got_code[...].astype(I32)
    hl = code // 256
    col = code % 256
    valid = hl > 0
    key = jnp.where(valid, (hl - 1) // 16, -1).astype(F32)
    hl_s[...] = hl.astype(F32)
    col_s[...] = col.astype(F32)
    position, base = ranks(key, BUCKETS, order[...])
    place = position.astype(I32)
    hp_s[...] = jnp.where(valid, place // BLK, -1).astype(F32)
    lp_s[...] = (place % BLK).astype(F32)
    lane = lax.broadcasted_iota(I32, (1, 128), 1)
    longest = jnp.zeros((1, 128), I32)
    before = None
    for k in range(BUCKETS + 1):
        start = jnp.zeros((1, 128), F32)
        for g in range(SETS):
            at = N_XY * k + SRC * g
            start = jnp.where(lane == g, base[at : at + 1, :], start)
        start = start.astype(I32)
        starts_v[k : k + 1, :] = start
        if k:
            longest = jnp.maximum(longest, start - before // 128 * 128)
        before = start
    starts_v[BUCKETS + 1 : BUCKETS + 2, :] = longest
    to_scalars = pltpu.make_async_copy(starts_v, starts_s, sem)
    to_scalars.start()

    def one_set(g, unused):
        take = lambda ref: lanes([ref[pl.ds(g * SRC + i, 1), :] for i in range(SRC)])
        values = lanes([two_parts(got_mass[g * SRC + i]) for i in range(SRC)])
        table = sort_slots(values, take(hl_s), take(col_s), take(hp_s), one_hot(take(lp_s)), 0, SRC)
        for half in range(2):
            side = slice(128 * half, 128 * half + 128)
            for d in range(SRC):
                rows_u[g, 2 * d + half] = table[16 * d : 16 * d + 16, side]
            hl_u[g, pl.ds(half, SRC, stride=2), :] = table[16 * SRC : 17 * SRC, side]
            col_u[g, pl.ds(half, SRC, stride=2), :] = table[17 * SRC : 18 * SRC, side]
        rows_u[g, UNITS:] = jnp.zeros((WIN, 16, 128), F32)
        hl_u[g, UNITS:, :] = jnp.zeros((8, 128), F32)
        col_u[g, UNITS:, :] = jnp.zeros((8, 128), F32)
        return unused

    lax.fori_loop(0, SETS, one_set, 0)
    to_scalars.wait()

    def place_of(k):
        return k // 2, pl.ds(pl.multiple_of((k % 2) * 16, 16), 16)

    def window(k, t):
        first_code = (k * 16 + 1).astype(F32)
        at = [jnp.minimum(starts_s[k, g] // 128 + WIN * t, UNITS) for g in range(SETS)]
        units = [(g, at[g] + i) for g in range(SETS) for i in range(WIN)]
        hl_row = lanes([hl_u[g, pl.ds(u, 1), :] for g, u in units])
        col_row = lanes([col_u[g, pl.ds(u, 1), :] for g, u in units])
        rows = lanes([rows_u[g, u] for g, u in units])
        width = 128 * WIN * SETS
        mine = jnp.broadcast_to(hl_row, (16, width)) == iota((16, width), 0) + first_code
        spread = [jnp.where(mine, jnp.broadcast_to(rows[q : q + 1, :], (16, width)), 0.0) for q in range(16)]
        spread.insert(8, jnp.where(mine, 1.0, 0.0))
        weighted = jnp.concatenate(spread, axis=0).astype(BF16)
        table = lax.dot_general(weighted, one_hot(col_row), NT, preferred_element_type=F32)
        table = table.reshape(17, 16, GY)
        return jnp.concatenate([table[:8] + table[9:], table[8:9]], axis=0)

    def one_bucket(k, unused):
        x, levels = place_of(k)
        total[x, :, levels, :] = window(k, 0)
        return unused

    lax.fori_loop(0, BUCKETS, one_bucket, 0, unroll=16)

    def rest(k, unused):
        x, levels = place_of(k)
        rounds = jnp.int32(1)
        for g in range(SETS):
            span = starts_s[k + 1, g] - starts_s[k, g] // 128 * 128
            rounds = jnp.maximum(rounds, (span + 128 * WIN - 1) // (128 * WIN))

        def again(t, unused):
            total[x, :, levels, :] += window(k, t)
            return unused

        lax.fori_loop(1, rounds, again, 0)
        return unused

    most = starts_s[BUCKETS + 1, 0]
    for g in range(1, SETS):
        most = jnp.maximum(most, starts_s[BUCKETS + 1, g])

    @pl.when(most > 128 * WIN)
    def _():
        lax.fori_loop(0, BUCKETS, rest, 0)


def correction(values, down, upward, p_col, e_col):
    shape = (BINS, LEV, GY)
    p_wide = lanes([p_col[...], p_col[...]]).reshape(shape)
    e_wide = lanes([e_col[...], e_col[...]]).reshape(shape)
    result = values.reshape(shape) + p_wide * down[:, None, :] + e_wide * upward[:, None, :]
    return result.reshape(ROWS, GY)


PARTS = ((0, 2), (2, 3), (5, 3))


def solve_kernel(
    total, first, diffusivity, wind, triple, p_col, e_col, factors,
    second, down_out, up_out,
    ext, fixed, diff_s, wind_s, edge, seen, seen_halo, edge2, seen2,
    load_sem, lev_send, lev_recv, diag_send, diag_recv, halo_send, halo_recv,
):
    me, level = lax.axis_index("xy"), lax.axis_index("lev")
    above, below = lax.rem(me + 1, N_XY), lax.rem(me + N_XY - 1, N_XY)
    barrier = pltpu.get_barrier_semaphore()

    def greet(where, least):
        for k in range(least, N_LEV):
            device = {"xy": where, "lev": lax.rem(level + k, N_LEV)}
            pl.semaphore_signal(barrier, inc=1, device_id=device, device_id_type=MESH)

    greet(me, 1)
    pl.when(me < N_XY - 1)(lambda: greet(above, 0))
    pl.when(me > 0)(lambda: greet(below, 0))
    sides = jnp.where(me < N_XY - 1, 1, 0) + jnp.where(me > 0, 1, 0)
    loads = plane_copies(diffusivity, diff_s, load_sem.at[0]) + plane_copies(wind, wind_s, load_sem.at[1])
    for copy in loads:
        copy.start()
    def product(values):
        high = values.astype(BF16)
        low = (values - high.astype(F32)).astype(BF16)
        return jnp.dot(triple[...], jnp.concatenate([high, low, high], axis=0), preferred_element_type=F32)

    def both(i):
        return lanes([factors[i], factors[i]])

    def edges(values, target, place):
        blocks = values.reshape(BINS, LEV, GY)
        last, start = blocks[:, LEV - 1, :], blocks[:, 0, :]
        target[0, place] = last
        target[1, place] = start + both(10) * last

    def carries(values, seen_at):
        down = jnp.zeros((BINS, GY), F32)
        upward = jnp.zeros((BINS, GY), F32)
        for f in range(N_LEV):
            here = jnp.where(level == f, 0.0, seen_at(f))
            down += both(f) * here
            upward += both(N_LEV + f) * here
        tail = values.reshape(BINS, LEV, GY)[:, LEV - 1, :]
        return down, upward + both(8) * tail + both(9) * down

    def peer_of(k):
        return lax.rem(level + k, N_LEV)

    def back(k):
        return lax.rem(level + N_LEV - k, N_LEV)

    def kind(k):
        return jnp.where(peer_of(k) > level, 0, 1)

    def lev_copies(turn, part, own):
        source, target = ((edge, seen), (edge2, seen2))[turn]
        span = pl.ds(*PARTS[part])
        return [
            remote(
                source.at[kind(k), span], target.at[level if own else back(k), span],
                lev_send.at[turn, part, k], lev_recv.at[turn, part, k], {"xy": me, "lev": peer_of(k)},
            )
            for k in range(1, N_LEV)
        ]

    def diag_copies(own):
        return [
            remote(
                edge.at[kind(k), 1 - side], seen_halo.at[side, level if own else back(k)],
                diag_send.at[side, k], diag_recv.at[side, k], {"xy": where, "lev": peer_of(k)},
            )
            for side, where in enumerate((above, below))
            for k in range(1, N_LEV)
        ]

    def start(copies):
        for copy in copies:
            copy.start()

    def wait(copies):
        for copy in copies:
            copy.wait()

    def solve_plane(x, place):
        counts = total[x, BINS]
        share = counts / (counts + 2.0)
        old = first[x].reshape(BINS, LEV, GY)
        blended = (1.0 - share)[None] * old + share[None] * total[x, 0:BINS]
        solved = product(blended.reshape(ROWS, GY))
        ext[x + 1] = solved
        edges(solved, edge, place)

    def some(function, begin, count, shift):
        def one(i, unused):
            function(i, i + shift)
            return unused

        lax.fori_loop(begin, begin + count, one, 0, unroll=count)

    solve_plane(0, 0)
    solve_plane(GX - 1, 1)
    pl.semaphore_wait(barrier, N_LEV - 1 + N_LEV * sides)
    halos = [
        remote(ext.at[GX], ext.at[0], halo_send.at[0], halo_recv.at[0], {"xy": above, "lev": level}),
        remote(ext.at[1], ext.at[GX + 1], halo_send.at[1], halo_recv.at[1], {"xy": below, "lev": level}),
    ]
    sent = diag_copies(True)
    seen_in = diag_copies(False)
    at_edges(me, sent[: N_LEV - 1], sent[N_LEV - 1 :], "start")
    start(lev_copies(0, 0, True))
    at_edges(me, halos[:1], halos[1:], "start")
    some(solve_plane, 1, 3, 1)
    start(lev_copies(0, 1, True))
    some(solve_plane, 4, 3, 1)
    start(lev_copies(0, 2, True))

    def correct_plane(x, place):
        down, upward = carries(ext[x + 1], lambda f: seen[f, place])
        fixed[x + 1] = correction(ext[x + 1], down, upward, p_col, e_col)

    def correct_halo(at, side):
        down, upward = carries(ext[at], lambda f: seen_halo[side, f])
        fixed[at] = correction(ext[at], down, upward, p_col, e_col)

    def second_plane(x, place):
        stepped = stencil(fixed[x + 1], fixed[x], fixed[x + 2], diff_s[x], wind_s[x])
        solved = product(stepped)
        second[x] = solved
        edges(solved, edge2, place)

    def last_plane(x, place):
        down, upward = carries(second[x], lambda f: seen2[f, place])
        second[x] = correction(second[x], down, upward, p_col, e_col)

    wait(loads)
    wait(lev_copies(0, 0, False) + lev_copies(0, 1, False))
    correct_plane(0, 0)
    correct_plane(GX - 1, 1)
    some(correct_plane, 1, 3, 1)
    some(second_plane, 1, 2, 1)
    wait(lev_copies(0, 2, False))
    some(correct_plane, 4, 3, 1)
    second_plane(3, 4)
    start(lev_copies(1, 1, True))
    some(second_plane, 4, 3, 1)
    start(lev_copies(1, 2, True))
    at_edges(me, seen_in[: N_LEV - 1] + halos[:1], seen_in[N_LEV - 1 :] + halos[1:], "wait")
    pl.when(me > 0)(lambda: correct_halo(0, 0))
    pl.when(me < N_XY - 1)(lambda: correct_halo(GX + 1, 1))

    @pl.when(me == 0)
    def _():
        fixed[0] = jnp.zeros((ROWS, GY), F32)

    @pl.when(me == N_XY - 1)
    def _():
        fixed[GX + 1] = jnp.zeros((ROWS, GY), F32)

    second_plane(0, 0)
    second_plane(GX - 1, 1)
    start(lev_copies(1, 0, True))
    for part in (1, 2):
        wait(lev_copies(1, part, False))
        some(last_plane, 3 * part - 2, 3, 1)
    wait(lev_copies(1, 0, False))
    for side in range(2):
        down, upward = carries(second[side * (GX - 1)], lambda f: seen2[f, side])
        down_out[side] = down
        up_out[side] = upward


def finish_kernel(second, down, upward, p_col, e_col, out, outer, sem):
    inner = [pltpu.make_async_copy(second.at[x], out.at[:, x, :], sem.at[x]) for x in range(1, GX - 1)]
    for copy in inner:
        copy.start()
    last = []
    for side in range(2):
        x = side * (GX - 1)
        outer[side] = correction(second[x], down[side], upward[side], p_col, e_col)
        last.append(pltpu.make_async_copy(outer.at[side], out.at[:, x, :], sem.at[x]))
        last[side].start()
    for copy in inner + last:
        copy.wait()


def vmem(*shape, dtype=F32):
    return pltpu.VMEM(shape, dtype)


def whole(count):
    return [pl.BlockSpec(memory_space=pltpu.VMEM)] * count


def somewhere(count):
    return [pl.BlockSpec(memory_space=pltpu.HBM)] * count


def shaped(*shape, dtype=F32):
    return jax.ShapeDtypeStruct(shape, dtype)


def shards(
    euler_field, parcel_mass, dest_device, dest_cell, diffusivity, wind_speed, inverses, lower_coupling, upper_coupling
):
    dma = pltpu.SemaphoreType.DMA
    euler, mass, dest, cell, diffusivity, wind, inv, low, up = [
        pltpu.with_memory_space_constraint(array, pltpu.HBM)
        for array in (
            euler_field.reshape(ROWS, GX, GY), parcel_mass, dest_device.reshape(32, 128), dest_cell.reshape(32, 128),
            diffusivity, wind_speed, inverses, lower_coupling, upper_coupling,
        )
    ]
    routed = pl.pallas_call(
        route_kernel,
        name="route",
        out_shape=[
            shaped(GX, ROWS, GY), shaped(N_XY, BINS, CAP), shaped(N_XY, CAP),
            shaped(N_XY * (BUCKETS + 1), N_XY * BUCKETS, dtype=BF16), shaped(ROWS, 3 * ROWS, dtype=BF16),
            shaped(ROWS, 128), shaped(ROWS, 128), shaped(11, BINS, 128),
        ],
        in_specs=somewhere(9),
        out_specs=whole(8),
        scratch_shapes=[
            vmem(GX + 2, ROWS, GY), vmem(GX, LEV, GY), vmem(GX, LEV, GY),
            vmem(BINS, PARC), vmem(32, 128, dtype=I32), vmem(32, 128, dtype=I32),
            vmem(2, BINS, 16, 16), vmem(2, BINS), vmem(2, BINS),
            vmem(N_XY, BINS, CAP), vmem(N_XY, CAP), vmem(CAP, PARC, dtype=BF16), vmem(N_LEV, 3, BINS, 128),
            dma((3, GX)), dma((6,)), dma((2,)), dma((2,)), dma((N_XY,)), dma((N_XY,)), dma((N_XY,)), dma((N_XY,)),
            dma((N_LEV,)), dma((N_LEV,)),
        ],
        compiler_params=pltpu.CompilerParams(collective_id=0, has_side_effects=True, vmem_limit_bytes=LIMIT),
    )(euler, mass, dest, cell, diffusivity, wind, inv, low, up)
    first, got_mass, got_code, order, triple, p_col, e_col, factors = routed
    total = pl.pallas_call(
        deposit_kernel,
        name="deposit",
        out_shape=shaped(GX, BINS + 1, LEV, GY),
        in_specs=whole(3),
        out_specs=pl.BlockSpec(memory_space=pltpu.VMEM),
        scratch_shapes=[
            vmem(SETS, UNITS + WIN, 16, 128), vmem(SETS, UNITS + 8, 128), vmem(SETS, UNITS + 8, 128),
            vmem(N_XY, BLK), vmem(N_XY, BLK), vmem(N_XY, BLK), vmem(N_XY, BLK),
            vmem(BUCKETS + 8, 128, dtype=I32), pltpu.SMEM((BUCKETS + 8, 128), I32), dma,
        ],
        compiler_params=pltpu.CompilerParams(vmem_limit_bytes=LIMIT),
    )(got_mass, got_code, order)
    second, down, upward = pl.pallas_call(
        solve_kernel,
        name="solve",
        out_shape=[shaped(GX, ROWS, GY), shaped(2, BINS, GY), shaped(2, BINS, GY)],
        in_specs=whole(2) + somewhere(2) + whole(4),
        out_specs=whole(3),
        scratch_shapes=[
            vmem(GX + 2, ROWS, GY), vmem(GX + 2, ROWS, GY),
            vmem(GX, LEV, GY), vmem(GX, LEV, GY),
            vmem(2, GX, BINS, GY), vmem(N_LEV, GX, BINS, GY), vmem(2, N_LEV, BINS, GY),
            vmem(2, GX, BINS, GY), vmem(N_LEV, GX, BINS, GY),
            dma((2, GX)), dma((2, 3, N_LEV)), dma((2, 3, N_LEV)), dma((2, N_LEV)), dma((2, N_LEV)), dma((2,)), dma((2,)),
        ],
        compiler_params=pltpu.CompilerParams(collective_id=1, has_side_effects=True, vmem_limit_bytes=LIMIT),
    )(total, first, diffusivity, wind, triple, p_col, e_col, factors)
    result = pl.pallas_call(
        finish_kernel,
        name="finish",
        out_shape=shaped(ROWS, GX, GY),
        in_specs=whole(5),
        out_specs=pl.BlockSpec(memory_space=pltpu.HBM),
        scratch_shapes=[vmem(2, ROWS, GY), dma((GX,))],
        compiler_params=pltpu.CompilerParams(vmem_limit_bytes=LIMIT),
    )(second, down, upward, p_col, e_col)
    return result.reshape(BINS, LEV, GX, GY)


def solution(mesh):
    placed = (
        P(None, "lev", "xy", None),
        P(None, ("xy", "lev")),
        P(("xy", "lev"), None),
        P(("xy", "lev")),
        P("lev", "xy", None),
        P("lev", "xy", None),
        P("lev", None, None, None),
        P("lev", None),
        P("lev", None),
    )
    return jax.shard_map(
        shards, mesh=mesh, in_specs=placed, out_specs=P(None, "lev", "xy", None), check_vma=False
    )
```

```python
import functools

import jax
import jax.numpy as jnp
from jax import lax
from jax.experimental import pallas as pl
from jax.experimental.pallas import tpu as pltpu
from jax.sharding import PartitionSpec as P

F32, BF16, I32 = jnp.float32, jnp.bfloat16, jnp.int32
MESH = pl.DeviceIdType.MESH
N_XY, N_LEV, BINS, LEV, GX, GY = 32, 4, 8, 32, 8, 256
ROWS = BINS * LEV
PARC, CAP, BLK = 4096, 256, 256
BUCKETS = 16
NT = (((1,), (1,)), ((), ()))
LIMIT = 24 << 20
SETS = 2
SRC = N_XY // SETS
SPAN = SRC * CAP
UNITS = SPAN // 128
WIN = 4


def iota(shape, dim, dtype=F32):
    return lax.broadcasted_iota(I32, shape, dim).astype(dtype)


def ranks(keys, count, lower):
    n = keys.shape[0]
    masks = [jnp.where(keys == k, 1.0, 0.0) for k in range(count)]
    stack = jnp.concatenate(masks, axis=0).astype(BF16)
    before = (iota((BLK, BLK), 0) < iota((BLK, BLK), 1)).astype(BF16)
    inside = jnp.dot(stack, before, preferred_element_type=F32)
    totals = jnp.dot(stack, jnp.ones((BLK, 128), BF16), preferred_element_type=F32)
    base = jnp.dot(lower, totals.astype(BF16), preferred_element_type=F32)
    wide = jnp.concatenate([base, base], axis=1)
    whole = inside + wide[: inside.shape[0]]
    position = jnp.zeros(keys.shape, F32)
    for k in range(count):
        position += masks[k] * whole[k * n : (k + 1) * n]
    return position, base


def lanes(pieces):
    return jnp.concatenate(pieces, axis=1)


def one_hot(row):
    width = row.shape[1]
    wide = jnp.broadcast_to(row, (BLK, width)).astype(BF16)
    ids = iota((BLK, width), 0, BF16)
    return jnp.where(ids == wide, jnp.ones((BLK, width), BF16), jnp.zeros((BLK, width), BF16))


def sort_slots(values16, high_low, column, target, spot, first, count):
    width = target.shape[1]
    chosen = jnp.broadcast_to(target, (16, width)).astype(BF16)
    zero = jnp.zeros((16, width), BF16)
    parts = [jnp.where(chosen == jnp.array(first + d, BF16), values16, zero) for d in range(count)]
    mine = iota((count, width), 0) + float(first) == target
    codes = jnp.concatenate([jnp.where(mine, high_low, 0.0), jnp.where(mine, column, 0.0)], axis=0)
    weighted = jnp.concatenate(parts + [codes.astype(BF16)], axis=0)
    return lax.dot_general(weighted, spot, NT, preferred_element_type=F32)


def two_parts(values):
    high = values.astype(BF16).astype(F32)
    return jnp.concatenate([high, values - high], axis=0).astype(BF16)


def stencil(centre, before, after, diffusivity, wind):
    shape = (BINS, LEV, GY)
    lane = lax.broadcasted_iota(I32, (ROWS, GY), 1)
    left = jnp.where(lane == 0, 0.0, pltpu.roll(centre, 1, 1))
    right = jnp.where(lane == GY - 1, 0.0, pltpu.roll(centre, GY - 1, 1))
    laplace = (after + before + right + left - 4.0 * centre).reshape(shape)
    drift = (centre - before).reshape(shape)
    result = centre.reshape(shape) + diffusivity[None] * laplace - wind[None] * drift
    return result.reshape(ROWS, GY)


def at_edges(me, upward, downward, action):
    @pl.when(me < N_XY - 1)
    def _():
        for copy in upward:
            copy.start() if action == "start" else copy.wait_send()
        for copy in downward if action == "wait" else []:
            copy.wait_recv()

    @pl.when(me > 0)
    def _():
        for copy in downward:
            copy.start() if action == "start" else copy.wait_send()
        for copy in upward if action == "wait" else []:
            copy.wait_recv()


def plane_copies(source, target, sems, at=0):
    return [pltpu.make_async_copy(source.at[:, x, :], target.at[at + x], sems.at[x]) for x in range(GX)]


def remote(src, dst, send, recv, device):
    return pltpu.make_async_remote_copy(
        src_ref=src, dst_ref=dst, send_sem=send, recv_sem=recv, device_id=device, device_id_type=MESH
    )


def compose(inv, low, up, triple, p_ref, e_ref):
    lane16 = lax.broadcasted_iota(I32, (16, ROWS), 1) % LEV
    row16 = lax.broadcasted_iota(I32, (16, ROWS), 0)
    own = lax.broadcasted_iota(I32, (BINS, 16, ROWS), 0) == (
        lax.broadcasted_iota(I32, (BINS, 16, ROWS), 2) // LEV
    )

    def spread(group):
        place = (lane16 == row16 + 16 * group).astype(F32)
        flat = inv[group].reshape(BINS * 16, 16)
        full = jnp.dot(flat, place, precision=lax.Precision.HIGHEST, preferred_element_type=F32)
        return jnp.where(own, full.reshape(BINS, 16, ROWS), 0.0)

    def per_bin(ref, group):
        wide = jnp.broadcast_to(ref[group : group + 1, :].reshape(1, 1, BINS), (BINS, 1, BINS))
        same = lax.broadcasted_iota(I32, (BINS, 1, BINS), 0) == lax.broadcasted_iota(
            I32, (BINS, 1, BINS), 2
        )
        return jnp.sum(jnp.where(same, wide, 0.0), axis=2, keepdims=True)

    t0, t1 = spread(0), spread(1)
    l0, l1, u0, u1 = per_bin(low, 0), per_bin(low, 1), per_bin(up, 0), per_bin(up, 1)
    m0, m1 = inv[0], inv[1]
    m0_first, m0_last = m0[:, :, 0:1], m0[:, :, 15:16]
    m1_first, m1_last = m1[:, :, 0:1], m1[:, :, 15:16]
    tail0 = t0[:, 15:16, :]
    link = (l1 * m1[:, 0:1, 0:1]) * tail0 + t1[:, 0:1, :]
    p0 = t0 + (u0 * m0_last) * link
    p1 = t1 + (l1 * m1_first) * tail0
    full = jnp.concatenate([p0, p1], axis=1).reshape(ROWS, ROWS)
    high = full.astype(BF16)
    triple[:, 0:ROWS] = high
    triple[:, ROWS : 2 * ROWS] = high
    triple[:, 2 * ROWS :] = (full - high.astype(F32)).astype(BF16)
    passed = l1 * l0 * m0[:, 15:16, 0:1]
    c0 = l0 * m0_first + (u0 * m0_last) * (passed * m1[:, 0:1, 0:1])
    c1 = passed * m1_first
    d0 = (u0 * u1 * m1[:, 0:1, 15:16]) * m0_last
    d1 = u1 * m1_last
    p_ref[...] = jnp.broadcast_to(jnp.concatenate([c0, c1], axis=1), (BINS, LEV, 128)).reshape(ROWS, 128)
    e_ref[...] = jnp.broadcast_to(jnp.concatenate([d0, d1], axis=1), (BINS, LEV, 128)).reshape(ROWS, 128)


def carry_factors(level, all_ref, out_ref):
    alpha = [all_ref[f, 0] for f in range(N_LEV)]
    beta = [all_ref[f, 1] for f in range(N_LEV)]
    gamma = [all_ref[f, 2] for f in range(N_LEV)]
    zero, one = jnp.zeros((BINS, 128), F32), jnp.ones((BINS, 128), F32)
    for f in range(N_LEV):
        down, product = zero, one
        for i in range(f + 1, N_LEV):
            down = jnp.where(level == i, product, down)
            product = product * alpha[i]
        upward, product = zero, one
        for i in range(f - 1, -1, -1):
            upward = jnp.where(level == i, product, upward)
            product = product * beta[i]
        out_ref[f] = down
        out_ref[N_LEV + f] = upward
    sigma = [zero] * N_LEV
    for f in range(N_LEV - 1, 0, -1):
        sigma[f - 1] = gamma[f] + beta[f] * alpha[f] * sigma[f]

    def own(values):
        result = values[0]
        for f in range(1, N_LEV):
            result = jnp.where(level == f, values[f], result)
        return result

    out_ref[8] = own(sigma)
    out_ref[9] = own([sigma[f] * alpha[f] for f in range(N_LEV)])
    out_ref[10] = own([sigma[f] * beta[f] for f in range(N_LEV)])


def route_kernel(
    euler, mass, dest, cell, diffusivity, wind, inv, low, up,
    first, got_mass, got_code, order, triple, p_col, e_col, factors,
    ext, diff_s, wind_s, mass_s, dest_in, cell_in, inv_s, low_s, up_s,
    send_mass, send_code, spot_s, links,
    load_sem, small_sem, halo_send, halo_recv, mass_send, mass_recv, code_send, code_recv, link_send, link_recv,
):
    me, level = lax.axis_index("xy"), lax.axis_index("lev")
    barrier = pltpu.get_barrier_semaphore()

    def greet(k, unused):
        pl.semaphore_signal(
            barrier, inc=1, device_id={"xy": lax.rem(me + k, N_XY), "lev": level}, device_id_type=MESH
        )
        return unused

    lax.fori_loop(1, N_XY, greet, 0)
    for k in range(1, N_LEV):
        pl.semaphore_signal(
            barrier, inc=1, device_id={"xy": me, "lev": lax.rem(level + k, N_LEV)}, device_id_type=MESH
        )

    small = [
        pltpu.make_async_copy(source, target, small_sem.at[i])
        for i, (source, target) in enumerate(
            [(dest, dest_in), (cell, cell_in), (mass, mass_s), (inv, inv_s), (low, low_s), (up, up_s)]
        )
    ]
    field = plane_copies(euler, ext, load_sem.at[0], 1)
    coefficients = plane_copies(diffusivity, diff_s, load_sem.at[1]) + plane_copies(wind, wind_s, load_sem.at[2])
    for copy in small[:3]:
        copy.start()

    above, below = lax.rem(me + 1, N_XY), lax.rem(me + N_XY - 1, N_XY)
    up_copy = remote(euler.at[:, GX - 1, :], ext.at[0], halo_send.at[0], halo_recv.at[0], {"xy": above, "lev": level})
    down_copy = remote(euler.at[:, 0, :], ext.at[GX + 1], halo_send.at[1], halo_recv.at[1], {"xy": below, "lev": level})
    pl.semaphore_wait(barrier, N_XY - 1 + N_LEV - 1)
    at_edges(me, [up_copy], [down_copy], "start")

    def wide(ref):
        return lanes([ref[pl.ds(0, 16, stride=2), :], ref[pl.ds(1, 16, stride=2), :]])

    def flat(rows):
        return lanes([rows[i : i + 1] for i in range(16)])

    for copy in small[:3]:
        copy.wait()
    target = wide(dest_in).astype(F32)
    cells = wide(cell_in)
    levels = cells // (GX * GY)
    bucket = (cells // GY) % GX * 2 + levels // 16
    high_low = flat((bucket * 16 + levels % 16 + 1).astype(F32))
    column = flat((cells % GY).astype(F32))
    r, c = (lax.broadcasted_iota(I32, (512, 512), d) for d in (0, 1))
    lower = jnp.where((c < r) & (c // 16 == r // 16), 1.0, 0.0).astype(BF16)
    slot, unused_base = ranks(target, N_XY, lower)
    for copy in small[3:] + field + coefficients:
        copy.start()
    spot_s[...] = one_hot(flat(slot))
    values = two_parts(mass_s[...])
    flat_target = flat(target)

    def copies(other, slot_id):
        device = {"xy": other, "lev": level}
        return (
            remote(send_mass.at[other], got_mass.at[slot_id], mass_send.at[other], mass_recv.at[slot_id], device),
            remote(
                send_code.at[pl.ds(other, 1)], got_code.at[pl.ds(slot_id, 1)],
                code_send.at[other], code_recv.at[slot_id], device,
            ),
        )

    half = N_XY // 2
    for begin in (0, half):
        table = sort_slots(values, high_low, column, flat_target, spot_s[...], begin, half)
        masses = table[: 16 * half].reshape(half, 16, CAP)
        send_mass[begin : begin + half] = masses[:, :8] + masses[:, 8:]
        send_code[begin : begin + half] = table[16 * half : 17 * half] * 256.0 + table[17 * half :]

        def send(k, unused):
            other = begin + lax.rem(me + k, half)

            @pl.when(other != me)
            def _():
                for copy in copies(other, me):
                    copy.start()

            return unused

        lax.fori_loop(0, half, send, 0)
    got_mass[me] = send_mass[me]
    got_code[pl.ds(me, 1), :] = send_code[pl.ds(me, 1), :]

    for copy in small[3:]:
        copy.wait()
    compose(inv_s, low_s, up_s, triple, p_col, e_col)
    r, c = (lax.broadcasted_iota(I32, (N_XY * (BUCKETS + 1), N_XY * BUCKETS), d) for d in (0, 1))
    order[...] = jnp.where((c < r) & (c % N_XY // SRC == r % N_XY // SRC), 1.0, 0.0).astype(BF16)
    links[level, 0] = p_col[pl.ds(LEV - 1, BINS, stride=LEV), :]
    links[level, 1] = e_col[pl.ds(0, BINS, stride=LEV), :]
    links[level, 2] = p_col[pl.ds(0, BINS, stride=LEV), :]

    def link_copy(k, owner):
        peer = lax.rem(level + k, N_LEV)
        return remote(
            links.at[owner], links.at[owner], link_send.at[k], link_recv.at[k], {"xy": me, "lev": peer}
        )

    for k in range(1, N_LEV):
        link_copy(k, level).start()

    for copy in field + coefficients:
        copy.wait()

    def step(x, unused):
        first[x] = stencil(ext[x + 1], ext[x], ext[x + 2], diff_s[x], wind_s[x])
        return unused

    lax.fori_loop(1, GX - 1, step, 0)
    at_edges(me, [up_copy], [down_copy], "wait")

    @pl.when(me == 0)
    def _():
        ext[0] = jnp.zeros((ROWS, GY), F32)

    @pl.when(me == N_XY - 1)
    def _():
        ext[GX + 1] = jnp.zeros((ROWS, GY), F32)

    lax.fori_loop(0, 2, lambda i, u: step(i * (GX - 1), u), 0)

    for k in range(1, N_LEV):
        link_copy(k, lax.rem(level + N_LEV - k, N_LEV)).wait()
    carry_factors(level, links, factors)

    def finish(k, unused):
        for copy in copies(lax.rem(me + k, N_XY), me):
            copy.wait_send()
        for copy in copies(me, lax.rem(me + k, N_XY)):
            copy.wait_recv()
        return unused

    lax.fori_loop(1, N_XY, finish, 0)


def deposit_kernel(
    got_mass, got_code, order, total,
    rows_u, hl_u, col_u, hp_s, lp_s, hl_s, col_s, starts_v, starts_s, sem,
):
    code = got_code[...].astype(I32)
    hl = code // 256
    col = code % 256
    valid = hl > 0
    key = jnp.where(valid, (hl - 1) // 16, -1).astype(F32)
    hl_s[...] = hl.astype(F32)
    col_s[...] = col.astype(F32)
    position, base = ranks(key, BUCKETS, order[...])
    place = position.astype(I32)
    hp_s[...] = jnp.where(valid, place // BLK, -1).astype(F32)
    lp_s[...] = (place % BLK).astype(F32)
    lane = lax.broadcasted_iota(I32, (1, 128), 1)
    longest = jnp.zeros((1, 128), I32)
    before = None
    for k in range(BUCKETS + 1):
        start = jnp.zeros((1, 128), F32)
        for g in range(SETS):
            at = N_XY * k + SRC * g
            start = jnp.where(lane == g, base[at : at + 1, :], start)
        start = start.astype(I32)
        starts_v[k : k + 1, :] = start
        if k:
            longest = jnp.maximum(longest, start - before // 128 * 128)
        before = start
    starts_v[BUCKETS + 1 : BUCKETS + 2, :] = longest
    to_scalars = pltpu.make_async_copy(starts_v, starts_s, sem)
    to_scalars.start()

    def one_set(g, unused):
        take = lambda ref: lanes([ref[pl.ds(g * SRC + i, 1), :] for i in range(SRC)])
        values = lanes([two_parts(got_mass[g * SRC + i]) for i in range(SRC)])
        table = sort_slots(values, take(hl_s), take(col_s), take(hp_s), one_hot(take(lp_s)), 0, SRC)
        for half in range(2):
            side = slice(128 * half, 128 * half + 128)
            for d in range(SRC):
                rows_u[g, 2 * d + half] = table[16 * d : 16 * d + 16, side]
            hl_u[g, pl.ds(half, SRC, stride=2), :] = table[16 * SRC : 17 * SRC, side]
            col_u[g, pl.ds(half, SRC, stride=2), :] = table[17 * SRC : 18 * SRC, side]
        rows_u[g, UNITS:] = jnp.zeros((WIN, 16, 128), F32)
        hl_u[g, UNITS:, :] = jnp.zeros((8, 128), F32)
        col_u[g, UNITS:, :] = jnp.zeros((8, 128), F32)
        return unused

    lax.fori_loop(0, SETS, one_set, 0)
    to_scalars.wait()

    def place_of(k):
        return k // 2, pl.ds(pl.multiple_of((k % 2) * 16, 16), 16)

    def window(k, t):
        first_code = (k * 16 + 1).astype(F32)
        at = [jnp.minimum(starts_s[k, g] // 128 + WIN * t, UNITS) for g in range(SETS)]
        units = [(g, at[g] + i) for g in range(SETS) for i in range(WIN)]
        hl_row = lanes([hl_u[g, pl.ds(u, 1), :] for g, u in units])
        col_row = lanes([col_u[g, pl.ds(u, 1), :] for g, u in units])
        rows = lanes([rows_u[g, u] for g, u in units])
        width = 128 * WIN * SETS
        mine = jnp.broadcast_to(hl_row, (16, width)) == iota((16, width), 0) + first_code
        spread = [jnp.where(mine, jnp.broadcast_to(rows[q : q + 1, :], (16, width)), 0.0) for q in range(16)]
        spread.insert(8, jnp.where(mine, 1.0, 0.0))
        weighted = jnp.concatenate(spread, axis=0).astype(BF16)
        table = lax.dot_general(weighted, one_hot(col_row), NT, preferred_element_type=F32)
        table = table.reshape(17, 16, GY)
        return jnp.concatenate([table[:8] + table[9:], table[8:9]], axis=0)

    def one_bucket(k, unused):
        x, levels = place_of(k)
        total[x, :, levels, :] = window(k, 0)
        return unused

    lax.fori_loop(0, BUCKETS, one_bucket, 0, unroll=16)

    def rest(k, unused):
        x, levels = place_of(k)
        rounds = jnp.int32(1)
        for g in range(SETS):
            span = starts_s[k + 1, g] - starts_s[k, g] // 128 * 128
            rounds = jnp.maximum(rounds, (span + 128 * WIN - 1) // (128 * WIN))

        def again(t, unused):
            total[x, :, levels, :] += window(k, t)
            return unused

        lax.fori_loop(1, rounds, again, 0)
        return unused

    most = starts_s[BUCKETS + 1, 0]
    for g in range(1, SETS):
        most = jnp.maximum(most, starts_s[BUCKETS + 1, g])

    @pl.when(most > 128 * WIN)
    def _():
        lax.fori_loop(0, BUCKETS, rest, 0)


def correction(values, down, upward, p_col, e_col):
    shape = (BINS, LEV, GY)
    p_wide = lanes([p_col[...], p_col[...]]).reshape(shape)
    e_wide = lanes([e_col[...], e_col[...]]).reshape(shape)
    result = values.reshape(shape) + p_wide * down[:, None, :] + e_wide * upward[:, None, :]
    return result.reshape(ROWS, GY)


PARTS = (((0, 2), (2, 3), (5, 3)), ((0, 3), (3, 3), (6, 2)))


def solve_kernel(
    total, first, diffusivity, wind, triple, p_col, e_col, factors,
    second, down_out, up_out,
    ext, fixed, diff_s, wind_s, sum_s, beside, edge, seen, seen_halo, edge2, seen2, edge3, seen_halo2,
    load_sem, lev_send, lev_recv, diag_send, diag_recv, halo_send, halo_recv, side_send, side_recv,
):
    me, level = lax.axis_index("xy"), lax.axis_index("lev")
    above, below = lax.rem(me + 1, N_XY), lax.rem(me + N_XY - 1, N_XY)
    barrier = pltpu.get_barrier_semaphore()

    def greet(where, least):
        for k in range(least, N_LEV):
            device = {"xy": where, "lev": lax.rem(level + k, N_LEV)}
            pl.semaphore_signal(barrier, inc=1, device_id=device, device_id_type=MESH)

    greet(me, 1)
    pl.when(me < N_XY - 1)(lambda: greet(above, 0))
    pl.when(me > 0)(lambda: greet(below, 0))
    sides = jnp.where(me < N_XY - 1, 1, 0) + jnp.where(me > 0, 1, 0)
    loads = plane_copies(diffusivity, diff_s, load_sem.at[0]) + plane_copies(wind, wind_s, load_sem.at[1])
    for copy in loads:
        copy.start()
    def product(values):
        high = values.astype(BF16)
        low = (values - high.astype(F32)).astype(BF16)
        return jnp.dot(triple[...], jnp.concatenate([high, low, high], axis=0), preferred_element_type=F32)

    def both(i):
        return lanes([factors[i], factors[i]])

    def edges(values, target, place):
        blocks = values.reshape(BINS, LEV, GY)
        last, start = blocks[:, LEV - 1, :], blocks[:, 0, :]
        target[0, place] = last
        target[1, place] = start + both(10) * last

    def carries(values, seen_at):
        down = jnp.zeros((BINS, GY), F32)
        upward = jnp.zeros((BINS, GY), F32)
        for f in range(N_LEV):
            here = jnp.where(level == f, 0.0, seen_at(f))
            down += both(f) * here
            upward += both(N_LEV + f) * here
        tail = values.reshape(BINS, LEV, GY)[:, LEV - 1, :]
        return down, upward + both(8) * tail + both(9) * down

    def peer_of(k):
        return lax.rem(level + k, N_LEV)

    def back(k):
        return lax.rem(level + N_LEV - k, N_LEV)

    def kind(k):
        return jnp.where(peer_of(k) > level, 0, 1)

    def lev_copies(turn, part, own):
        source, target = ((edge, seen), (edge2, seen2))[turn]
        span = pl.ds(*PARTS[turn][part])
        return [
            remote(
                source.at[kind(k), span], target.at[level if own else back(k), span],
                lev_send.at[turn, part, k], lev_recv.at[turn, part, k], {"xy": me, "lev": peer_of(k)},
            )
            for k in range(1, N_LEV)
        ]

    def diag_copies(turn, own):
        source, target = ((edge, seen_halo), (edge3, seen_halo2))[turn]
        return [
            remote(
                source.at[kind(k), 1 - side], target.at[side, level if own else back(k)],
                diag_send.at[turn, side, k], diag_recv.at[turn, side, k], {"xy": where, "lev": peer_of(k)},
            )
            for side, where in enumerate((above, below))
            for k in range(1, N_LEV)
        ]

    def start(copies):
        for copy in copies:
            copy.start()

    def wait(copies):
        for copy in copies:
            copy.wait()

    def solve_plane(x, place):
        counts = total[x, BINS]
        share = counts / (counts + 2.0)
        old = first[x].reshape(BINS, LEV, GY)
        blended = (1.0 - share)[None] * old + share[None] * total[x, 0:BINS]
        solved = product(blended.reshape(ROWS, GY))
        ext[x + 1] = solved
        edges(solved, edge, place)

    def some(function, begin, count, shift):
        def one(i, unused):
            function(i, i + shift)
            return unused

        lax.fori_loop(begin, begin + count, one, 0, unroll=count)

    solve_plane(0, 0)
    solve_plane(GX - 1, 1)
    wait(loads)
    sum_s[...] = diff_s[0] + wind_s[0]
    fixed[0] = jnp.zeros((ROWS, GY), F32)
    fixed[GX + 1] = jnp.zeros((ROWS, GY), F32)
    pl.semaphore_wait(barrier, N_LEV - 1 + N_LEV * sides)
    halos = [
        remote(ext.at[GX], ext.at[0], halo_send.at[0], halo_recv.at[0], {"xy": above, "lev": level}),
        remote(ext.at[1], ext.at[GX + 1], halo_send.at[1], halo_recv.at[1], {"xy": below, "lev": level}),
    ]
    weights = [
        remote(diff_s.at[GX - 1], beside.at[0], side_send.at[0], side_recv.at[0], {"xy": above, "lev": level}),
        remote(sum_s, beside.at[1], side_send.at[1], side_recv.at[1], {"xy": below, "lev": level}),
    ]
    sent, seen_in = diag_copies(0, True), diag_copies(0, False)
    sent2, seen_in2 = diag_copies(1, True), diag_copies(1, False)
    three = N_LEV - 1
    at_edges(me, sent[:three], sent[three:], "start")
    start(lev_copies(0, 0, True))
    at_edges(me, weights[:1], weights[1:], "start")
    at_edges(me, halos[:1], halos[1:], "start")
    some(solve_plane, 1, 3, 1)
    start(lev_copies(0, 1, True))
    some(solve_plane, 4, 3, 1)
    start(lev_copies(0, 2, True))

    def correct_plane(x, place):
        down, upward = carries(ext[x + 1], lambda f: seen[f, place])
        fixed[x + 1] = correction(ext[x + 1], down, upward, p_col, e_col)

    def scaled(plane, values):
        return (plane[None] * values.reshape(BINS, LEV, GY)).reshape(ROWS, GY)

    def second_plane(x, place):
        stepped = stencil(fixed[x + 1], fixed[x], fixed[x + 2], diff_s[x], wind_s[x])
        solved = product(stepped)
        second[x] = solved
        edges(solved, edge2, place)

    def share_up():
        edges(product(scaled(beside[1], fixed[GX])), edge3, 1)
        start(sent2[:three])

    def share_down():
        edges(product(scaled(beside[0], fixed[1])), edge3, 0)
        start(sent2[three:])

    wait(lev_copies(0, 0, False) + lev_copies(0, 1, False))
    correct_plane(0, 0)
    correct_plane(GX - 1, 1)
    at_edges(me, weights[:1], weights[1:], "wait")
    pl.when(me < N_XY - 1)(share_up)
    pl.when(me > 0)(share_down)
    some(correct_plane, 1, 3, 1)
    some(second_plane, 0, 3, 0)
    start(lev_copies(1, 0, True))
    wait(lev_copies(0, 2, False))
    some(correct_plane, 4, 3, 1)
    some(second_plane, 3, 3, 0)
    start(lev_copies(1, 1, True))
    some(second_plane, 6, 2, 0)
    start(lev_copies(1, 2, True))

    at_edges(me, seen_in[:three] + halos[:1], seen_in[three:] + halos[1:], "wait")

    def add_halo(at, side, x, plane):
        down, upward = carries(ext[at], lambda f: seen_halo[side, f])
        halo = correction(ext[at], down, upward, p_col, e_col)
        second[x] += product(scaled(plane, halo))

    pl.when(me > 0)(lambda: add_halo(0, 0, 0, sum_s[...]))
    pl.when(me < N_XY - 1)(lambda: add_halo(GX + 1, 1, GX - 1, diff_s[GX - 1]))
    at_edges(me, seen_in2[:three], seen_in2[three:], "wait")

    def no_share(side):
        seen_halo2[side] = jnp.zeros((N_LEV, BINS, GY), F32)

    pl.when(me == 0)(lambda: no_share(0))
    pl.when(me == N_XY - 1)(lambda: no_share(1))

    def seen_at(x):
        if x == 0:
            return lambda f: seen2[f, 0] + seen_halo2[0, f]
        if x == GX - 1:
            return lambda f: seen2[f, GX - 1] + seen_halo2[1, f]
        return lambda f: seen2[f, x]

    for part in range(2):
        wait(lev_copies(1, part, False))
        for x in range(3 * part, 3 * part + 3):
            down, upward = carries(second[x], seen_at(x))
            second[x] = correction(second[x], down, upward, p_col, e_col)
    wait(lev_copies(1, 2, False))
    for x in range(6, GX):
        down, upward = carries(second[x], seen_at(x))
        down_out[x - 6] = down
        up_out[x - 6] = upward


def finish_kernel(second, down, upward, p_col, e_col, out, outer, sem):
    inner = [pltpu.make_async_copy(second.at[x], out.at[:, x, :], sem.at[x]) for x in range(6)]
    for copy in inner:
        copy.start()
    last = []
    for i in range(2):
        x = 6 + i
        outer[i] = correction(second[x], down[i], upward[i], p_col, e_col)
        last.append(pltpu.make_async_copy(outer.at[i], out.at[:, x, :], sem.at[x]))
        last[i].start()
    for copy in inner + last:
        copy.wait()


def vmem(*shape, dtype=F32):
    return pltpu.VMEM(shape, dtype)


def whole(count):
    return [pl.BlockSpec(memory_space=pltpu.VMEM)] * count


def somewhere(count):
    return [pl.BlockSpec(memory_space=pltpu.HBM)] * count


def shaped(*shape, dtype=F32):
    return jax.ShapeDtypeStruct(shape, dtype)


def shards(
    euler_field, parcel_mass, dest_device, dest_cell, diffusivity, wind_speed, inverses, lower_coupling, upper_coupling
):
    dma = pltpu.SemaphoreType.DMA
    euler, mass, dest, cell, diffusivity, wind, inv, low, up = [
        pltpu.with_memory_space_constraint(array, pltpu.HBM)
        for array in (
            euler_field.reshape(ROWS, GX, GY), parcel_mass, dest_device.reshape(32, 128), dest_cell.reshape(32, 128),
            diffusivity, wind_speed, inverses, lower_coupling, upper_coupling,
        )
    ]
    routed = pl.pallas_call(
        route_kernel,
        name="route",
        out_shape=[
            shaped(GX, ROWS, GY), shaped(N_XY, BINS, CAP), shaped(N_XY, CAP),
            shaped(N_XY * (BUCKETS + 1), N_XY * BUCKETS, dtype=BF16), shaped(ROWS, 3 * ROWS, dtype=BF16),
            shaped(ROWS, 128), shaped(ROWS, 128), shaped(11, BINS, 128),
        ],
        in_specs=somewhere(9),
        out_specs=whole(8),
        scratch_shapes=[
            vmem(GX + 2, ROWS, GY), vmem(GX, LEV, GY), vmem(GX, LEV, GY),
            vmem(BINS, PARC), vmem(32, 128, dtype=I32), vmem(32, 128, dtype=I32),
            vmem(2, BINS, 16, 16), vmem(2, BINS), vmem(2, BINS),
            vmem(N_XY, BINS, CAP), vmem(N_XY, CAP), vmem(CAP, PARC, dtype=BF16), vmem(N_LEV, 3, BINS, 128),
            dma((3, GX)), dma((6,)), dma((2,)), dma((2,)), dma((N_XY,)), dma((N_XY,)), dma((N_XY,)), dma((N_XY,)),
            dma((N_LEV,)), dma((N_LEV,)),
        ],
        compiler_params=pltpu.CompilerParams(collective_id=0, has_side_effects=True, vmem_limit_bytes=LIMIT),
    )(euler, mass, dest, cell, diffusivity, wind, inv, low, up)
    first, got_mass, got_code, order, triple, p_col, e_col, factors = routed
    total = pl.pallas_call(
        deposit_kernel,
        name="deposit",
        out_shape=shaped(GX, BINS + 1, LEV, GY),
        in_specs=whole(3),
        out_specs=pl.BlockSpec(memory_space=pltpu.VMEM),
        scratch_shapes=[
            vmem(SETS, UNITS + WIN, 16, 128), vmem(SETS, UNITS + 8, 128), vmem(SETS, UNITS + 8, 128),
            vmem(N_XY, BLK), vmem(N_XY, BLK), vmem(N_XY, BLK), vmem(N_XY, BLK),
            vmem(BUCKETS + 8, 128, dtype=I32), pltpu.SMEM((BUCKETS + 8, 128), I32), dma,
        ],
        compiler_params=pltpu.CompilerParams(vmem_limit_bytes=LIMIT),
    )(got_mass, got_code, order)
    second, down, upward = pl.pallas_call(
        solve_kernel,
        name="solve",
        out_shape=[shaped(GX, ROWS, GY), shaped(2, BINS, GY), shaped(2, BINS, GY)],
        in_specs=whole(2) + somewhere(2) + whole(4),
        out_specs=whole(3),
        scratch_shapes=[
            vmem(GX + 2, ROWS, GY), vmem(GX + 2, ROWS, GY),
            vmem(GX, LEV, GY), vmem(GX, LEV, GY), vmem(LEV, GY), vmem(2, LEV, GY),
            vmem(2, GX, BINS, GY), vmem(N_LEV, GX, BINS, GY), vmem(2, N_LEV, BINS, GY),
            vmem(2, GX, BINS, GY), vmem(N_LEV, GX, BINS, GY), vmem(2, 2, BINS, GY), vmem(2, N_LEV, BINS, GY),
            dma((2, GX)), dma((2, 3, N_LEV)), dma((2, 3, N_LEV)), dma((2, 2, N_LEV)), dma((2, 2, N_LEV)),
            dma((2,)), dma((2,)), dma((2,)), dma((2,)),
        ],
        compiler_params=pltpu.CompilerParams(collective_id=1, has_side_effects=True, vmem_limit_bytes=LIMIT),
    )(total, first, diffusivity, wind, triple, p_col, e_col, factors)
    result = pl.pallas_call(
        finish_kernel,
        name="finish",
        out_shape=shaped(ROWS, GX, GY),
        in_specs=whole(5),
        out_specs=pl.BlockSpec(memory_space=pltpu.HBM),
        scratch_shapes=[vmem(2, ROWS, GY), dma((GX,))],
        compiler_params=pltpu.CompilerParams(vmem_limit_bytes=LIMIT),
    )(second, down, upward, p_col, e_col)
    return result.reshape(BINS, LEV, GX, GY)


def solution(mesh):
    placed = (
        P(None, "lev", "xy", None),
        P(None, ("xy", "lev")),
        P(("xy", "lev"), None),
        P(("xy", "lev")),
        P("lev", "xy", None),
        P("lev", "xy", None),
        P("lev", None, None, None),
        P("lev", None),
        P("lev", None),
    )
    return jax.shard_map(
        shards, mesh=mesh, in_specs=placed, out_specs=P(None, "lev", "xy", None), check_vma=False
    )
```

```python
import functools

import jax
import jax.numpy as jnp
from jax import lax
from jax.experimental import pallas as pl
from jax.experimental.pallas import tpu as pltpu
from jax.sharding import PartitionSpec as P

F32, BF16, I32 = jnp.float32, jnp.bfloat16, jnp.int32
MESH = pl.DeviceIdType.MESH
N_XY, N_LEV, BINS, LEV, GX, GY = 32, 4, 8, 32, 8, 256
ROWS = BINS * LEV
PARC, CAP, BLK = 4096, 256, 256
BUCKETS = 16
NT = (((1,), (1,)), ((), ()))
LIMIT = 24 << 20
SETS = 2
SRC = N_XY // SETS
SPAN = SRC * CAP
UNITS = SPAN // 128
WIN = 4


def iota(shape, dim, dtype=F32):
    return lax.broadcasted_iota(I32, shape, dim).astype(dtype)


def ranks(keys, count, lower):
    n = keys.shape[0]
    masks = [jnp.where(keys == k, 1.0, 0.0) for k in range(count)]
    stack = jnp.concatenate(masks, axis=0).astype(BF16)
    before = (iota((BLK, BLK), 0) < iota((BLK, BLK), 1)).astype(BF16)
    inside = jnp.dot(stack, before, preferred_element_type=F32)
    totals = jnp.dot(stack, jnp.ones((BLK, 128), BF16), preferred_element_type=F32)
    base = jnp.dot(lower, totals.astype(BF16), preferred_element_type=F32)
    wide = jnp.concatenate([base, base], axis=1)
    whole = inside + wide[: inside.shape[0]]
    position = jnp.zeros(keys.shape, F32)
    for k in range(count):
        position += masks[k] * whole[k * n : (k + 1) * n]
    return position, base


def lanes(pieces):
    return jnp.concatenate(pieces, axis=1)


def one_hot(row):
    width = row.shape[1]
    wide = jnp.broadcast_to(row, (BLK, width)).astype(BF16)
    ids = iota((BLK, width), 0, BF16)
    return jnp.where(ids == wide, jnp.ones((BLK, width), BF16), jnp.zeros((BLK, width), BF16))


def sort_slots(values16, high_low, column, target, spot, first, count):
    width = target.shape[1]
    chosen = jnp.broadcast_to(target, (16, width)).astype(BF16)
    zero = jnp.zeros((16, width), BF16)
    parts = [jnp.where(chosen == jnp.array(first + d, BF16), values16, zero) for d in range(count)]
    mine = iota((count, width), 0) + float(first) == target
    codes = jnp.concatenate([jnp.where(mine, high_low, 0.0), jnp.where(mine, column, 0.0)], axis=0)
    weighted = jnp.concatenate(parts + [codes.astype(BF16)], axis=0)
    return lax.dot_general(weighted, spot, NT, preferred_element_type=F32)


def two_parts(values):
    high = values.astype(BF16).astype(F32)
    return jnp.concatenate([high, values - high], axis=0).astype(BF16)


def stencil(centre, before, after, diffusivity, wind):
    shape = (BINS, LEV, GY)
    lane = lax.broadcasted_iota(I32, (ROWS, GY), 1)
    left = jnp.where(lane == 0, 0.0, pltpu.roll(centre, 1, 1))
    right = jnp.where(lane == GY - 1, 0.0, pltpu.roll(centre, GY - 1, 1))
    laplace = (after + before + right + left - 4.0 * centre).reshape(shape)
    drift = (centre - before).reshape(shape)
    result = centre.reshape(shape) + diffusivity[None] * laplace - wind[None] * drift
    return result.reshape(ROWS, GY)


def at_edges(me, upward, downward, action):
    @pl.when(me < N_XY - 1)
    def _():
        for copy in upward:
            copy.start() if action == "start" else copy.wait_send()
        for copy in downward if action == "wait" else []:
            copy.wait_recv()

    @pl.when(me > 0)
    def _():
        for copy in downward:
            copy.start() if action == "start" else copy.wait_send()
        for copy in upward if action == "wait" else []:
            copy.wait_recv()


def plane_copies(source, target, sems, at=0):
    return [pltpu.make_async_copy(source.at[:, x, :], target.at[at + x], sems.at[x]) for x in range(GX)]


def remote(src, dst, send, recv, device):
    return pltpu.make_async_remote_copy(
        src_ref=src, dst_ref=dst, send_sem=send, recv_sem=recv, device_id=device, device_id_type=MESH
    )


def compose(inv, low, up, triple, p_ref, e_ref):
    lane16 = lax.broadcasted_iota(I32, (16, ROWS), 1) % LEV
    row16 = lax.broadcasted_iota(I32, (16, ROWS), 0)
    own = lax.broadcasted_iota(I32, (BINS, 16, ROWS), 0) == (
        lax.broadcasted_iota(I32, (BINS, 16, ROWS), 2) // LEV
    )

    def spread(group):
        place = (lane16 == row16 + 16 * group).astype(F32)
        flat = inv[group].reshape(BINS * 16, 16)
        full = jnp.dot(flat, place, precision=lax.Precision.HIGHEST, preferred_element_type=F32)
        return jnp.where(own, full.reshape(BINS, 16, ROWS), 0.0)

    def per_bin(ref, group):
        wide = jnp.broadcast_to(ref[group : group + 1, :].reshape(1, 1, BINS), (BINS, 1, BINS))
        same = lax.broadcasted_iota(I32, (BINS, 1, BINS), 0) == lax.broadcasted_iota(
            I32, (BINS, 1, BINS), 2
        )
        return jnp.sum(jnp.where(same, wide, 0.0), axis=2, keepdims=True)

    t0, t1 = spread(0), spread(1)
    l0, l1, u0, u1 = per_bin(low, 0), per_bin(low, 1), per_bin(up, 0), per_bin(up, 1)
    m0, m1 = inv[0], inv[1]
    m0_first, m0_last = m0[:, :, 0:1], m0[:, :, 15:16]
    m1_first, m1_last = m1[:, :, 0:1], m1[:, :, 15:16]
    tail0 = t0[:, 15:16, :]
    link = (l1 * m1[:, 0:1, 0:1]) * tail0 + t1[:, 0:1, :]
    p0 = t0 + (u0 * m0_last) * link
    p1 = t1 + (l1 * m1_first) * tail0
    full = jnp.concatenate([p0, p1], axis=1).reshape(ROWS, ROWS)
    high = full.astype(BF16)
    triple[:, 0:ROWS] = high
    triple[:, ROWS : 2 * ROWS] = high
    triple[:, 2 * ROWS :] = (full - high.astype(F32)).astype(BF16)
    passed = l1 * l0 * m0[:, 15:16, 0:1]
    c0 = l0 * m0_first + (u0 * m0_last) * (passed * m1[:, 0:1, 0:1])
    c1 = passed * m1_first
    d0 = (u0 * u1 * m1[:, 0:1, 15:16]) * m0_last
    d1 = u1 * m1_last
    p_ref[...] = jnp.broadcast_to(jnp.concatenate([c0, c1], axis=1), (BINS, LEV, 128)).reshape(ROWS, 128)
    e_ref[...] = jnp.broadcast_to(jnp.concatenate([d0, d1], axis=1), (BINS, LEV, 128)).reshape(ROWS, 128)
    blocks = full.reshape(BINS, LEV, ROWS)
    eye = lax.broadcasted_iota(I32, (ROWS, ROWS), 0) == lax.broadcasted_iota(I32, (ROWS, ROWS), 1)
    across = [jnp.sum(jnp.where(eye, lanes([ref[...], ref[...]]), 0.0), axis=0, keepdims=True) for ref in (p_ref, e_ref)]
    rows = jnp.concatenate([blocks[:, at, :] * col for at in (LEV - 1, 0) for col in across], axis=0)
    fold = (
        lax.broadcasted_iota(I32, (ROWS, LEV), 0) % LEV == lax.broadcasted_iota(I32, (ROWS, LEV), 1)
    ).astype(F32)
    return jnp.dot(rows, fold, precision=lax.Precision.HIGHEST, preferred_element_type=F32)


def carry_factors(level, all_ref, out_ref):
    alpha = [all_ref[f, 0] for f in range(N_LEV)]
    beta = [all_ref[f, 1] for f in range(N_LEV)]
    gamma = [all_ref[f, 2] for f in range(N_LEV)]
    zero, one = jnp.zeros((BINS, 128), F32), jnp.ones((BINS, 128), F32)
    for f in range(N_LEV):
        down, product = zero, one
        for i in range(f + 1, N_LEV):
            down = jnp.where(level == i, product, down)
            product = product * alpha[i]
        upward, product = zero, one
        for i in range(f - 1, -1, -1):
            upward = jnp.where(level == i, product, upward)
            product = product * beta[i]
        out_ref[f] = down
        out_ref[N_LEV + f] = upward
    sigma = [zero] * N_LEV
    for f in range(N_LEV - 1, 0, -1):
        sigma[f - 1] = gamma[f] + beta[f] * alpha[f] * sigma[f]

    def own(values):
        result = values[0]
        for f in range(1, N_LEV):
            result = jnp.where(level == f, values[f], result)
        return result

    out_ref[8] = own(sigma)
    out_ref[9] = own([sigma[f] * alpha[f] for f in range(N_LEV)])
    out_ref[10] = own([sigma[f] * beta[f] for f in range(N_LEV)])


def route_kernel(
    euler, mass, dest, cell, diffusivity, wind, inv, low, up,
    first, got_mass, got_code, order, triple, p_col, e_col, factors, kept, turned,
    ext, diff_s, wind_s, mass_s, dest_in, cell_in, inv_s, low_s, up_s,
    send_mass, send_code, spare, spot_s, links,
    load_sem, small_sem, halo_send, halo_recv, mass_send, mass_recv, code_send, code_recv, link_send, link_recv,
):
    me, level = lax.axis_index("xy"), lax.axis_index("lev")
    barrier = pltpu.get_barrier_semaphore()

    def greet(k, unused):
        pl.semaphore_signal(
            barrier, inc=1, device_id={"xy": lax.rem(me + k, N_XY), "lev": level}, device_id_type=MESH
        )
        return unused

    lax.fori_loop(1, N_XY, greet, 0)
    for k in range(1, N_LEV):
        pl.semaphore_signal(
            barrier, inc=1, device_id={"xy": me, "lev": lax.rem(level + k, N_LEV)}, device_id_type=MESH
        )

    small = [
        pltpu.make_async_copy(source, target, small_sem.at[i])
        for i, (source, target) in enumerate(
            [(dest, dest_in), (cell, cell_in), (mass, mass_s), (inv, inv_s), (low, low_s), (up, up_s)]
        )
    ]
    field = plane_copies(euler, ext, load_sem.at[0], 1)
    coefficients = plane_copies(diffusivity, diff_s, load_sem.at[1]) + plane_copies(wind, wind_s, load_sem.at[2])
    for copy in small[:3]:
        copy.start()

    above, below = lax.rem(me + 1, N_XY), lax.rem(me + N_XY - 1, N_XY)
    up_copy = remote(euler.at[:, GX - 1, :], ext.at[0], halo_send.at[0], halo_recv.at[0], {"xy": above, "lev": level})
    down_copy = remote(euler.at[:, 0, :], ext.at[GX + 1], halo_send.at[1], halo_recv.at[1], {"xy": below, "lev": level})
    pl.semaphore_wait(barrier, N_XY - 1 + N_LEV - 1)
    at_edges(me, [up_copy], [down_copy], "start")

    def wide(ref):
        return lanes([ref[pl.ds(0, 16, stride=2), :], ref[pl.ds(1, 16, stride=2), :]])

    def flat(rows):
        return lanes([rows[i : i + 1] for i in range(16)])

    for copy in small[:3]:
        copy.wait()
    target = wide(dest_in).astype(F32)
    cells = wide(cell_in)
    levels = cells // (GX * GY)
    bucket = (cells // GY) % GX * 2 + levels // 16
    high_low = flat((bucket * 16 + levels % 16 + 1).astype(F32))
    column = flat((cells % GY).astype(F32))
    r, c = (lax.broadcasted_iota(I32, (512, 512), d) for d in (0, 1))
    lower = jnp.where((c < r) & (c // 16 == r // 16), 1.0, 0.0).astype(BF16)
    slot, unused_base = ranks(target, N_XY, lower)
    for copy in small[3:] + field + coefficients:
        copy.start()
    spot_s[...] = one_hot(flat(slot))
    values = two_parts(mass_s[...])
    flat_target = flat(target)

    def mass_copy(other):
        device = {"xy": other, "lev": level}
        return remote(send_mass.at[other], got_mass.at[me], mass_send, mass_recv, device)

    def code_copy(other):
        source, target = send_code.at[pl.ds(other, 1)], got_code.at[pl.ds(me, 1)]
        return remote(source, target, code_send, code_recv, {"xy": other, "lev": level})

    half = N_XY // 2
    for begin in (0, half):
        table = sort_slots(values, high_low, column, flat_target, spot_s[...], begin, half)
        masses = table[: 16 * half].reshape(half, 16, CAP)
        send_mass[begin : begin + half] = masses[:, :8] + masses[:, 8:]
        send_code[begin : begin + half] = table[16 * half : 17 * half] * 256.0 + table[17 * half :]

        def send(k, unused):
            other = begin + lax.rem(me + k, half)

            @pl.when(other != me)
            def _():
                mass_copy(other).start()
                code_copy(other).start()

            return unused

        lax.fori_loop(0, half, send, 0)
    got_mass[me] = send_mass[me]
    pltpu.make_async_copy(send_code.at[pl.ds(me, 1)], got_code.at[pl.ds(me, 1)], code_recv).start()
    pltpu.make_async_copy(send_code.at[pl.ds(me, 1)], spare, code_send).start()

    for copy in small[3:]:
        copy.wait()
    edge_matrix = compose(inv_s, low_s, up_s, triple, p_col, e_col)
    r, c = (lax.broadcasted_iota(I32, (N_XY * (BUCKETS + 1), N_XY * BUCKETS), d) for d in (0, 1))
    order[...] = jnp.where((c < r) & (c % N_XY // SRC == r % N_XY // SRC), 1.0, 0.0).astype(BF16)
    links[level, 0] = p_col[pl.ds(LEV - 1, BINS, stride=LEV), :]
    links[level, 1] = e_col[pl.ds(0, BINS, stride=LEV), :]
    links[level, 2] = p_col[pl.ds(0, BINS, stride=LEV), :]

    def link_copy(k, owner):
        peer = lax.rem(level + k, N_LEV)
        return remote(
            links.at[owner], links.at[owner], link_send.at[k], link_recv.at[k], {"xy": me, "lev": peer}
        )

    for k in range(1, N_LEV):
        link_copy(k, level).start()

    for copy in field + coefficients:
        copy.wait()

    def step(x, unused):
        first[x] = stencil(ext[x + 1], ext[x], ext[x + 2], diff_s[x], wind_s[x])
        return unused

    lax.fori_loop(1, GX - 1, step, 0)

    kept[...] = jnp.broadcast_to(jnp.sum(edge_matrix, axis=1, keepdims=True), (4 * BINS, 128)).reshape(4, BINS, 128)
    high = edge_matrix.astype(BF16)
    low = (edge_matrix - high.astype(F32)).astype(BF16)
    three_parts = lanes([high, high, low])

    def turn(x, unused):
        for i, ref in enumerate((diff_s, wind_s)):
            top = ref[x].astype(BF16)
            rest = (ref[x] - top.astype(F32)).astype(BF16)
            result = jnp.dot(three_parts, jnp.concatenate([top, rest, top], axis=0), preferred_element_type=F32)
            turned[i, x] = result.reshape(4, BINS, GY)
        return unused

    lax.fori_loop(0, GX, turn, 0, unroll=2)
    at_edges(me, [up_copy], [down_copy], "wait")

    @pl.when(me == 0)
    def _():
        ext[0] = jnp.zeros((ROWS, GY), F32)

    @pl.when(me == N_XY - 1)
    def _():
        ext[GX + 1] = jnp.zeros((ROWS, GY), F32)

    lax.fori_loop(0, 2, lambda i, u: step(i * (GX - 1), u), 0)

    for k in range(1, N_LEV):
        link_copy(k, lax.rem(level + N_LEV - k, N_LEV)).wait()
    carry_factors(level, links, factors)

    remote(send_code, got_code, code_send, code_recv, {"xy": above, "lev": level}).wait()
    others = pl.ds(0, N_XY - 1)
    remote(send_mass.at[others], got_mass.at[others], mass_send, mass_recv, {"xy": above, "lev": level}).wait()


def deposit_kernel(
    got_mass, got_code, order, total,
    rows_u, hl_u, col_u, hp_s, lp_s, hl_s, col_s, starts_v, starts_s, sem,
):
    code = got_code[...].astype(I32)
    hl = code // 256
    col = code % 256
    valid = hl > 0
    key = jnp.where(valid, (hl - 1) // 16, -1).astype(F32)
    hl_s[...] = hl.astype(F32)
    col_s[...] = col.astype(F32)
    position, base = ranks(key, BUCKETS, order[...])
    place = position.astype(I32)
    hp_s[...] = jnp.where(valid, place // BLK, -1).astype(F32)
    lp_s[...] = (place % BLK).astype(F32)
    lane = lax.broadcasted_iota(I32, (1, 128), 1)
    longest = jnp.zeros((1, 128), I32)
    before = None
    for k in range(BUCKETS + 1):
        start = jnp.zeros((1, 128), F32)
        for g in range(SETS):
            at = N_XY * k + SRC * g
            start = jnp.where(lane == g, base[at : at + 1, :], start)
        start = start.astype(I32)
        starts_v[k : k + 1, :] = start
        if k:
            longest = jnp.maximum(longest, start - before // 128 * 128)
        before = start
    starts_v[BUCKETS + 1 : BUCKETS + 2, :] = longest
    to_scalars = pltpu.make_async_copy(starts_v, starts_s, sem)
    to_scalars.start()

    def one_set(g, unused):
        take = lambda ref: lanes([ref[pl.ds(g * SRC + i, 1), :] for i in range(SRC)])
        values = lanes([two_parts(got_mass[g * SRC + i]) for i in range(SRC)])
        table = sort_slots(values, take(hl_s), take(col_s), take(hp_s), one_hot(take(lp_s)), 0, SRC)
        for half in range(2):
            side = slice(128 * half, 128 * half + 128)
            for d in range(SRC):
                rows_u[g, 2 * d + half] = table[16 * d : 16 * d + 16, side]
            hl_u[g, pl.ds(half, SRC, stride=2), :] = table[16 * SRC : 17 * SRC, side]
            col_u[g, pl.ds(half, SRC, stride=2), :] = table[17 * SRC : 18 * SRC, side]
        rows_u[g, UNITS:] = jnp.zeros((WIN, 16, 128), F32)
        hl_u[g, UNITS:, :] = jnp.zeros((8, 128), F32)
        col_u[g, UNITS:, :] = jnp.zeros((8, 128), F32)
        return unused

    lax.fori_loop(0, SETS, one_set, 0)
    to_scalars.wait()

    def place_of(k):
        return k // 2, pl.ds(pl.multiple_of((k % 2) * 16, 16), 16)

    def window(k, t):
        first_code = (k * 16 + 1).astype(F32)
        at = [jnp.minimum(starts_s[k, g] // 128 + WIN * t, UNITS) for g in range(SETS)]
        units = [(g, at[g] + i) for g in range(SETS) for i in range(WIN)]
        hl_row = lanes([hl_u[g, pl.ds(u, 1), :] for g, u in units])
        col_row = lanes([col_u[g, pl.ds(u, 1), :] for g, u in units])
        rows = lanes([rows_u[g, u] for g, u in units])
        width = 128 * WIN * SETS
        mine = jnp.broadcast_to(hl_row, (16, width)) == iota((16, width), 0) + first_code
        spread = [jnp.where(mine, jnp.broadcast_to(rows[q : q + 1, :], (16, width)), 0.0) for q in range(16)]
        spread.insert(8, jnp.where(mine, 1.0, 0.0))
        weighted = jnp.concatenate(spread, axis=0).astype(BF16)
        table = lax.dot_general(weighted, one_hot(col_row), NT, preferred_element_type=F32)
        table = table.reshape(17, 16, GY)
        return jnp.concatenate([table[:8] + table[9:], table[8:9]], axis=0)

    def one_bucket(k, unused):
        x, levels = place_of(k)
        total[x, :, levels, :] = window(k, 0)
        return unused

    lax.fori_loop(0, BUCKETS, one_bucket, 0, unroll=16)

    def rest(k, unused):
        x, levels = place_of(k)
        rounds = jnp.int32(1)
        for g in range(SETS):
            span = starts_s[k + 1, g] - starts_s[k, g] // 128 * 128
            rounds = jnp.maximum(rounds, (span + 128 * WIN - 1) // (128 * WIN))

        def again(t, unused):
            total[x, :, levels, :] += window(k, t)
            return unused

        lax.fori_loop(1, rounds, again, 0)
        return unused

    most = starts_s[BUCKETS + 1, 0]
    for g in range(1, SETS):
        most = jnp.maximum(most, starts_s[BUCKETS + 1, g])

    @pl.when(most > 128 * WIN)
    def _():
        lax.fori_loop(0, BUCKETS, rest, 0)


def correction(values, down, upward, p_col, e_col):
    shape = (BINS, LEV, GY)
    p_wide = lanes([p_col[...], p_col[...]]).reshape(shape)
    e_wide = lanes([e_col[...], e_col[...]]).reshape(shape)
    result = values.reshape(shape) + p_wide * down[:, None, :] + e_wide * upward[:, None, :]
    return result.reshape(ROWS, GY)


PARTS = (((0, 2), (2, 3), (5, 3)), ((0, 4), (4, 4)))


def solve_kernel(
    total, first, diffusivity, wind, triple, p_col, e_col, factors, kept, turned,
    second, down_out, up_out,
    ext, fixed, diff_s, wind_s, sum_s, beside, edge, seen, seen_halo, edge_w, edge2, seen2, edge3, seen_halo2, carry,
    load_sem, lev_send, lev_recv, diag_send, diag_recv, halo_send, halo_recv, side_send, side_recv,
):
    me, level = lax.axis_index("xy"), lax.axis_index("lev")
    above, below = lax.rem(me + 1, N_XY), lax.rem(me + N_XY - 1, N_XY)
    barrier = pltpu.get_barrier_semaphore()

    def greet(where, least):
        for k in range(least, N_LEV):
            device = {"xy": where, "lev": lax.rem(level + k, N_LEV)}
            pl.semaphore_signal(barrier, inc=1, device_id=device, device_id_type=MESH)

    greet(me, 1)
    pl.when(me < N_XY - 1)(lambda: greet(above, 0))
    pl.when(me > 0)(lambda: greet(below, 0))
    sides = jnp.where(me < N_XY - 1, 1, 0) + jnp.where(me > 0, 1, 0)
    loads = plane_copies(diffusivity, diff_s, load_sem.at[0]) + plane_copies(wind, wind_s, load_sem.at[1])
    for copy in loads:
        copy.start()
    def product(values):
        high = values.astype(BF16)
        low = (values - high.astype(F32)).astype(BF16)
        return jnp.dot(triple[...], jnp.concatenate([high, low, high], axis=0), preferred_element_type=F32)

    def both(i):
        return lanes([factors[i], factors[i]])

    def edges(values, target, place):
        blocks = values.reshape(BINS, LEV, GY)
        last, start = blocks[:, LEV - 1, :], blocks[:, 0, :]
        target[0, place] = last
        target[1, place] = start + both(10) * last

    def carries(tail, seen_at):
        down = jnp.zeros((BINS, GY), F32)
        upward = jnp.zeros((BINS, GY), F32)
        for f in range(N_LEV):
            here = jnp.where(level == f, 0.0, seen_at(f))
            down += both(f) * here
            upward += both(N_LEV + f) * here
        return down, upward + both(8) * tail + both(9) * down

    def tail_of(values):
        return values.reshape(BINS, LEV, GY)[:, LEV - 1, :]

    def peer_of(k):
        return lax.rem(level + k, N_LEV)

    def back(k):
        return lax.rem(level + N_LEV - k, N_LEV)

    def kind(k):
        return jnp.where(peer_of(k) > level, 0, 1)

    def lev_copies(turn, part, own):
        source, target = ((edge, seen), (edge2, seen2))[turn]
        span = pl.ds(*PARTS[turn][part])
        return [
            remote(
                source.at[kind(k), span], target.at[level if own else back(k), span],
                lev_send.at[turn, part, k], lev_recv.at[turn, part, k], {"xy": me, "lev": peer_of(k)},
            )
            for k in range(1, N_LEV)
        ]

    def diag_copies(turn, own):
        source, target = ((edge, seen_halo), (edge3, seen_halo2))[turn]
        return [
            remote(
                source.at[kind(k) if k else 0, 1 - side], target.at[side, level if own else back(k)],
                diag_send.at[turn, side, k], diag_recv.at[turn, side, k], {"xy": where, "lev": peer_of(k)},
            )
            for side, where in enumerate((above, below))
            for k in range(turn, N_LEV)
        ]

    def start(copies):
        for copy in copies:
            copy.start()

    def wait(copies):
        for copy in copies:
            copy.wait()

    def solve_plane(x, place):
        counts = total[x, BINS]
        share = counts / (counts + 2.0)
        old = first[x].reshape(BINS, LEV, GY)
        blended = (1.0 - share)[None] * old + share[None] * total[x, 0:BINS]
        solved = product(blended.reshape(ROWS, GY))
        ext[x + 1] = solved
        edges(solved, edge, place)

    def some(function, begin, count, shift):
        def one(i, unused):
            function(i, i + shift)
            return unused

        lax.fori_loop(begin, begin + count, one, 0, unroll=count)

    solve_plane(0, 0)
    solve_plane(GX - 1, 1)
    wait(loads)
    sum_s[...] = diff_s[0] + wind_s[0]
    pl.semaphore_wait(barrier, N_LEV - 1 + N_LEV * sides)
    halos = [
        remote(ext.at[GX], ext.at[0], halo_send.at[0], halo_recv.at[0], {"xy": above, "lev": level}),
        remote(ext.at[1], ext.at[GX + 1], halo_send.at[1], halo_recv.at[1], {"xy": below, "lev": level}),
    ]
    weights = [
        remote(diff_s.at[GX - 1], beside.at[0], side_send.at[0], side_recv.at[0], {"xy": above, "lev": level}),
        remote(sum_s, beside.at[1], side_send.at[1], side_recv.at[1], {"xy": below, "lev": level}),
    ]
    sent, seen_in = diag_copies(0, True), diag_copies(0, False)
    sent2, seen_in2 = diag_copies(1, True), diag_copies(1, False)
    three = N_LEV - 1
    at_edges(me, sent[:N_LEV], sent[N_LEV:], "start")
    start(lev_copies(0, 0, True))
    at_edges(me, weights[:1], weights[1:], "start")
    at_edges(me, halos[:1], halos[1:], "start")
    some(solve_plane, 1, 3, 1)
    start(lev_copies(0, 1, True))
    some(solve_plane, 4, 3, 1)
    start(lev_copies(0, 2, True))

    def early_plane(x, before, after):
        edges(product(stencil(ext[x + 1], before, after, diff_s[x], wind_s[x])), edge_w, x)

    nothing = jnp.zeros((ROWS, GY), F32)
    early_plane(0, nothing, ext[2])
    some(lambda x, place: early_plane(x, ext[x], ext[x + 2]), 1, 3, 0)
    some(lambda x, place: early_plane(x, ext[x], ext[x + 2]), 4, 3, 0)
    early_plane(GX - 1, ext[GX - 1], nothing)

    def scaled(plane, values):
        return (plane[None] * values.reshape(BINS, LEV, GY)).reshape(ROWS, GY)

    def share_up():
        edges(product(scaled(beside[1], ext[GX])), edge3, 1)
        start(sent2[:three])

    def share_down():
        edges(product(scaled(beside[0], ext[1])), edge3, 0)
        start(sent2[three:])

    at_edges(me, weights[:1], weights[1:], "wait")
    pl.when(me < N_XY - 1)(share_up)
    pl.when(me > 0)(share_down)

    for part in range(3):
        wait(lev_copies(0, part, False))
    at_edges(me, seen_in[:N_LEV], seen_in[N_LEV:], "wait")

    def keep_carries(at, found):
        carry[0, at] = found[0]
        carry[1, at] = found[1]

    def halo_carries(side):
        keep_carries(side * (GX + 1), carries(seen_halo[side, level], lambda f: seen_halo[side, f]))

    def no_carries(side):
        keep_carries(side * (GX + 1), (jnp.zeros((BINS, GY), F32),) * 2)

    pl.when(me > 0)(lambda: halo_carries(0))
    pl.when(me < N_XY - 1)(lambda: halo_carries(1))
    pl.when(me == 0)(lambda: no_carries(0))
    pl.when(me == N_XY - 1)(lambda: no_carries(1))
    for x in range(GX):
        place = {0: 0, GX - 1: 1}.get(x, x + 1)
        keep_carries(x + 1, carries(edge[0, place], lambda f: seen[f, place]))
    lane = lax.broadcasted_iota(I32, (BINS, GY), 1)

    def late_edges(x):
        added = [jnp.zeros((BINS, GY), F32)] * 2
        for v in range(2):
            here, before = carry[v, x + 1], carry[v, x]
            left = jnp.where(lane == 0, 0.0, pltpu.roll(here, 1, 1))
            right = jnp.where(lane == GY - 1, 0.0, pltpu.roll(here, GY - 1, 1))
            laplace = carry[v, x + 2] + before + right + left - 4.0 * here
            drift = here - before
            for end in range(2):
                i = 2 * end + v
                keep = lanes([kept[i], kept[i]])
                added[end] += keep * here + turned[0, x, i] * laplace - turned[1, x, i] * drift
        edge2[0, x] = edge_w[0, x] + added[0]
        edge2[1, x] = edge_w[1, x] + added[1] + both(10) * added[0]

    for part in range(2):
        for x in range(4 * part, 4 * part + 4):
            late_edges(x)
        start(lev_copies(1, part, True))

    def correct_plane(at, unused):
        fixed[at] = correction(ext[at], carry[0, at], carry[1, at], p_col, e_col)

    def second_plane(x, unused):
        second[x] = product(stencil(fixed[x + 1], fixed[x], fixed[x + 2], diff_s[x], wind_s[x]))

    def no_plane(at):
        fixed[at] = nothing

    some(correct_plane, 1, 4, 0)
    some(correct_plane, 5, 4, 0)
    some(second_plane, 1, 3, 0)
    some(second_plane, 4, 3, 0)
    at_edges(me, halos[:1], halos[1:], "wait")
    pl.when(me > 0)(lambda: correct_plane(0, 0))
    pl.when(me < N_XY - 1)(lambda: correct_plane(GX + 1, 0))
    pl.when(me == 0)(lambda: no_plane(0))
    pl.when(me == N_XY - 1)(lambda: no_plane(GX + 1))
    second_plane(0, 0)
    second_plane(GX - 1, 0)
    at_edges(me, seen_in2[:three], seen_in2[three:], "wait")

    def no_share(side):
        seen_halo2[side] = jnp.zeros((N_LEV, BINS, GY), F32)

    pl.when(me == 0)(lambda: no_share(0))
    pl.when(me == N_XY - 1)(lambda: no_share(1))

    def seen_at(x):
        if x == 0:
            return lambda f: seen2[f, 0] + seen_halo2[0, f]
        if x == GX - 1:
            return lambda f: seen2[f, GX - 1] + seen_halo2[1, f]
        return lambda f: seen2[f, x]

    wait(lev_copies(1, 0, False))
    for x in range(4):
        down, upward = carries(tail_of(second[x]), seen_at(x))
        second[x] = correction(second[x], down, upward, p_col, e_col)
    wait(lev_copies(1, 1, False))
    for x in range(4, GX):
        down, upward = carries(tail_of(second[x]), seen_at(x))
        down_out[x - 4] = down
        up_out[x - 4] = upward


def finish_kernel(second, down, upward, p_col, e_col, out, outer, sem):
    inner = [pltpu.make_async_copy(second.at[x], out.at[:, x, :], sem.at[x]) for x in range(4)]
    for copy in inner:
        copy.start()
    last = []
    for i in range(4):
        x = 4 + i
        outer[i] = correction(second[x], down[i], upward[i], p_col, e_col)
        last.append(pltpu.make_async_copy(outer.at[i], out.at[:, x, :], sem.at[x]))
        last[i].start()
    for copy in inner + last:
        copy.wait()


def vmem(*shape, dtype=F32):
    return pltpu.VMEM(shape, dtype)


def whole(count):
    return [pl.BlockSpec(memory_space=pltpu.VMEM)] * count


def somewhere(count):
    return [pl.BlockSpec(memory_space=pltpu.HBM)] * count


def shaped(*shape, dtype=F32):
    return jax.ShapeDtypeStruct(shape, dtype)


def shards(
    euler_field, parcel_mass, dest_device, dest_cell, diffusivity, wind_speed, inverses, lower_coupling, upper_coupling
):
    dma = pltpu.SemaphoreType.DMA
    euler, mass, dest, cell, diffusivity, wind, inv, low, up = [
        pltpu.with_memory_space_constraint(array, pltpu.HBM)
        for array in (
            euler_field.reshape(ROWS, GX, GY), parcel_mass, dest_device.reshape(32, 128), dest_cell.reshape(32, 128),
            diffusivity, wind_speed, inverses, lower_coupling, upper_coupling,
        )
    ]
    routed = pl.pallas_call(
        route_kernel,
        name="route",
        out_shape=[
            shaped(GX, ROWS, GY), shaped(N_XY, BINS, CAP), shaped(N_XY, CAP),
            shaped(N_XY * (BUCKETS + 1), N_XY * BUCKETS, dtype=BF16), shaped(ROWS, 3 * ROWS, dtype=BF16),
            shaped(ROWS, 128), shaped(ROWS, 128), shaped(11, BINS, 128),
            shaped(4, BINS, 128), shaped(2, GX, 4, BINS, GY),
        ],
        in_specs=somewhere(9),
        out_specs=whole(10),
        scratch_shapes=[
            vmem(GX + 2, ROWS, GY), vmem(GX, LEV, GY), vmem(GX, LEV, GY),
            vmem(BINS, PARC), vmem(32, 128, dtype=I32), vmem(32, 128, dtype=I32),
            vmem(2, BINS, 16, 16), vmem(2, BINS), vmem(2, BINS),
            vmem(N_XY, BINS, CAP), vmem(N_XY, CAP), vmem(1, CAP), vmem(CAP, PARC, dtype=BF16), vmem(N_LEV, 3, BINS, 128),
            dma((3, GX)), dma((6,)), dma((2,)), dma((2,)), dma, dma, dma, dma,
            dma((N_LEV,)), dma((N_LEV,)),
        ],
        compiler_params=pltpu.CompilerParams(collective_id=0, has_side_effects=True, vmem_limit_bytes=LIMIT),
    )(euler, mass, dest, cell, diffusivity, wind, inv, low, up)
    first, got_mass, got_code, order, triple, p_col, e_col, factors, kept, turned = routed
    total = pl.pallas_call(
        deposit_kernel,
        name="deposit",
        out_shape=shaped(GX, BINS + 1, LEV, GY),
        in_specs=whole(3),
        out_specs=pl.BlockSpec(memory_space=pltpu.VMEM),
        scratch_shapes=[
            vmem(SETS, UNITS + WIN, 16, 128), vmem(SETS, UNITS + 8, 128), vmem(SETS, UNITS + 8, 128),
            vmem(N_XY, BLK), vmem(N_XY, BLK), vmem(N_XY, BLK), vmem(N_XY, BLK),
            vmem(BUCKETS + 8, 128, dtype=I32), pltpu.SMEM((BUCKETS + 8, 128), I32), dma,
        ],
        compiler_params=pltpu.CompilerParams(vmem_limit_bytes=LIMIT),
    )(got_mass, got_code, order)
    second, down, upward = pl.pallas_call(
        solve_kernel,
        name="solve",
        out_shape=[shaped(GX, ROWS, GY), shaped(4, BINS, GY), shaped(4, BINS, GY)],
        in_specs=whole(2) + somewhere(2) + whole(6),
        out_specs=whole(3),
        scratch_shapes=[
            vmem(GX + 2, ROWS, GY), vmem(GX + 2, ROWS, GY),
            vmem(GX, LEV, GY), vmem(GX, LEV, GY), vmem(LEV, GY), vmem(2, LEV, GY),
            vmem(2, GX, BINS, GY), vmem(N_LEV, GX, BINS, GY), vmem(2, N_LEV, BINS, GY),
            vmem(2, GX, BINS, GY), vmem(2, GX, BINS, GY), vmem(N_LEV, GX, BINS, GY),
            vmem(2, 2, BINS, GY), vmem(2, N_LEV, BINS, GY), vmem(2, GX + 2, BINS, GY),
            dma((2, GX)), dma((2, 3, N_LEV)), dma((2, 3, N_LEV)), dma((2, 2, N_LEV)), dma((2, 2, N_LEV)),
            dma((2,)), dma((2,)), dma((2,)), dma((2,)),
        ],
        compiler_params=pltpu.CompilerParams(collective_id=1, has_side_effects=True, vmem_limit_bytes=LIMIT),
    )(total, first, diffusivity, wind, triple, p_col, e_col, factors, kept, turned)
    result = pl.pallas_call(
        finish_kernel,
        name="finish",
        out_shape=shaped(ROWS, GX, GY),
        in_specs=whole(5),
        out_specs=pl.BlockSpec(memory_space=pltpu.HBM),
        scratch_shapes=[vmem(4, ROWS, GY), dma((GX,))],
        compiler_params=pltpu.CompilerParams(vmem_limit_bytes=LIMIT),
    )(second, down, upward, p_col, e_col)
    return result.reshape(BINS, LEV, GX, GY)


def solution(mesh):
    placed = (
        P(None, "lev", "xy", None),
        P(None, ("xy", "lev")),
        P(("xy", "lev"), None),
        P(("xy", "lev")),
        P("lev", "xy", None),
        P("lev", "xy", None),
        P("lev", None, None, None),
        P("lev", None),
        P("lev", None),
    )
    return jax.shard_map(
        shards, mesh=mesh, in_specs=placed, out_specs=P(None, "lev", "xy", None), check_vma=False
    )
```

```python
import functools

import jax
import jax.numpy as jnp
from jax import lax
from jax.experimental import pallas as pl
from jax.experimental.pallas import tpu as pltpu
from jax.sharding import PartitionSpec as P

F32, BF16, I32 = jnp.float32, jnp.bfloat16, jnp.int32
MESH = pl.DeviceIdType.MESH
N_XY, N_LEV, BINS, LEV, GX, GY = 32, 4, 8, 32, 8, 256
ROWS = BINS * LEV
PARC, CAP, BLK = 4096, 256, 256
BUCKETS = 16
NT = (((1,), (1,)), ((), ()))
LIMIT = 24 << 20
SETS = 2
SRC = N_XY // SETS
SPAN = SRC * CAP
UNITS = SPAN // 128
WIN = 4


def iota(shape, dim, dtype=F32):
    return lax.broadcasted_iota(I32, shape, dim).astype(dtype)


def ranks(keys, count, lower):
    n = keys.shape[0]
    masks = [jnp.where(keys == k, 1.0, 0.0) for k in range(count)]
    stack = jnp.concatenate(masks, axis=0).astype(BF16)
    before = (iota((BLK, BLK), 0) < iota((BLK, BLK), 1)).astype(BF16)
    inside = jnp.dot(stack, before, preferred_element_type=F32)
    totals = jnp.dot(stack, jnp.ones((BLK, 128), BF16), preferred_element_type=F32)
    base = jnp.dot(lower, totals.astype(BF16), preferred_element_type=F32)
    wide = jnp.concatenate([base, base], axis=1)
    whole = inside + wide[: inside.shape[0]]
    position = jnp.zeros(keys.shape, F32)
    for k in range(count):
        position += masks[k] * whole[k * n : (k + 1) * n]
    return position, base


def lanes(pieces):
    return jnp.concatenate(pieces, axis=1)


def one_hot(row):
    width = row.shape[1]
    wide = jnp.broadcast_to(row, (BLK, width)).astype(BF16)
    ids = iota((BLK, width), 0, BF16)
    return jnp.where(ids == wide, jnp.ones((BLK, width), BF16), jnp.zeros((BLK, width), BF16))


def sort_slots(values16, high_low, column, target, spot, first, count):
    width = target.shape[1]
    chosen = jnp.broadcast_to(target, (16, width)).astype(BF16)
    zero = jnp.zeros((16, width), BF16)
    parts = [jnp.where(chosen == jnp.array(first + d, BF16), values16, zero) for d in range(count)]
    mine = iota((count, width), 0) + float(first) == target
    codes = jnp.concatenate([jnp.where(mine, high_low, 0.0), jnp.where(mine, column, 0.0)], axis=0)
    weighted = jnp.concatenate(parts + [codes.astype(BF16)], axis=0)
    return lax.dot_general(weighted, spot, NT, preferred_element_type=F32)


def two_parts(values):
    high = values.astype(BF16).astype(F32)
    return jnp.concatenate([high, values - high], axis=0).astype(BF16)


def stencil(centre, before, after, diffusivity, wind):
    shape = (BINS, LEV, GY)
    lane = lax.broadcasted_iota(I32, (ROWS, GY), 1)
    left = jnp.where(lane == 0, 0.0, pltpu.roll(centre, 1, 1))
    right = jnp.where(lane == GY - 1, 0.0, pltpu.roll(centre, GY - 1, 1))
    laplace = (after + before + right + left - 4.0 * centre).reshape(shape)
    drift = (centre - before).reshape(shape)
    result = centre.reshape(shape) + diffusivity[None] * laplace - wind[None] * drift
    return result.reshape(ROWS, GY)


def at_edges(me, upward, downward, action):
    @pl.when(me < N_XY - 1)
    def _():
        for copy in upward:
            copy.start() if action == "start" else copy.wait_send()
        for copy in downward if action == "wait" else []:
            copy.wait_recv()

    @pl.when(me > 0)
    def _():
        for copy in downward:
            copy.start() if action == "start" else copy.wait_send()
        for copy in upward if action == "wait" else []:
            copy.wait_recv()


def plane_copies(source, target, sems, at=0):
    return [pltpu.make_async_copy(source.at[:, x, :], target.at[at + x], sems.at[x]) for x in range(GX)]


def remote(src, dst, send, recv, device):
    return pltpu.make_async_remote_copy(
        src_ref=src, dst_ref=dst, send_sem=send, recv_sem=recv, device_id=device, device_id_type=MESH
    )


def compose(inv, low, up, triple, p_ref, e_ref):
    lane16 = lax.broadcasted_iota(I32, (16, ROWS), 1) % LEV
    row16 = lax.broadcasted_iota(I32, (16, ROWS), 0)
    own = lax.broadcasted_iota(I32, (BINS, 16, ROWS), 0) == (
        lax.broadcasted_iota(I32, (BINS, 16, ROWS), 2) // LEV
    )

    def spread(group):
        place = (lane16 == row16 + 16 * group).astype(F32)
        flat = inv[group].reshape(BINS * 16, 16)
        full = jnp.dot(flat, place, precision=lax.Precision.HIGHEST, preferred_element_type=F32)
        return jnp.where(own, full.reshape(BINS, 16, ROWS), 0.0)

    def per_bin(ref, group):
        wide = jnp.broadcast_to(ref[group : group + 1, :].reshape(1, 1, BINS), (BINS, 1, BINS))
        same = lax.broadcasted_iota(I32, (BINS, 1, BINS), 0) == lax.broadcasted_iota(
            I32, (BINS, 1, BINS), 2
        )
        return jnp.sum(jnp.where(same, wide, 0.0), axis=2, keepdims=True)

    t0, t1 = spread(0), spread(1)
    l0, l1, u0, u1 = per_bin(low, 0), per_bin(low, 1), per_bin(up, 0), per_bin(up, 1)
    m0, m1 = inv[0], inv[1]
    m0_first, m0_last = m0[:, :, 0:1], m0[:, :, 15:16]
    m1_first, m1_last = m1[:, :, 0:1], m1[:, :, 15:16]
    tail0 = t0[:, 15:16, :]
    link = (l1 * m1[:, 0:1, 0:1]) * tail0 + t1[:, 0:1, :]
    p0 = t0 + (u0 * m0_last) * link
    p1 = t1 + (l1 * m1_first) * tail0
    full = jnp.concatenate([p0, p1], axis=1).reshape(ROWS, ROWS)
    high = full.astype(BF16)
    triple[:, 0:ROWS] = high
    triple[:, ROWS : 2 * ROWS] = high
    triple[:, 2 * ROWS :] = (full - high.astype(F32)).astype(BF16)
    passed = l1 * l0 * m0[:, 15:16, 0:1]
    c0 = l0 * m0_first + (u0 * m0_last) * (passed * m1[:, 0:1, 0:1])
    c1 = passed * m1_first
    d0 = (u0 * u1 * m1[:, 0:1, 15:16]) * m0_last
    d1 = u1 * m1_last
    p_ref[...] = jnp.broadcast_to(jnp.concatenate([c0, c1], axis=1), (BINS, LEV, 128)).reshape(ROWS, 128)
    e_ref[...] = jnp.broadcast_to(jnp.concatenate([d0, d1], axis=1), (BINS, LEV, 128)).reshape(ROWS, 128)
    blocks = full.reshape(BINS, LEV, ROWS)
    eye = lax.broadcasted_iota(I32, (ROWS, ROWS), 0) == lax.broadcasted_iota(I32, (ROWS, ROWS), 1)
    across = [jnp.sum(jnp.where(eye, lanes([ref[...], ref[...]]), 0.0), axis=0, keepdims=True) for ref in (p_ref, e_ref)]
    rows = jnp.concatenate([blocks[:, at, :] * col for at in (LEV - 1, 0) for col in across], axis=0)
    fold = (
        lax.broadcasted_iota(I32, (ROWS, LEV), 0) % LEV == lax.broadcasted_iota(I32, (ROWS, LEV), 1)
    ).astype(F32)
    return jnp.dot(rows, fold, precision=lax.Precision.HIGHEST, preferred_element_type=F32)


def carry_factors(level, all_ref, out_ref):
    alpha = [all_ref[f, 0] for f in range(N_LEV)]
    beta = [all_ref[f, 1] for f in range(N_LEV)]
    gamma = [all_ref[f, 2] for f in range(N_LEV)]
    zero, one = jnp.zeros((BINS, 128), F32), jnp.ones((BINS, 128), F32)
    for f in range(N_LEV):
        down, product = zero, one
        for i in range(f + 1, N_LEV):
            down = jnp.where(level == i, product, down)
            product = product * alpha[i]
        upward, product = zero, one
        for i in range(f - 1, -1, -1):
            upward = jnp.where(level == i, product, upward)
            product = product * beta[i]
        out_ref[f] = down
        out_ref[N_LEV + f] = upward
    sigma = [zero] * N_LEV
    for f in range(N_LEV - 1, 0, -1):
        sigma[f - 1] = gamma[f] + beta[f] * alpha[f] * sigma[f]

    def own(values):
        result = values[0]
        for f in range(1, N_LEV):
            result = jnp.where(level == f, values[f], result)
        return result

    out_ref[8] = own(sigma)
    out_ref[9] = own([sigma[f] * alpha[f] for f in range(N_LEV)])
    out_ref[10] = own([sigma[f] * beta[f] for f in range(N_LEV)])


def route_kernel(
    euler, mass, dest, cell, diffusivity, wind, inv, low, up,
    first, got_mass, got_code, order, triple, p_col, e_col, factors, kept, turned,
    ext, diff_s, wind_s, mass_s, dest_in, cell_in, inv_s, low_s, up_s,
    send_mass, send_code, spare, spot_s, links,
    load_sem, small_sem, halo_send, halo_recv, mass_send, mass_recv, code_send, code_recv, link_send, link_recv,
):
    me, level = lax.axis_index("xy"), lax.axis_index("lev")
    barrier = pltpu.get_barrier_semaphore()

    def greet(k, unused):
        pl.semaphore_signal(
            barrier, inc=1, device_id={"xy": lax.rem(me + k, N_XY), "lev": level}, device_id_type=MESH
        )
        return unused

    lax.fori_loop(1, N_XY, greet, 0)
    for k in range(1, N_LEV):
        pl.semaphore_signal(
            barrier, inc=1, device_id={"xy": me, "lev": lax.rem(level + k, N_LEV)}, device_id_type=MESH
        )

    small = [
        pltpu.make_async_copy(source, target, small_sem.at[i])
        for i, (source, target) in enumerate(
            [(dest, dest_in), (cell, cell_in), (mass, mass_s), (inv, inv_s), (low, low_s), (up, up_s)]
        )
    ]
    field = plane_copies(euler, ext, load_sem.at[0], 1)
    coefficients = plane_copies(diffusivity, diff_s, load_sem.at[1]) + plane_copies(wind, wind_s, load_sem.at[2])
    for copy in small[:3]:
        copy.start()

    above, below = lax.rem(me + 1, N_XY), lax.rem(me + N_XY - 1, N_XY)
    up_copy = remote(euler.at[:, GX - 1, :], ext.at[0], halo_send.at[0], halo_recv.at[0], {"xy": above, "lev": level})
    down_copy = remote(euler.at[:, 0, :], ext.at[GX + 1], halo_send.at[1], halo_recv.at[1], {"xy": below, "lev": level})
    pl.semaphore_wait(barrier, N_XY - 1 + N_LEV - 1)
    at_edges(me, [up_copy], [down_copy], "start")

    def wide(ref):
        return lanes([ref[pl.ds(0, 16, stride=2), :], ref[pl.ds(1, 16, stride=2), :]])

    def flat(rows):
        return lanes([rows[i : i + 1] for i in range(16)])

    for copy in small[:3]:
        copy.wait()
    target = wide(dest_in).astype(F32)
    cells = wide(cell_in)
    levels = cells // (GX * GY)
    bucket = (cells // GY) % GX * 2 + levels // 16
    high_low = flat((bucket * 16 + levels % 16 + 1).astype(F32))
    column = flat((cells % GY).astype(F32))
    r, c = (lax.broadcasted_iota(I32, (512, 512), d) for d in (0, 1))
    lower = jnp.where((c < r) & (c // 16 == r // 16), 1.0, 0.0).astype(BF16)
    slot, unused_base = ranks(target, N_XY, lower)
    for copy in small[3:] + field + coefficients:
        copy.start()
    spot_s[...] = one_hot(flat(slot))
    values = two_parts(mass_s[...])
    flat_target = flat(target)

    def mass_copy(other):
        device = {"xy": other, "lev": level}
        return remote(send_mass.at[other], got_mass.at[me], mass_send, mass_recv, device)

    def code_copy(other):
        source, target = send_code.at[pl.ds(other, 1)], got_code.at[pl.ds(me, 1)]
        return remote(source, target, code_send, code_recv, {"xy": other, "lev": level})

    half = N_XY // 2
    for begin in (0, half):
        table = sort_slots(values, high_low, column, flat_target, spot_s[...], begin, half)
        masses = table[: 16 * half].reshape(half, 16, CAP)
        send_mass[begin : begin + half] = masses[:, :8] + masses[:, 8:]
        send_code[begin : begin + half] = table[16 * half : 17 * half] * 256.0 + table[17 * half :]

        def send(k, unused):
            other = begin + lax.rem(me + k, half)

            @pl.when(other != me)
            def _():
                mass_copy(other).start()
                code_copy(other).start()

            return unused

        lax.fori_loop(0, half, send, 0)
    got_mass[me] = send_mass[me]
    pltpu.make_async_copy(send_code.at[pl.ds(me, 1)], got_code.at[pl.ds(me, 1)], code_recv).start()
    pltpu.make_async_copy(send_code.at[pl.ds(me, 1)], spare, code_send).start()

    for copy in small[3:]:
        copy.wait()
    edge_matrix = compose(inv_s, low_s, up_s, triple, p_col, e_col)
    r, c = (lax.broadcasted_iota(I32, (N_XY * (BUCKETS + 1), N_XY * BUCKETS), d) for d in (0, 1))
    order[...] = jnp.where((c < r) & (c % N_XY // SRC == r % N_XY // SRC), 1.0, 0.0).astype(BF16)
    links[level, 0] = p_col[pl.ds(LEV - 1, BINS, stride=LEV), :]
    links[level, 1] = e_col[pl.ds(0, BINS, stride=LEV), :]
    links[level, 2] = p_col[pl.ds(0, BINS, stride=LEV), :]

    def link_copy(k, owner):
        peer = lax.rem(level + k, N_LEV)
        return remote(
            links.at[owner], links.at[owner], link_send.at[k], link_recv.at[k], {"xy": me, "lev": peer}
        )

    for k in range(1, N_LEV):
        link_copy(k, level).start()

    for copy in field + coefficients:
        copy.wait()

    def step(x, unused):
        first[x] = stencil(ext[x + 1], ext[x], ext[x + 2], diff_s[x], wind_s[x])
        return unused

    lax.fori_loop(1, GX - 1, step, 0)

    kept[...] = jnp.broadcast_to(jnp.sum(edge_matrix, axis=1, keepdims=True), (4 * BINS, 128)).reshape(4, BINS, 128)
    high = edge_matrix.astype(BF16)
    low = (edge_matrix - high.astype(F32)).astype(BF16)
    three_parts = lanes([high, high, low])

    def turn(x, unused):
        for i, ref in enumerate((diff_s, wind_s)):
            top = ref[x].astype(BF16)
            rest = (ref[x] - top.astype(F32)).astype(BF16)
            result = jnp.dot(three_parts, jnp.concatenate([top, rest, top], axis=0), preferred_element_type=F32)
            turned[i, x] = result.reshape(4, BINS, GY)
        return unused

    lax.fori_loop(0, GX, turn, 0, unroll=2)
    at_edges(me, [up_copy], [down_copy], "wait")

    @pl.when(me == 0)
    def _():
        ext[0] = jnp.zeros((ROWS, GY), F32)

    @pl.when(me == N_XY - 1)
    def _():
        ext[GX + 1] = jnp.zeros((ROWS, GY), F32)

    lax.fori_loop(0, 2, lambda i, u: step(i * (GX - 1), u), 0)

    for k in range(1, N_LEV):
        link_copy(k, lax.rem(level + N_LEV - k, N_LEV)).wait()
    carry_factors(level, links, factors)

    remote(send_code, got_code, code_send, code_recv, {"xy": above, "lev": level}).wait()
    others = pl.ds(0, N_XY - 1)
    remote(send_mass.at[others], got_mass.at[others], mass_send, mass_recv, {"xy": above, "lev": level}).wait()


def deposit_kernel(
    got_mass, got_code, order, total,
    rows_u, hl_u, col_u, hp_s, lp_s, hl_s, col_s, starts_v, starts_s, sem,
):
    code = got_code[...].astype(I32)
    hl = code // 256
    col = code % 256
    valid = hl > 0
    key = jnp.where(valid, (hl - 1) // 16, -1).astype(F32)
    hl_s[...] = hl.astype(F32)
    col_s[...] = col.astype(F32)
    position, base = ranks(key, BUCKETS, order[...])
    place = position.astype(I32)
    hp_s[...] = jnp.where(valid, place // BLK, -1).astype(F32)
    lp_s[...] = (place % BLK).astype(F32)
    lane = lax.broadcasted_iota(I32, (1, 128), 1)
    longest = jnp.zeros((1, 128), I32)
    before = None
    for k in range(BUCKETS + 1):
        start = jnp.zeros((1, 128), F32)
        for g in range(SETS):
            at = N_XY * k + SRC * g
            start = jnp.where(lane == g, base[at : at + 1, :], start)
        start = start.astype(I32)
        starts_v[k : k + 1, :] = start
        if k:
            longest = jnp.maximum(longest, start - before // 128 * 128)
        before = start
    starts_v[BUCKETS + 1 : BUCKETS + 2, :] = longest
    to_scalars = pltpu.make_async_copy(starts_v, starts_s, sem)
    to_scalars.start()

    def one_set(g, unused):
        take = lambda ref: lanes([ref[pl.ds(g * SRC + i, 1), :] for i in range(SRC)])
        values = lanes([two_parts(got_mass[g * SRC + i]) for i in range(SRC)])
        table = sort_slots(values, take(hl_s), take(col_s), take(hp_s), one_hot(take(lp_s)), 0, SRC)
        for half in range(2):
            side = slice(128 * half, 128 * half + 128)
            for d in range(SRC):
                rows_u[g, 2 * d + half] = table[16 * d : 16 * d + 16, side]
            hl_u[g, pl.ds(half, SRC, stride=2), :] = table[16 * SRC : 17 * SRC, side]
            col_u[g, pl.ds(half, SRC, stride=2), :] = table[17 * SRC : 18 * SRC, side]
        rows_u[g, UNITS:] = jnp.zeros((WIN, 16, 128), F32)
        hl_u[g, UNITS:, :] = jnp.zeros((8, 128), F32)
        col_u[g, UNITS:, :] = jnp.zeros((8, 128), F32)
        return unused

    lax.fori_loop(0, SETS, one_set, 0)
    to_scalars.wait()

    def place_of(k):
        return k // 2, pl.ds(pl.multiple_of((k % 2) * 16, 16), 16)

    def window(k, t):
        first_code = (k * 16 + 1).astype(F32)
        at = [jnp.minimum(starts_s[k, g] // 128 + WIN * t, UNITS) for g in range(SETS)]
        units = [(g, at[g] + i) for g in range(SETS) for i in range(WIN)]
        hl_row = lanes([hl_u[g, pl.ds(u, 1), :] for g, u in units])
        col_row = lanes([col_u[g, pl.ds(u, 1), :] for g, u in units])
        rows = lanes([rows_u[g, u] for g, u in units])
        width = 128 * WIN * SETS
        mine = jnp.broadcast_to(hl_row, (16, width)) == iota((16, width), 0) + first_code
        spread = [jnp.where(mine, jnp.broadcast_to(rows[q : q + 1, :], (16, width)), 0.0) for q in range(16)]
        spread.insert(8, jnp.where(mine, 1.0, 0.0))
        weighted = jnp.concatenate(spread, axis=0).astype(BF16)
        table = lax.dot_general(weighted, one_hot(col_row), NT, preferred_element_type=F32)
        table = table.reshape(17, 16, GY)
        return jnp.concatenate([table[:8] + table[9:], table[8:9]], axis=0)

    def one_bucket(k, unused):
        x, levels = place_of(k)
        total[x, :, levels, :] = window(k, 0)
        return unused

    lax.fori_loop(0, BUCKETS, one_bucket, 0, unroll=16)

    def rest(k, unused):
        x, levels = place_of(k)
        rounds = jnp.int32(1)
        for g in range(SETS):
            span = starts_s[k + 1, g] - starts_s[k, g] // 128 * 128
            rounds = jnp.maximum(rounds, (span + 128 * WIN - 1) // (128 * WIN))

        def again(t, unused):
            total[x, :, levels, :] += window(k, t)
            return unused

        lax.fori_loop(1, rounds, again, 0)
        return unused

    most = starts_s[BUCKETS + 1, 0]
    for g in range(1, SETS):
        most = jnp.maximum(most, starts_s[BUCKETS + 1, g])

    @pl.when(most > 128 * WIN)
    def _():
        lax.fori_loop(0, BUCKETS, rest, 0)


def correction(values, down, upward, p_col, e_col):
    shape = (BINS, LEV, GY)
    p_wide = lanes([p_col[...], p_col[...]]).reshape(shape)
    e_wide = lanes([e_col[...], e_col[...]]).reshape(shape)
    result = values.reshape(shape) + p_wide * down[:, None, :] + e_wide * upward[:, None, :]
    return result.reshape(ROWS, GY)


PARTS = (((0, 3), (3, 2), (5, 3)), ((0, 2), (2, 3), (5, 3)))
PLACE = (0, 2, 3, 4, 5, 6, 7, 1)


def solve_kernel(
    total, first, diffusivity, wind, triple, p_col, e_col, factors, kept, turned,
    second, down_out, up_out,
    ext, fixed, diff_s, wind_s, sum_s, beside, edge, seen, seen_halo, edge_w, edge2, seen2, edge3, seen_halo2, carry,
    load_sem, lev_send, lev_recv, diag_send, diag_recv, halo_send, halo_recv, side_send, side_recv,
):
    me, level = lax.axis_index("xy"), lax.axis_index("lev")
    above, below = lax.rem(me + 1, N_XY), lax.rem(me + N_XY - 1, N_XY)
    barrier = pltpu.get_barrier_semaphore()

    def greet(where, least):
        for k in range(least, N_LEV):
            device = {"xy": where, "lev": lax.rem(level + k, N_LEV)}
            pl.semaphore_signal(barrier, inc=1, device_id=device, device_id_type=MESH)

    greet(me, 1)
    pl.when(me < N_XY - 1)(lambda: greet(above, 0))
    pl.when(me > 0)(lambda: greet(below, 0))
    sides = jnp.where(me < N_XY - 1, 1, 0) + jnp.where(me > 0, 1, 0)
    loads = plane_copies(diffusivity, diff_s, load_sem.at[0]) + plane_copies(wind, wind_s, load_sem.at[1])
    for copy in loads:
        copy.start()
    def product(values):
        high = values.astype(BF16)
        low = (values - high.astype(F32)).astype(BF16)
        return jnp.dot(triple[...], jnp.concatenate([high, low, high], axis=0), preferred_element_type=F32)

    def both(i):
        return lanes([factors[i], factors[i]])

    def edges(values, target, place):
        blocks = values.reshape(BINS, LEV, GY)
        last, start = blocks[:, LEV - 1, :], blocks[:, 0, :]
        target[0, place] = last
        target[1, place] = start + both(10) * last

    def carries(tail, seen_at):
        down = jnp.zeros((BINS, GY), F32)
        upward = jnp.zeros((BINS, GY), F32)
        for f in range(N_LEV):
            here = jnp.where(level == f, 0.0, seen_at(f))
            down += both(f) * here
            upward += both(N_LEV + f) * here
        return down, upward + both(8) * tail + both(9) * down

    def tail_of(values):
        return values.reshape(BINS, LEV, GY)[:, LEV - 1, :]

    def peer_of(k):
        return lax.rem(level + k, N_LEV)

    def back(k):
        return lax.rem(level + N_LEV - k, N_LEV)

    def kind(k):
        return jnp.where(peer_of(k) > level, 0, 1)

    def lev_copies(turn, part, own):
        source, target = ((edge, seen), (edge2, seen2))[turn]
        span = pl.ds(*PARTS[turn][part])
        return [
            remote(
                source.at[kind(k), span], target.at[level if own else back(k), span],
                lev_send.at[turn, part, k], lev_recv.at[turn, part, k], {"xy": me, "lev": peer_of(k)},
            )
            for k in range(1, N_LEV)
        ]

    def diag_copies(turn, own):
        source, target = ((edge, seen_halo), (edge3, seen_halo2))[turn]
        return [
            remote(
                source.at[kind(k) if k else 0, ((GX - 1, 0), (1, 0))[turn][side]], target.at[side, level if own else back(k)],
                diag_send.at[turn, side, k], diag_recv.at[turn, side, k], {"xy": where, "lev": peer_of(k)},
            )
            for side, where in enumerate((above, below))
            for k in range(turn, N_LEV)
        ]

    def start(copies):
        for copy in copies:
            copy.start()

    def wait(copies):
        for copy in copies:
            copy.wait()

    def solve_plane(x, place):
        counts = total[x, BINS]
        share = counts / (counts + 2.0)
        old = first[x].reshape(BINS, LEV, GY)
        blended = (1.0 - share)[None] * old + share[None] * total[x, 0:BINS]
        solved = product(blended.reshape(ROWS, GY))
        ext[x + 1] = solved
        edges(solved, edge, place)

    def some(function, begin, count, shift):
        def one(i, unused):
            function(i, i + shift)
            return unused

        lax.fori_loop(begin, begin + count, one, 0, unroll=count)

    some(solve_plane, 0, 3, 0)
    some(solve_plane, 3, 2, 0)
    some(solve_plane, 5, 3, 0)
    wait(loads)
    sum_s[...] = diff_s[0] + wind_s[0]
    pl.semaphore_wait(barrier, N_LEV - 1 + N_LEV * sides)
    halos = [
        remote(ext.at[GX], ext.at[0], halo_send.at[0], halo_recv.at[0], {"xy": above, "lev": level}),
        remote(ext.at[1], ext.at[GX + 1], halo_send.at[1], halo_recv.at[1], {"xy": below, "lev": level}),
    ]
    weights = [
        remote(diff_s.at[GX - 1], beside.at[0], side_send.at[0], side_recv.at[0], {"xy": above, "lev": level}),
        remote(sum_s, beside.at[1], side_send.at[1], side_recv.at[1], {"xy": below, "lev": level}),
    ]
    sent, seen_in = diag_copies(0, True), diag_copies(0, False)
    sent2, seen_in2 = diag_copies(1, True), diag_copies(1, False)
    three = N_LEV - 1
    for part in range(3):
        start(lev_copies(0, part, True))
    at_edges(me, sent[:N_LEV], sent[N_LEV:], "start")
    at_edges(me, weights[:1], weights[1:], "start")
    at_edges(me, halos[:1], halos[1:], "start")

    def early_plane(x, before, after):
        edges(product(stencil(ext[x + 1], before, after, diff_s[x], wind_s[x])), edge_w, x)

    nothing = jnp.zeros((ROWS, GY), F32)
    early_plane(0, nothing, ext[2])
    some(lambda x, place: early_plane(x, ext[x], ext[x + 2]), 1, 3, 0)
    some(lambda x, place: early_plane(x, ext[x], ext[x + 2]), 4, 3, 0)
    early_plane(GX - 1, ext[GX - 1], nothing)

    def scaled(plane, values):
        return (plane[None] * values.reshape(BINS, LEV, GY)).reshape(ROWS, GY)

    def share_up():
        edges(product(scaled(beside[1], ext[GX])), edge3, 1)
        start(sent2[:three])

    def share_down():
        edges(product(scaled(beside[0], ext[1])), edge3, 0)
        start(sent2[three:])

    at_edges(me, weights[:1], weights[1:], "wait")
    pl.when(me < N_XY - 1)(share_up)
    pl.when(me > 0)(share_down)

    def keep_carries(at, found):
        carry[0, at] = found[0]
        carry[1, at] = found[1]

    def halo_carries(side):
        keep_carries(side * (GX + 1), carries(seen_halo[side, level], lambda f: seen_halo[side, f]))

    def no_carries(side):
        keep_carries(side * (GX + 1), (jnp.zeros((BINS, GY), F32),) * 2)

    def plane_carries(begin, end):
        for x in range(begin, end):
            keep_carries(x + 1, carries(edge[0, x], lambda f: seen[f, x]))

    lane = lax.broadcasted_iota(I32, (BINS, GY), 1)

    def late_edges(x):
        added = [jnp.zeros((BINS, GY), F32)] * 2
        for v in range(2):
            here, before = carry[v, x + 1], carry[v, x]
            left = jnp.where(lane == 0, 0.0, pltpu.roll(here, 1, 1))
            right = jnp.where(lane == GY - 1, 0.0, pltpu.roll(here, GY - 1, 1))
            laplace = carry[v, x + 2] + before + right + left - 4.0 * here
            drift = here - before
            for end in range(2):
                i = 2 * end + v
                keep = lanes([kept[i], kept[i]])
                added[end] += keep * here + turned[0, x, i] * laplace - turned[1, x, i] * drift
        edge2[0, PLACE[x]] = edge_w[0, x] + added[0]
        edge2[1, PLACE[x]] = edge_w[1, x] + added[1] + both(10) * added[0]

    wait(lev_copies(0, 0, False) + lev_copies(0, 1, False))
    plane_carries(0, 5)
    for x in range(1, 4):
        late_edges(x)
    start(lev_copies(1, 1, True))
    wait(lev_copies(0, 2, False))
    plane_carries(5, GX)
    for x in range(4, GX - 1):
        late_edges(x)
    start(lev_copies(1, 2, True))
    at_edges(me, seen_in[:N_LEV], seen_in[N_LEV:], "wait")
    pl.when(me > 0)(lambda: halo_carries(0))
    pl.when(me < N_XY - 1)(lambda: halo_carries(1))
    pl.when(me == 0)(lambda: no_carries(0))
    pl.when(me == N_XY - 1)(lambda: no_carries(1))
    late_edges(0)
    late_edges(GX - 1)
    start(lev_copies(1, 0, True))

    def correct_plane(at, unused):
        fixed[at] = correction(ext[at], carry[0, at], carry[1, at], p_col, e_col)

    def second_plane(x, unused):
        second[x] = product(stencil(fixed[x + 1], fixed[x], fixed[x + 2], diff_s[x], wind_s[x]))

    def no_plane(at):
        fixed[at] = nothing

    some(correct_plane, 1, 4, 0)
    some(correct_plane, 5, 4, 0)
    some(second_plane, 1, 3, 0)
    some(second_plane, 4, 3, 0)
    at_edges(me, halos[:1], halos[1:], "wait")
    pl.when(me > 0)(lambda: correct_plane(0, 0))
    pl.when(me < N_XY - 1)(lambda: correct_plane(GX + 1, 0))
    pl.when(me == 0)(lambda: no_plane(0))
    pl.when(me == N_XY - 1)(lambda: no_plane(GX + 1))
    second_plane(0, 0)
    second_plane(GX - 1, 0)
    at_edges(me, seen_in2[:three], seen_in2[three:], "wait")

    def no_share(side):
        seen_halo2[side] = jnp.zeros((N_LEV, BINS, GY), F32)

    pl.when(me == 0)(lambda: no_share(0))
    pl.when(me == N_XY - 1)(lambda: no_share(1))

    def seen_at(x):
        if x == 0:
            return lambda f: seen2[f, 0] + seen_halo2[0, f]
        if x == GX - 1:
            return lambda f: seen2[f, 1] + seen_halo2[1, f]
        return lambda f: seen2[f, PLACE[x]]

    wait(lev_copies(1, 1, False))
    for x in range(1, 4):
        down, upward = carries(tail_of(second[x]), seen_at(x))
        second[x] = correction(second[x], down, upward, p_col, e_col)
    wait(lev_copies(1, 2, False) + lev_copies(1, 0, False))
    for i, x in enumerate(LATE):
        down, upward = carries(tail_of(second[x]), seen_at(x))
        down_out[i] = down
        up_out[i] = upward


LATE = (4, 5, 6, 0, 7)


def finish_kernel(second, down, upward, p_col, e_col, out, outer, sem):
    inner = [pltpu.make_async_copy(second.at[x], out.at[:, x, :], sem.at[x]) for x in range(1, 4)]
    for copy in inner:
        copy.start()
    last = []
    for i, x in enumerate(LATE):
        outer[i] = correction(second[x], down[i], upward[i], p_col, e_col)
        last.append(pltpu.make_async_copy(outer.at[i], out.at[:, x, :], sem.at[x]))
        last[i].start()
    for copy in inner + last:
        copy.wait()


def vmem(*shape, dtype=F32):
    return pltpu.VMEM(shape, dtype)


def whole(count):
    return [pl.BlockSpec(memory_space=pltpu.VMEM)] * count


def somewhere(count):
    return [pl.BlockSpec(memory_space=pltpu.HBM)] * count


def shaped(*shape, dtype=F32):
    return jax.ShapeDtypeStruct(shape, dtype)


def shards(
    euler_field, parcel_mass, dest_device, dest_cell, diffusivity, wind_speed, inverses, lower_coupling, upper_coupling
):
    dma = pltpu.SemaphoreType.DMA
    euler, mass, dest, cell, diffusivity, wind, inv, low, up = [
        pltpu.with_memory_space_constraint(array, pltpu.HBM)
        for array in (
            euler_field.reshape(ROWS, GX, GY), parcel_mass, dest_device.reshape(32, 128), dest_cell.reshape(32, 128),
            diffusivity, wind_speed, inverses, lower_coupling, upper_coupling,
        )
    ]
    routed = pl.pallas_call(
        route_kernel,
        name="route",
        out_shape=[
            shaped(GX, ROWS, GY), shaped(N_XY, BINS, CAP), shaped(N_XY, CAP),
            shaped(N_XY * (BUCKETS + 1), N_XY * BUCKETS, dtype=BF16), shaped(ROWS, 3 * ROWS, dtype=BF16),
            shaped(ROWS, 128), shaped(ROWS, 128), shaped(11, BINS, 128),
            shaped(4, BINS, 128), shaped(2, GX, 4, BINS, GY),
        ],
        in_specs=somewhere(9),
        out_specs=whole(10),
        scratch_shapes=[
            vmem(GX + 2, ROWS, GY), vmem(GX, LEV, GY), vmem(GX, LEV, GY),
            vmem(BINS, PARC), vmem(32, 128, dtype=I32), vmem(32, 128, dtype=I32),
            vmem(2, BINS, 16, 16), vmem(2, BINS), vmem(2, BINS),
            vmem(N_XY, BINS, CAP), vmem(N_XY, CAP), vmem(1, CAP), vmem(CAP, PARC, dtype=BF16), vmem(N_LEV, 3, BINS, 128),
            dma((3, GX)), dma((6,)), dma((2,)), dma((2,)), dma, dma, dma, dma,
            dma((N_LEV,)), dma((N_LEV,)),
        ],
        compiler_params=pltpu.CompilerParams(collective_id=0, has_side_effects=True, vmem_limit_bytes=LIMIT),
    )(euler, mass, dest, cell, diffusivity, wind, inv, low, up)
    first, got_mass, got_code, order, triple, p_col, e_col, factors, kept, turned = routed
    total = pl.pallas_call(
        deposit_kernel,
        name="deposit",
        out_shape=shaped(GX, BINS + 1, LEV, GY),
        in_specs=whole(3),
        out_specs=pl.BlockSpec(memory_space=pltpu.VMEM),
        scratch_shapes=[
            vmem(SETS, UNITS + WIN, 16, 128), vmem(SETS, UNITS + 8, 128), vmem(SETS, UNITS + 8, 128),
            vmem(N_XY, BLK), vmem(N_XY, BLK), vmem(N_XY, BLK), vmem(N_XY, BLK),
            vmem(BUCKETS + 8, 128, dtype=I32), pltpu.SMEM((BUCKETS + 8, 128), I32), dma,
        ],
        compiler_params=pltpu.CompilerParams(vmem_limit_bytes=LIMIT),
    )(got_mass, got_code, order)
    second, down, upward = pl.pallas_call(
        solve_kernel,
        name="solve",
        out_shape=[shaped(GX, ROWS, GY), shaped(len(LATE), BINS, GY), shaped(len(LATE), BINS, GY)],
        in_specs=whole(2) + somewhere(2) + whole(6),
        out_specs=whole(3),
        scratch_shapes=[
            vmem(GX + 2, ROWS, GY), vmem(GX + 2, ROWS, GY),
            vmem(GX, LEV, GY), vmem(GX, LEV, GY), vmem(LEV, GY), vmem(2, LEV, GY),
            vmem(2, GX, BINS, GY), vmem(N_LEV, GX, BINS, GY), vmem(2, N_LEV, BINS, GY),
            vmem(2, GX, BINS, GY), vmem(2, GX, BINS, GY), vmem(N_LEV, GX, BINS, GY),
            vmem(2, 2, BINS, GY), vmem(2, N_LEV, BINS, GY), vmem(2, GX + 2, BINS, GY),
            dma((2, GX)), dma((2, 3, N_LEV)), dma((2, 3, N_LEV)), dma((2, 2, N_LEV)), dma((2, 2, N_LEV)),
            dma((2,)), dma((2,)), dma((2,)), dma((2,)),
        ],
        compiler_params=pltpu.CompilerParams(collective_id=1, has_side_effects=True, vmem_limit_bytes=LIMIT),
    )(total, first, diffusivity, wind, triple, p_col, e_col, factors, kept, turned)
    result = pl.pallas_call(
        finish_kernel,
        name="finish",
        out_shape=shaped(ROWS, GX, GY),
        in_specs=whole(5),
        out_specs=pl.BlockSpec(memory_space=pltpu.HBM),
        scratch_shapes=[vmem(len(LATE), ROWS, GY), dma((GX,))],
        compiler_params=pltpu.CompilerParams(vmem_limit_bytes=LIMIT),
    )(second, down, upward, p_col, e_col)
    return result.reshape(BINS, LEV, GX, GY)


def solution(mesh):
    placed = (
        P(None, "lev", "xy", None),
        P(None, ("xy", "lev")),
        P(("xy", "lev"), None),
        P(("xy", "lev")),
        P("lev", "xy", None),
        P("lev", "xy", None),
        P("lev", None, None, None),
        P("lev", None),
        P("lev", None),
    )
    return jax.shard_map(
        shards, mesh=mesh, in_specs=placed, out_specs=P(None, "lev", "xy", None), check_vma=False
    )
```

```python
import functools

import jax
import jax.numpy as jnp
from jax import lax
from jax.experimental import pallas as pl
from jax.experimental.pallas import tpu as pltpu
from jax.sharding import PartitionSpec as P

F32, BF16, I32 = jnp.float32, jnp.bfloat16, jnp.int32
MESH = pl.DeviceIdType.MESH
N_XY, N_LEV, BINS, LEV, GX, GY = 32, 4, 8, 32, 8, 256
ROWS = BINS * LEV
PARC, CAP, BLK = 4096, 256, 256
BUCKETS = 16
NT = (((1,), (1,)), ((), ()))
LIMIT = 24 << 20
SETS = 2
SRC = N_XY // SETS
SPAN = SRC * CAP
UNITS = SPAN // 128
WIN = 4


def iota(shape, dim, dtype=F32):
    return lax.broadcasted_iota(I32, shape, dim).astype(dtype)


def ranks(keys, count, lower):
    n = keys.shape[0]
    masks = [jnp.where(keys == k, 1.0, 0.0) for k in range(count)]
    stack = jnp.concatenate(masks, axis=0).astype(BF16)
    before = (iota((BLK, BLK), 0) < iota((BLK, BLK), 1)).astype(BF16)
    inside = jnp.dot(stack, before, preferred_element_type=F32)
    totals = jnp.dot(stack, jnp.ones((BLK, 128), BF16), preferred_element_type=F32)
    base = jnp.dot(lower, totals.astype(BF16), preferred_element_type=F32)
    wide = jnp.concatenate([base, base], axis=1)
    whole = inside + wide[: inside.shape[0]]
    position = jnp.zeros(keys.shape, F32)
    for k in range(count):
        position += masks[k] * whole[k * n : (k + 1) * n]
    return position, base


def lanes(pieces):
    return jnp.concatenate(pieces, axis=1)


def one_hot(row):
    width = row.shape[1]
    wide = jnp.broadcast_to(row, (BLK, width)).astype(BF16)
    ids = iota((BLK, width), 0, BF16)
    return jnp.where(ids == wide, jnp.ones((BLK, width), BF16), jnp.zeros((BLK, width), BF16))


def sort_slots(values16, high_low, column, target, spot, first, count):
    width = target.shape[1]
    chosen = jnp.broadcast_to(target, (16, width)).astype(BF16)
    zero = jnp.zeros((16, width), BF16)
    parts = [jnp.where(chosen == jnp.array(first + d, BF16), values16, zero) for d in range(count)]
    mine = iota((count, width), 0) + float(first) == target
    codes = jnp.concatenate([jnp.where(mine, high_low, 0.0), jnp.where(mine, column, 0.0)], axis=0)
    weighted = jnp.concatenate(parts + [codes.astype(BF16)], axis=0)
    return lax.dot_general(weighted, spot, NT, preferred_element_type=F32)


def two_parts(values):
    high = values.astype(BF16).astype(F32)
    return jnp.concatenate([high, values - high], axis=0).astype(BF16)


def stencil(centre, before, after, diffusivity, wind):
    shape = (BINS, LEV, GY)
    lane = lax.broadcasted_iota(I32, (ROWS, GY), 1)
    left = jnp.where(lane == 0, 0.0, pltpu.roll(centre, 1, 1))
    right = jnp.where(lane == GY - 1, 0.0, pltpu.roll(centre, GY - 1, 1))
    laplace = (after + before + right + left - 4.0 * centre).reshape(shape)
    drift = (centre - before).reshape(shape)
    result = centre.reshape(shape) + diffusivity[None] * laplace - wind[None] * drift
    return result.reshape(ROWS, GY)


def at_edges(me, upward, downward, action):
    @pl.when(me < N_XY - 1)
    def _():
        for copy in upward:
            copy.start() if action == "start" else copy.wait_send()
        for copy in downward if action == "wait" else []:
            copy.wait_recv()

    @pl.when(me > 0)
    def _():
        for copy in downward:
            copy.start() if action == "start" else copy.wait_send()
        for copy in upward if action == "wait" else []:
            copy.wait_recv()


def plane_copies(source, target, sems, at=0):
    return [pltpu.make_async_copy(source.at[:, x, :], target.at[at + x], sems.at[x]) for x in range(GX)]


def remote(src, dst, send, recv, device):
    return pltpu.make_async_remote_copy(
        src_ref=src, dst_ref=dst, send_sem=send, recv_sem=recv, device_id=device, device_id_type=MESH
    )


def compose(inv, low, up, triple, p_ref, e_ref):
    lane16 = lax.broadcasted_iota(I32, (16, ROWS), 1) % LEV
    row16 = lax.broadcasted_iota(I32, (16, ROWS), 0)
    own = lax.broadcasted_iota(I32, (BINS, 16, ROWS), 0) == (
        lax.broadcasted_iota(I32, (BINS, 16, ROWS), 2) // LEV
    )

    def spread(group):
        place = (lane16 == row16 + 16 * group).astype(F32)
        flat = inv[group].reshape(BINS * 16, 16)
        full = jnp.dot(flat, place, precision=lax.Precision.HIGHEST, preferred_element_type=F32)
        return jnp.where(own, full.reshape(BINS, 16, ROWS), 0.0)

    def per_bin(ref, group):
        wide = jnp.broadcast_to(ref[group : group + 1, :].reshape(1, 1, BINS), (BINS, 1, BINS))
        same = lax.broadcasted_iota(I32, (BINS, 1, BINS), 0) == lax.broadcasted_iota(
            I32, (BINS, 1, BINS), 2
        )
        return jnp.sum(jnp.where(same, wide, 0.0), axis=2, keepdims=True)

    t0, t1 = spread(0), spread(1)
    l0, l1, u0, u1 = per_bin(low, 0), per_bin(low, 1), per_bin(up, 0), per_bin(up, 1)
    m0, m1 = inv[0], inv[1]
    m0_first, m0_last = m0[:, :, 0:1], m0[:, :, 15:16]
    m1_first, m1_last = m1[:, :, 0:1], m1[:, :, 15:16]
    tail0 = t0[:, 15:16, :]
    link = (l1 * m1[:, 0:1, 0:1]) * tail0 + t1[:, 0:1, :]
    p0 = t0 + (u0 * m0_last) * link
    p1 = t1 + (l1 * m1_first) * tail0
    full = jnp.concatenate([p0, p1], axis=1).reshape(ROWS, ROWS)
    high = full.astype(BF16)
    triple[:, 0:ROWS] = high
    triple[:, ROWS : 2 * ROWS] = high
    triple[:, 2 * ROWS :] = (full - high.astype(F32)).astype(BF16)
    passed = l1 * l0 * m0[:, 15:16, 0:1]
    c0 = l0 * m0_first + (u0 * m0_last) * (passed * m1[:, 0:1, 0:1])
    c1 = passed * m1_first
    d0 = (u0 * u1 * m1[:, 0:1, 15:16]) * m0_last
    d1 = u1 * m1_last
    p_ref[...] = jnp.broadcast_to(jnp.concatenate([c0, c1], axis=1), (BINS, LEV, 128)).reshape(ROWS, 128)
    e_ref[...] = jnp.broadcast_to(jnp.concatenate([d0, d1], axis=1), (BINS, LEV, 128)).reshape(ROWS, 128)
    blocks = full.reshape(BINS, LEV, ROWS)
    eye = lax.broadcasted_iota(I32, (ROWS, ROWS), 0) == lax.broadcasted_iota(I32, (ROWS, ROWS), 1)
    across = [jnp.sum(jnp.where(eye, lanes([ref[...], ref[...]]), 0.0), axis=0, keepdims=True) for ref in (p_ref, e_ref)]
    rows = jnp.concatenate([blocks[:, at, :] * col for at in (LEV - 1, 0) for col in across], axis=0)
    fold = (
        lax.broadcasted_iota(I32, (ROWS, LEV), 0) % LEV == lax.broadcasted_iota(I32, (ROWS, LEV), 1)
    ).astype(F32)
    return jnp.dot(rows, fold, precision=lax.Precision.HIGHEST, preferred_element_type=F32)


def carry_factors(level, all_ref, out_ref):
    alpha = [all_ref[f, 0] for f in range(N_LEV)]
    beta = [all_ref[f, 1] for f in range(N_LEV)]
    gamma = [all_ref[f, 2] for f in range(N_LEV)]
    zero, one = jnp.zeros((BINS, 128), F32), jnp.ones((BINS, 128), F32)
    for f in range(N_LEV):
        down, product = zero, one
        for i in range(f + 1, N_LEV):
            down = jnp.where(level == i, product, down)
            product = product * alpha[i]
        upward, product = zero, one
        for i in range(f - 1, -1, -1):
            upward = jnp.where(level == i, product, upward)
            product = product * beta[i]
        out_ref[f] = down
        out_ref[N_LEV + f] = upward
    sigma = [zero] * N_LEV
    for f in range(N_LEV - 1, 0, -1):
        sigma[f - 1] = gamma[f] + beta[f] * alpha[f] * sigma[f]

    def own(values):
        result = values[0]
        for f in range(1, N_LEV):
            result = jnp.where(level == f, values[f], result)
        return result

    out_ref[8] = own(sigma)
    out_ref[9] = own([sigma[f] * alpha[f] for f in range(N_LEV)])
    out_ref[10] = own([sigma[f] * beta[f] for f in range(N_LEV)])


def route_kernel(
    euler, mass, dest, cell, diffusivity, wind, inv, low, up,
    first, rows_u, hl_u, col_u, starts_v, triple, p_col, e_col, factors, kept, turned,
    got_mass, got_code, order, hp_s, lp_s, hl_s, col_s, ext, diff_s, wind_s, mass_s, dest_in, cell_in, inv_s, low_s, up_s,
    send_mass, send_code, spare, spot_s, links,
    load_sem, small_sem, halo_send, halo_recv, mass_send, mass_recv, code_send, code_recv, link_send, link_recv,
):
    me, level = lax.axis_index("xy"), lax.axis_index("lev")
    barrier = pltpu.get_barrier_semaphore()

    def greet(k, unused):
        pl.semaphore_signal(
            barrier, inc=1, device_id={"xy": lax.rem(me + k, N_XY), "lev": level}, device_id_type=MESH
        )
        return unused

    lax.fori_loop(1, N_XY, greet, 0)
    for k in range(1, N_LEV):
        pl.semaphore_signal(
            barrier, inc=1, device_id={"xy": me, "lev": lax.rem(level + k, N_LEV)}, device_id_type=MESH
        )

    small = [
        pltpu.make_async_copy(source, target, small_sem.at[i])
        for i, (source, target) in enumerate(
            [(dest, dest_in), (cell, cell_in), (mass, mass_s), (inv, inv_s), (low, low_s), (up, up_s)]
        )
    ]
    field = plane_copies(euler, ext, load_sem.at[0], 1)
    coefficients = plane_copies(diffusivity, diff_s, load_sem.at[1]) + plane_copies(wind, wind_s, load_sem.at[2])
    for copy in small[:3]:
        copy.start()

    above, below = lax.rem(me + 1, N_XY), lax.rem(me + N_XY - 1, N_XY)
    up_copy = remote(euler.at[:, GX - 1, :], ext.at[0], halo_send.at[0], halo_recv.at[0], {"xy": above, "lev": level})
    down_copy = remote(euler.at[:, 0, :], ext.at[GX + 1], halo_send.at[1], halo_recv.at[1], {"xy": below, "lev": level})
    def wide(ref):
        return lanes([ref[pl.ds(0, 16, stride=2), :], ref[pl.ds(1, 16, stride=2), :]])

    def flat(rows):
        return lanes([rows[i : i + 1] for i in range(16)])

    for copy in small[:3]:
        copy.wait()
    target = wide(dest_in).astype(F32)
    cells = wide(cell_in)
    levels = cells // (GX * GY)
    bucket = (cells // GY) % GX * 2 + levels // 16
    high_low = flat((bucket * 16 + levels % 16 + 1).astype(F32))
    column = flat((cells % GY).astype(F32))
    r, c = (lax.broadcasted_iota(I32, (512, 512), d) for d in (0, 1))
    lower = jnp.where((c < r) & (c // 16 == r // 16), 1.0, 0.0).astype(BF16)
    slot, unused_base = ranks(target, N_XY, lower)
    for copy in small[3:] + field + coefficients:
        copy.start()
    spot_s[...] = one_hot(flat(slot))
    values = two_parts(mass_s[...])
    flat_target = flat(target)

    def mass_copy(other):
        device = {"xy": other, "lev": level}
        return remote(send_mass.at[other], got_mass.at[me], mass_send, mass_recv, device)

    def code_copy(other):
        source, target = send_code.at[pl.ds(other, 1)], got_code.at[pl.ds(me, 1)]
        return remote(source, target, code_send, code_recv, {"xy": other, "lev": level})

    table = sort_slots(values, high_low, column, flat_target, spot_s[...], 0, N_XY)
    masses = table[: 16 * N_XY].reshape(N_XY, 16, CAP)
    send_mass[...] = masses[:, :8] + masses[:, 8:]
    send_code[...] = table[16 * N_XY : 17 * N_XY] * 256.0 + table[17 * N_XY :]
    pl.semaphore_wait(barrier, N_XY - 1 + N_LEV - 1)

    def send(k, unused):
        other = lax.rem(me + k, N_XY)
        mass_copy(other).start()
        code_copy(other).start()
        return unused

    lax.fori_loop(1, N_XY, send, 0)
    at_edges(me, [up_copy], [down_copy], "start")
    got_mass[me] = send_mass[me]
    pltpu.make_async_copy(send_code.at[pl.ds(me, 1)], got_code.at[pl.ds(me, 1)], code_recv).start()
    pltpu.make_async_copy(send_code.at[pl.ds(me, 1)], spare, code_send).start()

    for copy in small[3:]:
        copy.wait()
    edge_matrix = compose(inv_s, low_s, up_s, triple, p_col, e_col)
    r, c = (lax.broadcasted_iota(I32, (N_XY * (BUCKETS + 1), N_XY * BUCKETS), d) for d in (0, 1))
    order[...] = jnp.where((c < r) & (c % N_XY // SRC == r % N_XY // SRC), 1.0, 0.0).astype(BF16)
    links[level, 0] = p_col[pl.ds(LEV - 1, BINS, stride=LEV), :]
    links[level, 1] = e_col[pl.ds(0, BINS, stride=LEV), :]
    links[level, 2] = p_col[pl.ds(0, BINS, stride=LEV), :]

    def link_copy(k, owner):
        peer = lax.rem(level + k, N_LEV)
        return remote(
            links.at[owner], links.at[owner], link_send.at[k], link_recv.at[k], {"xy": me, "lev": peer}
        )

    for k in range(1, N_LEV):
        link_copy(k, level).start()

    for copy in field + coefficients:
        copy.wait()

    def step(x, unused):
        first[x] = stencil(ext[x + 1], ext[x], ext[x + 2], diff_s[x], wind_s[x])
        return unused

    lax.fori_loop(1, GX - 1, step, 0)

    kept[...] = jnp.broadcast_to(jnp.sum(edge_matrix, axis=1, keepdims=True), (4 * BINS, 128)).reshape(4, BINS, 128)
    high = edge_matrix.astype(BF16)
    low = (edge_matrix - high.astype(F32)).astype(BF16)
    three_parts = lanes([high, high, low])

    def turn(x, unused):
        for i, ref in enumerate((diff_s, wind_s)):
            top = ref[x].astype(BF16)
            rest = (ref[x] - top.astype(F32)).astype(BF16)
            result = jnp.dot(three_parts, jnp.concatenate([top, rest, top], axis=0), preferred_element_type=F32)
            turned[i, x] = result.reshape(4, BINS, GY)
        return unused

    lax.fori_loop(0, GX, turn, 0, unroll=2)
    for k in range(1, N_LEV):
        link_copy(k, lax.rem(level + N_LEV - k, N_LEV)).wait()
    carry_factors(level, links, factors)

    remote(send_code, got_code, code_send, code_recv, {"xy": above, "lev": level}).wait()
    code = got_code[...].astype(I32)
    hl = code // 256
    col = code % 256
    valid = hl > 0
    key = jnp.where(valid, (hl - 1) // 16, -1).astype(F32)
    hl_s[...] = hl.astype(F32)
    col_s[...] = col.astype(F32)
    position, base = ranks(key, BUCKETS, order[...])
    place = position.astype(I32)
    hp_s[...] = jnp.where(valid, place // BLK, -1).astype(F32)
    lp_s[...] = (place % BLK).astype(F32)
    lane = lax.broadcasted_iota(I32, (1, 128), 1)
    longest = jnp.zeros((1, 128), I32)
    before = None
    for k in range(BUCKETS + 1):
        start = jnp.zeros((1, 128), F32)
        for g in range(SETS):
            at = N_XY * k + SRC * g
            start = jnp.where(lane == g, base[at : at + 1, :], start)
        start = start.astype(I32)
        starts_v[k : k + 1, :] = start
        if k:
            longest = jnp.maximum(longest, start - before // 128 * 128)
        before = start
    starts_v[BUCKETS + 1 : BUCKETS + 2, :] = longest

    others = pl.ds(0, N_XY - 1)
    remote(send_mass.at[others], got_mass.at[others], mass_send, mass_recv, {"xy": above, "lev": level}).wait()

    def one_set(g, unused):
        take = lambda ref: lanes([ref[pl.ds(g * SRC + i, 1), :] for i in range(SRC)])
        values = lanes([two_parts(got_mass[g * SRC + i]) for i in range(SRC)])
        table = sort_slots(values, take(hl_s), take(col_s), take(hp_s), one_hot(take(lp_s)), 0, SRC)
        for half in range(2):
            side = slice(128 * half, 128 * half + 128)
            for d in range(SRC):
                rows_u[g, 2 * d + half] = table[16 * d : 16 * d + 16, side]
            hl_u[g, pl.ds(half, SRC, stride=2), :] = table[16 * SRC : 17 * SRC, side]
            col_u[g, pl.ds(half, SRC, stride=2), :] = table[17 * SRC : 18 * SRC, side]
        rows_u[g, UNITS:] = jnp.zeros((WIN, 16, 128), F32)
        hl_u[g, UNITS:, :] = jnp.zeros((8, 128), F32)
        col_u[g, UNITS:, :] = jnp.zeros((8, 128), F32)
        return unused

    lax.fori_loop(0, SETS, one_set, 0)
    at_edges(me, [up_copy], [down_copy], "wait")

    @pl.when(me == 0)
    def _():
        ext[0] = jnp.zeros((ROWS, GY), F32)

    @pl.when(me == N_XY - 1)
    def _():
        ext[GX + 1] = jnp.zeros((ROWS, GY), F32)

    lax.fori_loop(0, 2, lambda i, u: step(i * (GX - 1), u), 0)


def deposit_kernel(starts_v, rows_u, hl_u, col_u, total, starts_s, sem):
    to_scalars = pltpu.make_async_copy(starts_v, starts_s, sem)
    to_scalars.start()
    to_scalars.wait()

    def place_of(k):
        return k // 2, pl.ds(pl.multiple_of((k % 2) * 16, 16), 16)

    def window(k, t):
        first_code = (k * 16 + 1).astype(F32)
        at = [jnp.minimum(starts_s[k, g] // 128 + WIN * t, UNITS) for g in range(SETS)]
        units = [(g, at[g] + i) for g in range(SETS) for i in range(WIN)]
        hl_row = lanes([hl_u[g, pl.ds(u, 1), :] for g, u in units])
        col_row = lanes([col_u[g, pl.ds(u, 1), :] for g, u in units])
        rows = lanes([rows_u[g, u] for g, u in units])
        width = 128 * WIN * SETS
        mine = jnp.broadcast_to(hl_row, (16, width)) == iota((16, width), 0) + first_code
        spread = [jnp.where(mine, jnp.broadcast_to(rows[q : q + 1, :], (16, width)), 0.0) for q in range(16)]
        spread.insert(8, jnp.where(mine, 1.0, 0.0))
        weighted = jnp.concatenate(spread, axis=0).astype(BF16)
        table = lax.dot_general(weighted, one_hot(col_row), NT, preferred_element_type=F32)
        table = table.reshape(17, 16, GY)
        return jnp.concatenate([table[:8] + table[9:], table[8:9]], axis=0)

    def one_bucket(k, unused):
        x, levels = place_of(k)
        total[x, :, levels, :] = window(k, 0)
        return unused

    lax.fori_loop(0, BUCKETS, one_bucket, 0, unroll=16)

    def rest(k, unused):
        x, levels = place_of(k)
        rounds = jnp.int32(1)
        for g in range(SETS):
            span = starts_s[k + 1, g] - starts_s[k, g] // 128 * 128
            rounds = jnp.maximum(rounds, (span + 128 * WIN - 1) // (128 * WIN))

        def again(t, unused):
            total[x, :, levels, :] += window(k, t)
            return unused

        lax.fori_loop(1, rounds, again, 0)
        return unused

    most = starts_s[BUCKETS + 1, 0]
    for g in range(1, SETS):
        most = jnp.maximum(most, starts_s[BUCKETS + 1, g])

    @pl.when(most > 128 * WIN)
    def _():
        lax.fori_loop(0, BUCKETS, rest, 0)


def correction(values, down, upward, p_col, e_col):
    shape = (BINS, LEV, GY)
    p_wide = lanes([p_col[...], p_col[...]]).reshape(shape)
    e_wide = lanes([e_col[...], e_col[...]]).reshape(shape)
    result = values.reshape(shape) + p_wide * down[:, None, :] + e_wide * upward[:, None, :]
    return result.reshape(ROWS, GY)


PARTS = (((0, 3), (3, 2), (5, 3)), ((0, 2), (2, 3), (5, 3)))
PLACE = (0, 2, 3, 4, 5, 6, 7, 1)


def solve_kernel(
    total, first, diffusivity, wind, triple, p_col, e_col, factors, kept, turned,
    second, down_out, up_out,
    ext, fixed, diff_s, wind_s, sum_s, beside, edge, seen, seen_halo, edge_w, edge2, seen2, edge3, seen_halo2, carry,
    load_sem, lev_send, lev_recv, diag_send, diag_recv, halo_send, halo_recv, side_send, side_recv,
):
    me, level = lax.axis_index("xy"), lax.axis_index("lev")
    above, below = lax.rem(me + 1, N_XY), lax.rem(me + N_XY - 1, N_XY)
    barrier = pltpu.get_barrier_semaphore()

    def greet(where, least):
        for k in range(least, N_LEV):
            device = {"xy": where, "lev": lax.rem(level + k, N_LEV)}
            pl.semaphore_signal(barrier, inc=1, device_id=device, device_id_type=MESH)

    greet(me, 1)
    pl.when(me < N_XY - 1)(lambda: greet(above, 0))
    pl.when(me > 0)(lambda: greet(below, 0))
    sides = jnp.where(me < N_XY - 1, 1, 0) + jnp.where(me > 0, 1, 0)
    loads = plane_copies(diffusivity, diff_s, load_sem.at[0]) + plane_copies(wind, wind_s, load_sem.at[1])
    for copy in loads:
        copy.start()
    def product(values):
        high = values.astype(BF16)
        low = (values - high.astype(F32)).astype(BF16)
        return jnp.dot(triple[...], jnp.concatenate([high, low, high], axis=0), preferred_element_type=F32)

    def both(i):
        return lanes([factors[i], factors[i]])

    def edges(values, target, place):
        blocks = values.reshape(BINS, LEV, GY)
        last, start = blocks[:, LEV - 1, :], blocks[:, 0, :]
        target[0, place] = last
        target[1, place] = start + both(10) * last

    def carries(tail, seen_at):
        down = jnp.zeros((BINS, GY), F32)
        upward = jnp.zeros((BINS, GY), F32)
        for f in range(N_LEV):
            here = jnp.where(level == f, 0.0, seen_at(f))
            down += both(f) * here
            upward += both(N_LEV + f) * here
        return down, upward + both(8) * tail + both(9) * down

    def tail_of(values):
        return values.reshape(BINS, LEV, GY)[:, LEV - 1, :]

    def peer_of(k):
        return lax.rem(level + k, N_LEV)

    def back(k):
        return lax.rem(level + N_LEV - k, N_LEV)

    def kind(k):
        return jnp.where(peer_of(k) > level, 0, 1)

    def lev_copies(turn, part, own):
        source, target = ((edge, seen), (edge2, seen2))[turn]
        span = pl.ds(*PARTS[turn][part])
        return [
            remote(
                source.at[kind(k), span], target.at[level if own else back(k), span],
                lev_send.at[turn, part, k], lev_recv.at[turn, part, k], {"xy": me, "lev": peer_of(k)},
            )
            for k in range(1, N_LEV)
        ]

    def diag_copies(turn, own):
        source, target = ((edge, seen_halo), (edge3, seen_halo2))[turn]
        return [
            remote(
                source.at[kind(k) if k else 0, ((GX - 1, 0), (1, 0))[turn][side]], target.at[side, level if own else back(k)],
                diag_send.at[turn, side, k], diag_recv.at[turn, side, k], {"xy": where, "lev": peer_of(k)},
            )
            for side, where in enumerate((above, below))
            for k in range(turn, N_LEV)
        ]

    def start(copies):
        for copy in copies:
            copy.start()

    def wait(copies):
        for copy in copies:
            copy.wait()

    def solve_plane(x, place):
        counts = total[x, BINS]
        share = counts / (counts + 2.0)
        old = first[x].reshape(BINS, LEV, GY)
        blended = (1.0 - share)[None] * old + share[None] * total[x, 0:BINS]
        solved = product(blended.reshape(ROWS, GY))
        ext[x + 1] = solved
        edges(solved, edge, place)

    def some(function, begin, count, shift):
        def one(i, unused):
            function(i, i + shift)
            return unused

        lax.fori_loop(begin, begin + count, one, 0, unroll=count)

    some(solve_plane, 0, 3, 0)
    some(solve_plane, 3, 2, 0)
    some(solve_plane, 5, 3, 0)
    wait(loads)
    sum_s[...] = diff_s[0] + wind_s[0]
    pl.semaphore_wait(barrier, N_LEV - 1 + N_LEV * sides)
    halos = [
        remote(ext.at[GX], ext.at[0], halo_send.at[0], halo_recv.at[0], {"xy": above, "lev": level}),
        remote(ext.at[1], ext.at[GX + 1], halo_send.at[1], halo_recv.at[1], {"xy": below, "lev": level}),
    ]
    weights = [
        remote(diff_s.at[GX - 1], beside.at[0], side_send.at[0], side_recv.at[0], {"xy": above, "lev": level}),
        remote(sum_s, beside.at[1], side_send.at[1], side_recv.at[1], {"xy": below, "lev": level}),
    ]
    sent, seen_in = diag_copies(0, True), diag_copies(0, False)
    sent2, seen_in2 = diag_copies(1, True), diag_copies(1, False)
    three = N_LEV - 1
    for part in range(3):
        start(lev_copies(0, part, True))
    at_edges(me, sent[:N_LEV], sent[N_LEV:], "start")
    at_edges(me, weights[:1], weights[1:], "start")
    at_edges(me, halos[:1], halos[1:], "start")

    def early_plane(x, before, after):
        edges(product(stencil(ext[x + 1], before, after, diff_s[x], wind_s[x])), edge_w, x)

    nothing = jnp.zeros((ROWS, GY), F32)
    early_plane(0, nothing, ext[2])
    some(lambda x, place: early_plane(x, ext[x], ext[x + 2]), 1, 3, 0)
    some(lambda x, place: early_plane(x, ext[x], ext[x + 2]), 4, 3, 0)
    early_plane(GX - 1, ext[GX - 1], nothing)

    def scaled(plane, values):
        return (plane[None] * values.reshape(BINS, LEV, GY)).reshape(ROWS, GY)

    def share_up():
        edges(product(scaled(beside[1], ext[GX])), edge3, 1)
        start(sent2[:three])

    def share_down():
        edges(product(scaled(beside[0], ext[1])), edge3, 0)
        start(sent2[three:])

    at_edges(me, weights[:1], weights[1:], "wait")
    pl.when(me < N_XY - 1)(share_up)
    pl.when(me > 0)(share_down)

    def keep_carries(at, found):
        carry[0, at] = found[0]
        carry[1, at] = found[1]

    def halo_carries(side):
        keep_carries(side * (GX + 1), carries(seen_halo[side, level], lambda f: seen_halo[side, f]))

    def no_carries(side):
        keep_carries(side * (GX + 1), (jnp.zeros((BINS, GY), F32),) * 2)

    def plane_carries(begin, end):
        for x in range(begin, end):
            keep_carries(x + 1, carries(edge[0, x], lambda f: seen[f, x]))

    lane = lax.broadcasted_iota(I32, (BINS, GY), 1)

    def late_edges(x):
        added = [jnp.zeros((BINS, GY), F32)] * 2
        for v in range(2):
            here, before = carry[v, x + 1], carry[v, x]
            left = jnp.where(lane == 0, 0.0, pltpu.roll(here, 1, 1))
            right = jnp.where(lane == GY - 1, 0.0, pltpu.roll(here, GY - 1, 1))
            laplace = carry[v, x + 2] + before + right + left - 4.0 * here
            drift = here - before
            for end in range(2):
                i = 2 * end + v
                keep = lanes([kept[i], kept[i]])
                added[end] += keep * here + turned[0, x, i] * laplace - turned[1, x, i] * drift
        edge2[0, PLACE[x]] = edge_w[0, x] + added[0]
        edge2[1, PLACE[x]] = edge_w[1, x] + added[1] + both(10) * added[0]

    wait(lev_copies(0, 0, False) + lev_copies(0, 1, False))
    plane_carries(0, 5)
    for x in range(1, 4):
        late_edges(x)
    start(lev_copies(1, 1, True))
    wait(lev_copies(0, 2, False))
    plane_carries(5, GX)
    for x in range(4, GX - 1):
        late_edges(x)
    start(lev_copies(1, 2, True))
    at_edges(me, seen_in[:N_LEV], seen_in[N_LEV:], "wait")
    pl.when(me > 0)(lambda: halo_carries(0))
    pl.when(me < N_XY - 1)(lambda: halo_carries(1))
    pl.when(me == 0)(lambda: no_carries(0))
    pl.when(me == N_XY - 1)(lambda: no_carries(1))
    late_edges(0)
    late_edges(GX - 1)
    start(lev_copies(1, 0, True))

    def correct_plane(at, unused):
        fixed[at] = correction(ext[at], carry[0, at], carry[1, at], p_col, e_col)

    def second_plane(x, unused):
        second[x] = product(stencil(fixed[x + 1], fixed[x], fixed[x + 2], diff_s[x], wind_s[x]))

    def no_plane(at):
        fixed[at] = nothing

    some(correct_plane, 1, 4, 0)
    some(correct_plane, 5, 4, 0)
    some(second_plane, 1, 3, 0)
    some(second_plane, 4, 3, 0)
    at_edges(me, halos[:1], halos[1:], "wait")
    pl.when(me > 0)(lambda: correct_plane(0, 0))
    pl.when(me < N_XY - 1)(lambda: correct_plane(GX + 1, 0))
    pl.when(me == 0)(lambda: no_plane(0))
    pl.when(me == N_XY - 1)(lambda: no_plane(GX + 1))
    second_plane(0, 0)
    second_plane(GX - 1, 0)
    at_edges(me, seen_in2[:three], seen_in2[three:], "wait")

    def no_share(side):
        seen_halo2[side] = jnp.zeros((N_LEV, BINS, GY), F32)

    pl.when(me == 0)(lambda: no_share(0))
    pl.when(me == N_XY - 1)(lambda: no_share(1))

    def seen_at(x):
        if x == 0:
            return lambda f: seen2[f, 0] + seen_halo2[0, f]
        if x == GX - 1:
            return lambda f: seen2[f, 1] + seen_halo2[1, f]
        return lambda f: seen2[f, PLACE[x]]

    wait(lev_copies(1, 1, False))
    for x in range(1, 4):
        down, upward = carries(tail_of(second[x]), seen_at(x))
        second[x] = correction(second[x], down, upward, p_col, e_col)
    wait(lev_copies(1, 2, False) + lev_copies(1, 0, False))
    for i, x in enumerate(LATE):
        down, upward = carries(tail_of(second[x]), seen_at(x))
        down_out[i] = down
        up_out[i] = upward


LATE = (4, 5, 6, 0, 7)


def finish_kernel(second, down, upward, p_col, e_col, out, outer, sem):
    inner = [pltpu.make_async_copy(second.at[x], out.at[:, x, :], sem.at[x]) for x in range(1, 4)]
    for copy in inner:
        copy.start()
    last = []
    for i, x in enumerate(LATE):
        outer[i] = correction(second[x], down[i], upward[i], p_col, e_col)
        last.append(pltpu.make_async_copy(outer.at[i], out.at[:, x, :], sem.at[x]))
        last[i].start()
    for copy in inner + last:
        copy.wait()


def vmem(*shape, dtype=F32):
    return pltpu.VMEM(shape, dtype)


def whole(count):
    return [pl.BlockSpec(memory_space=pltpu.VMEM)] * count


def somewhere(count):
    return [pl.BlockSpec(memory_space=pltpu.HBM)] * count


def shaped(*shape, dtype=F32):
    return jax.ShapeDtypeStruct(shape, dtype)


def shards(
    euler_field, parcel_mass, dest_device, dest_cell, diffusivity, wind_speed, inverses, lower_coupling, upper_coupling
):
    dma = pltpu.SemaphoreType.DMA
    euler, mass, dest, cell, diffusivity, wind, inv, low, up = [
        pltpu.with_memory_space_constraint(array, pltpu.HBM)
        for array in (
            euler_field.reshape(ROWS, GX, GY), parcel_mass, dest_device.reshape(32, 128), dest_cell.reshape(32, 128),
            diffusivity, wind_speed, inverses, lower_coupling, upper_coupling,
        )
    ]
    routed = pl.pallas_call(
        route_kernel,
        name="route",
        out_shape=[
            shaped(GX, ROWS, GY), shaped(SETS, UNITS + WIN, 16, 128), shaped(SETS, UNITS + 8, 128),
            shaped(SETS, UNITS + 8, 128), shaped(BUCKETS + 8, 128, dtype=I32), shaped(ROWS, 3 * ROWS, dtype=BF16),
            shaped(ROWS, 128), shaped(ROWS, 128), shaped(11, BINS, 128),
            shaped(4, BINS, 128), shaped(2, GX, 4, BINS, GY),
        ],
        in_specs=somewhere(9),
        out_specs=whole(11),
        scratch_shapes=[
            vmem(N_XY, BINS, CAP), vmem(N_XY, CAP), vmem(N_XY * (BUCKETS + 1), N_XY * BUCKETS, dtype=BF16),
            vmem(N_XY, BLK), vmem(N_XY, BLK), vmem(N_XY, BLK), vmem(N_XY, BLK),
            vmem(GX + 2, ROWS, GY), vmem(GX, LEV, GY), vmem(GX, LEV, GY),
            vmem(BINS, PARC), vmem(32, 128, dtype=I32), vmem(32, 128, dtype=I32),
            vmem(2, BINS, 16, 16), vmem(2, BINS), vmem(2, BINS),
            vmem(N_XY, BINS, CAP), vmem(N_XY, CAP), vmem(1, CAP), vmem(CAP, PARC, dtype=BF16), vmem(N_LEV, 3, BINS, 128),
            dma((3, GX)), dma((6,)), dma((2,)), dma((2,)), dma, dma, dma, dma,
            dma((N_LEV,)), dma((N_LEV,)),
        ],
        compiler_params=pltpu.CompilerParams(collective_id=0, has_side_effects=True, vmem_limit_bytes=LIMIT),
    )(euler, mass, dest, cell, diffusivity, wind, inv, low, up)
    first, rows_u, hl_u, col_u, starts, triple, p_col, e_col, factors, kept, turned = routed
    total = pl.pallas_call(
        deposit_kernel,
        name="deposit",
        out_shape=shaped(GX, BINS + 1, LEV, GY),
        in_specs=whole(4),
        out_specs=pl.BlockSpec(memory_space=pltpu.VMEM),
        scratch_shapes=[pltpu.SMEM((BUCKETS + 8, 128), I32), dma],
        compiler_params=pltpu.CompilerParams(vmem_limit_bytes=LIMIT),
    )(starts, rows_u, hl_u, col_u)
    second, down, upward = pl.pallas_call(
        solve_kernel,
        name="solve",
        out_shape=[shaped(GX, ROWS, GY), shaped(len(LATE), BINS, GY), shaped(len(LATE), BINS, GY)],
        in_specs=whole(2) + somewhere(2) + whole(6),
        out_specs=whole(3),
        scratch_shapes=[
            vmem(GX + 2, ROWS, GY), vmem(GX + 2, ROWS, GY),
            vmem(GX, LEV, GY), vmem(GX, LEV, GY), vmem(LEV, GY), vmem(2, LEV, GY),
            vmem(2, GX, BINS, GY), vmem(N_LEV, GX, BINS, GY), vmem(2, N_LEV, BINS, GY),
            vmem(2, GX, BINS, GY), vmem(2, GX, BINS, GY), vmem(N_LEV, GX, BINS, GY),
            vmem(2, 2, BINS, GY), vmem(2, N_LEV, BINS, GY), vmem(2, GX + 2, BINS, GY),
            dma((2, GX)), dma((2, 3, N_LEV)), dma((2, 3, N_LEV)), dma((2, 2, N_LEV)), dma((2, 2, N_LEV)),
            dma((2,)), dma((2,)), dma((2,)), dma((2,)),
        ],
        compiler_params=pltpu.CompilerParams(collective_id=1, has_side_effects=True, vmem_limit_bytes=LIMIT),
    )(total, first, diffusivity, wind, triple, p_col, e_col, factors, kept, turned)
    result = pl.pallas_call(
        finish_kernel,
        name="finish",
        out_shape=shaped(ROWS, GX, GY),
        in_specs=whole(5),
        out_specs=pl.BlockSpec(memory_space=pltpu.HBM),
        scratch_shapes=[vmem(len(LATE), ROWS, GY), dma((GX,))],
        compiler_params=pltpu.CompilerParams(vmem_limit_bytes=LIMIT),
    )(second, down, upward, p_col, e_col)
    return result.reshape(BINS, LEV, GX, GY)


def solution(mesh):
    placed = (
        P(None, "lev", "xy", None),
        P(None, ("xy", "lev")),
        P(("xy", "lev"), None),
        P(("xy", "lev")),
        P("lev", "xy", None),
        P("lev", "xy", None),
        P("lev", None, None, None),
        P("lev", None),
        P("lev", None),
    )
    return jax.shard_map(
        shards, mesh=mesh, in_specs=placed, out_specs=P(None, "lev", "xy", None), check_vma=False
    )
```

```python
import functools

import jax
import jax.numpy as jnp
from jax import lax
from jax.experimental import pallas as pl
from jax.experimental.pallas import tpu as pltpu
from jax.sharding import PartitionSpec as P

F32, BF16, I32 = jnp.float32, jnp.bfloat16, jnp.int32
MESH = pl.DeviceIdType.MESH
N_XY, N_LEV, BINS, LEV, GX, GY = 32, 4, 8, 32, 8, 256
ROWS = BINS * LEV
PARC, CAP, BLK = 4096, 256, 256
BUCKETS = 16
NT = (((1,), (1,)), ((), ()))
LIMIT = 24 << 20
SETS = 2
SRC = N_XY // SETS
SPAN = SRC * CAP
UNITS = SPAN // 128
WIN = 4


def iota(shape, dim, dtype=F32):
    return lax.broadcasted_iota(I32, shape, dim).astype(dtype)


def ranks(keys, count, lower):
    n = keys.shape[0]
    masks = [jnp.where(keys == k, 1.0, 0.0) for k in range(count)]
    stack = jnp.concatenate(masks, axis=0).astype(BF16)
    before = (iota((BLK, BLK), 0) < iota((BLK, BLK), 1)).astype(BF16)
    inside = jnp.dot(stack, before, preferred_element_type=F32)
    totals = jnp.dot(stack, jnp.ones((BLK, 128), BF16), preferred_element_type=F32)
    base = jnp.dot(lower, totals.astype(BF16), preferred_element_type=F32)
    wide = jnp.concatenate([base, base], axis=1)
    whole = inside + wide[: inside.shape[0]]
    position = jnp.zeros(keys.shape, F32)
    for k in range(count):
        position += masks[k] * whole[k * n : (k + 1) * n]
    return position, base


def lanes(pieces):
    return jnp.concatenate(pieces, axis=1)


def one_hot(row):
    width = row.shape[1]
    wide = jnp.broadcast_to(row, (BLK, width)).astype(BF16)
    ids = iota((BLK, width), 0, BF16)
    return jnp.where(ids == wide, jnp.ones((BLK, width), BF16), jnp.zeros((BLK, width), BF16))


def sort_slots(values16, high_low, column, target, spot, first, count):
    width = target.shape[1]
    chosen = jnp.broadcast_to(target, (16, width)).astype(BF16)
    zero = jnp.zeros((16, width), BF16)
    parts = [jnp.where(chosen == jnp.array(first + d, BF16), values16, zero) for d in range(count)]
    mine = iota((count, width), 0) + float(first) == target
    codes = jnp.concatenate([jnp.where(mine, high_low, 0.0), jnp.where(mine, column, 0.0)], axis=0)
    weighted = jnp.concatenate(parts + [codes.astype(BF16)], axis=0)
    return lax.dot_general(weighted, spot, NT, preferred_element_type=F32)


def two_parts(values):
    high = values.astype(BF16).astype(F32)
    return jnp.concatenate([high, values - high], axis=0).astype(BF16)


def stencil(centre, before, after, diffusivity, wind):
    shape = (BINS, LEV, GY)
    lane = lax.broadcasted_iota(I32, (ROWS, GY), 1)
    left = jnp.where(lane == 0, 0.0, pltpu.roll(centre, 1, 1))
    right = jnp.where(lane == GY - 1, 0.0, pltpu.roll(centre, GY - 1, 1))
    laplace = (after + before + right + left - 4.0 * centre).reshape(shape)
    drift = (centre - before).reshape(shape)
    result = centre.reshape(shape) + diffusivity[None] * laplace - wind[None] * drift
    return result.reshape(ROWS, GY)


def at_edges(me, upward, downward, action):
    @pl.when(me < N_XY - 1)
    def _():
        for copy in upward:
            copy.start() if action == "start" else copy.wait_send()
        for copy in downward if action == "wait" else []:
            copy.wait_recv()

    @pl.when(me > 0)
    def _():
        for copy in downward:
            copy.start() if action == "start" else copy.wait_send()
        for copy in upward if action == "wait" else []:
            copy.wait_recv()


def plane_copies(source, target, sems, at=0):
    return [pltpu.make_async_copy(source.at[:, x, :], target.at[at + x], sems.at[x]) for x in range(GX)]


def remote(src, dst, send, recv, device):
    return pltpu.make_async_remote_copy(
        src_ref=src, dst_ref=dst, send_sem=send, recv_sem=recv, device_id=device, device_id_type=MESH
    )


def compose(inv, low, up, triple, p_ref, e_ref):
    lane16 = lax.broadcasted_iota(I32, (16, ROWS), 1) % LEV
    row16 = lax.broadcasted_iota(I32, (16, ROWS), 0)
    own = lax.broadcasted_iota(I32, (BINS, 16, ROWS), 0) == (
        lax.broadcasted_iota(I32, (BINS, 16, ROWS), 2) // LEV
    )

    def spread(group):
        place = (lane16 == row16 + 16 * group).astype(F32)
        flat = inv[group].reshape(BINS * 16, 16)
        full = jnp.dot(flat, place, precision=lax.Precision.HIGHEST, preferred_element_type=F32)
        return jnp.where(own, full.reshape(BINS, 16, ROWS), 0.0)

    def per_bin(ref, group):
        wide = jnp.broadcast_to(ref[group : group + 1, :].reshape(1, 1, BINS), (BINS, 1, BINS))
        same = lax.broadcasted_iota(I32, (BINS, 1, BINS), 0) == lax.broadcasted_iota(
            I32, (BINS, 1, BINS), 2
        )
        return jnp.sum(jnp.where(same, wide, 0.0), axis=2, keepdims=True)

    t0, t1 = spread(0), spread(1)
    l0, l1, u0, u1 = per_bin(low, 0), per_bin(low, 1), per_bin(up, 0), per_bin(up, 1)
    m0, m1 = inv[0], inv[1]
    m0_first, m0_last = m0[:, :, 0:1], m0[:, :, 15:16]
    m1_first, m1_last = m1[:, :, 0:1], m1[:, :, 15:16]
    tail0 = t0[:, 15:16, :]
    link = (l1 * m1[:, 0:1, 0:1]) * tail0 + t1[:, 0:1, :]
    p0 = t0 + (u0 * m0_last) * link
    p1 = t1 + (l1 * m1_first) * tail0
    full = jnp.concatenate([p0, p1], axis=1).reshape(ROWS, ROWS)
    high = full.astype(BF16)
    triple[:, 0:ROWS] = high
    triple[:, ROWS : 2 * ROWS] = high
    triple[:, 2 * ROWS :] = (full - high.astype(F32)).astype(BF16)
    passed = l1 * l0 * m0[:, 15:16, 0:1]
    c0 = l0 * m0_first + (u0 * m0_last) * (passed * m1[:, 0:1, 0:1])
    c1 = passed * m1_first
    d0 = (u0 * u1 * m1[:, 0:1, 15:16]) * m0_last
    d1 = u1 * m1_last
    p_ref[...] = jnp.broadcast_to(jnp.concatenate([c0, c1], axis=1), (BINS, LEV, 128)).reshape(ROWS, 128)
    e_ref[...] = jnp.broadcast_to(jnp.concatenate([d0, d1], axis=1), (BINS, LEV, 128)).reshape(ROWS, 128)
    blocks = full.reshape(BINS, LEV, ROWS)
    eye = lax.broadcasted_iota(I32, (ROWS, ROWS), 0) == lax.broadcasted_iota(I32, (ROWS, ROWS), 1)
    across = [jnp.sum(jnp.where(eye, lanes([ref[...], ref[...]]), 0.0), axis=0, keepdims=True) for ref in (p_ref, e_ref)]
    rows = jnp.concatenate([blocks[:, at, :] * col for at in (LEV - 1, 0) for col in across], axis=0)
    fold = (
        lax.broadcasted_iota(I32, (ROWS, LEV), 0) % LEV == lax.broadcasted_iota(I32, (ROWS, LEV), 1)
    ).astype(F32)
    return jnp.dot(rows, fold, precision=lax.Precision.HIGHEST, preferred_element_type=F32)


def carry_factors(level, all_ref, out_ref):
    alpha = [all_ref[f, 0] for f in range(N_LEV)]
    beta = [all_ref[f, 1] for f in range(N_LEV)]
    gamma = [all_ref[f, 2] for f in range(N_LEV)]
    zero, one = jnp.zeros((BINS, 128), F32), jnp.ones((BINS, 128), F32)
    for f in range(N_LEV):
        down, product = zero, one
        for i in range(f + 1, N_LEV):
            down = jnp.where(level == i, product, down)
            product = product * alpha[i]
        upward, product = zero, one
        for i in range(f - 1, -1, -1):
            upward = jnp.where(level == i, product, upward)
            product = product * beta[i]
        out_ref[f] = down
        out_ref[N_LEV + f] = upward
    sigma = [zero] * N_LEV
    for f in range(N_LEV - 1, 0, -1):
        sigma[f - 1] = gamma[f] + beta[f] * alpha[f] * sigma[f]

    def own(values):
        result = values[0]
        for f in range(1, N_LEV):
            result = jnp.where(level == f, values[f], result)
        return result

    out_ref[8] = own(sigma)
    out_ref[9] = own([sigma[f] * alpha[f] for f in range(N_LEV)])
    out_ref[10] = own([sigma[f] * beta[f] for f in range(N_LEV)])


def route_kernel(
    euler, mass, dest, cell, diffusivity, wind, inv, low, up,
    first, rows_u, hl_u, col_u, starts_v, triple, p_col, e_col, factors, kept, turned,
    got_mass, got_code, order, hp_s, lp_s, hl_s, col_s, ext, diff_s, wind_s, mass_s, dest_in, cell_in, inv_s, low_s, up_s,
    send_mass, send_code, spare, spot_s, links,
    load_sem, small_sem, halo_send, halo_recv, mass_send, mass_recv, code_send, code_recv, link_send, link_recv,
):
    me, level = lax.axis_index("xy"), lax.axis_index("lev")
    barrier = pltpu.get_barrier_semaphore()

    def greet(k, unused):
        pl.semaphore_signal(
            barrier, inc=1, device_id={"xy": lax.rem(me + k, N_XY), "lev": level}, device_id_type=MESH
        )
        return unused

    lax.fori_loop(1, N_XY, greet, 0)
    for k in range(1, N_LEV):
        pl.semaphore_signal(
            barrier, inc=1, device_id={"xy": me, "lev": lax.rem(level + k, N_LEV)}, device_id_type=MESH
        )

    small = [
        pltpu.make_async_copy(source, target, small_sem.at[i])
        for i, (source, target) in enumerate(
            [(dest, dest_in), (cell, cell_in), (mass, mass_s), (inv, inv_s), (low, low_s), (up, up_s)]
        )
    ]
    field = plane_copies(euler, ext, load_sem.at[0], 1)
    coefficients = plane_copies(diffusivity, diff_s, load_sem.at[1]) + plane_copies(wind, wind_s, load_sem.at[2])
    for copy in small[:3]:
        copy.start()

    above, below = lax.rem(me + 1, N_XY), lax.rem(me + N_XY - 1, N_XY)
    up_copy = remote(euler.at[:, GX - 1, :], ext.at[0], halo_send.at[0], halo_recv.at[0], {"xy": above, "lev": level})
    down_copy = remote(euler.at[:, 0, :], ext.at[GX + 1], halo_send.at[1], halo_recv.at[1], {"xy": below, "lev": level})
    def wide(ref):
        return lanes([ref[pl.ds(0, 16, stride=2), :], ref[pl.ds(1, 16, stride=2), :]])

    def flat(rows):
        return lanes([rows[i : i + 1] for i in range(16)])

    for copy in small[:3]:
        copy.wait()
    target = wide(dest_in).astype(F32)
    cells = wide(cell_in)
    levels = cells // (GX * GY)
    bucket = (cells // GY) % GX * 2 + levels // 16
    high_low = flat((bucket * 16 + levels % 16 + 1).astype(F32))
    column = flat((cells % GY).astype(F32))
    r, c = (lax.broadcasted_iota(I32, (512, 512), d) for d in (0, 1))
    lower = jnp.where((c < r) & (c // 16 == r // 16), 1.0, 0.0).astype(BF16)
    slot, unused_base = ranks(target, N_XY, lower)
    for copy in small[3:] + field + coefficients:
        copy.start()
    spot_s[...] = one_hot(flat(slot))
    values = two_parts(mass_s[...])
    flat_target = flat(target)

    def mass_copy(other):
        device = {"xy": other, "lev": level}
        return remote(send_mass.at[other], got_mass.at[me], mass_send, mass_recv, device)

    def code_copy(other):
        source, target = send_code.at[pl.ds(other, 1)], got_code.at[pl.ds(me, 1)]
        return remote(source, target, code_send, code_recv, {"xy": other, "lev": level})

    table = sort_slots(values, high_low, column, flat_target, spot_s[...], 0, N_XY)
    masses = table[: 16 * N_XY].reshape(N_XY, 16, CAP)
    send_mass[...] = masses[:, :8] + masses[:, 8:]
    send_code[...] = table[16 * N_XY : 17 * N_XY] * 256.0 + table[17 * N_XY :]
    pl.semaphore_wait(barrier, N_XY - 1 + N_LEV - 1)

    def send(k, unused):
        other = lax.rem(me + k, N_XY)
        mass_copy(other).start()
        code_copy(other).start()
        return unused

    lax.fori_loop(1, N_XY, send, 0)
    at_edges(me, [up_copy], [down_copy], "start")
    got_mass[me] = send_mass[me]
    pltpu.make_async_copy(send_code.at[pl.ds(me, 1)], got_code.at[pl.ds(me, 1)], code_recv).start()
    pltpu.make_async_copy(send_code.at[pl.ds(me, 1)], spare, code_send).start()

    for copy in small[3:]:
        copy.wait()
    edge_matrix = compose(inv_s, low_s, up_s, triple, p_col, e_col)
    r, c = (lax.broadcasted_iota(I32, (N_XY * (BUCKETS + 1), N_XY * BUCKETS), d) for d in (0, 1))
    order[...] = jnp.where((c < r) & (c % N_XY // SRC == r % N_XY // SRC), 1.0, 0.0).astype(BF16)
    links[level, 0] = p_col[pl.ds(LEV - 1, BINS, stride=LEV), :]
    links[level, 1] = e_col[pl.ds(0, BINS, stride=LEV), :]
    links[level, 2] = p_col[pl.ds(0, BINS, stride=LEV), :]

    def link_copy(k, owner):
        peer = lax.rem(level + k, N_LEV)
        return remote(
            links.at[owner], links.at[owner], link_send.at[k], link_recv.at[k], {"xy": me, "lev": peer}
        )

    for k in range(1, N_LEV):
        link_copy(k, level).start()

    for copy in field + coefficients:
        copy.wait()

    def step(x, unused):
        first[x] = stencil(ext[x + 1], ext[x], ext[x + 2], diff_s[x], wind_s[x])
        return unused

    lax.fori_loop(1, GX - 1, step, 0)
    nothing = jnp.zeros((ROWS, GY), F32)
    first[0] = stencil(ext[1], nothing, ext[2], diff_s[0], wind_s[0])
    first[GX - 1] = stencil(ext[GX], ext[GX - 1], nothing, diff_s[GX - 1], wind_s[GX - 1])

    kept[...] = jnp.broadcast_to(jnp.sum(edge_matrix, axis=1, keepdims=True), (4 * BINS, 128)).reshape(4, BINS, 128)
    high = edge_matrix.astype(BF16)
    low = (edge_matrix - high.astype(F32)).astype(BF16)
    three_parts = lanes([high, high, low])

    def turn(x, unused):
        for i, ref in enumerate((diff_s, wind_s)):
            top = ref[x].astype(BF16)
            rest = (ref[x] - top.astype(F32)).astype(BF16)
            result = jnp.dot(three_parts, jnp.concatenate([top, rest, top], axis=0), preferred_element_type=F32)
            turned[i, x] = result.reshape(4, BINS, GY)
        return unused

    lax.fori_loop(0, GX, turn, 0, unroll=2)
    for k in range(1, N_LEV):
        link_copy(k, lax.rem(level + N_LEV - k, N_LEV)).wait()
    carry_factors(level, links, factors)

    remote(send_code, got_code, code_send, code_recv, {"xy": above, "lev": level}).wait()
    code = got_code[...].astype(I32)
    hl = code // 256
    col = code % 256
    valid = hl > 0
    key = jnp.where(valid, (hl - 1) // 16, -1).astype(F32)
    hl_s[...] = hl.astype(F32)
    col_s[...] = col.astype(F32)
    position, base = ranks(key, BUCKETS, order[...])
    place = position.astype(I32)
    hp_s[...] = jnp.where(valid, place // BLK, -1).astype(F32)
    lp_s[...] = (place % BLK).astype(F32)
    lane = lax.broadcasted_iota(I32, (1, 128), 1)
    longest = jnp.zeros((1, 128), I32)
    before = None
    for k in range(BUCKETS + 1):
        start = jnp.zeros((1, 128), F32)
        for g in range(SETS):
            at = N_XY * k + SRC * g
            start = jnp.where(lane == g, base[at : at + 1, :], start)
        start = start.astype(I32)
        starts_v[k : k + 1, :] = start
        if k:
            longest = jnp.maximum(longest, start - before // 128 * 128)
        before = start
    starts_v[BUCKETS + 1 : BUCKETS + 2, :] = longest

    others = pl.ds(0, N_XY - 1)
    remote(send_mass.at[others], got_mass.at[others], mass_send, mass_recv, {"xy": above, "lev": level}).wait()

    def one_set(g, unused):
        take = lambda ref: lanes([ref[pl.ds(g * SRC + i, 1), :] for i in range(SRC)])
        values = lanes([two_parts(got_mass[g * SRC + i]) for i in range(SRC)])
        table = sort_slots(values, take(hl_s), take(col_s), take(hp_s), one_hot(take(lp_s)), 0, SRC)
        for half in range(2):
            side = slice(128 * half, 128 * half + 128)
            for d in range(SRC):
                rows_u[g, 2 * d + half] = table[16 * d : 16 * d + 16, side]
            hl_u[g, pl.ds(half, SRC, stride=2), :] = table[16 * SRC : 17 * SRC, side]
            col_u[g, pl.ds(half, SRC, stride=2), :] = table[17 * SRC : 18 * SRC, side]
        rows_u[g, UNITS:] = jnp.zeros((WIN, 16, 128), F32)
        hl_u[g, UNITS:, :] = jnp.zeros((8, 128), F32)
        col_u[g, UNITS:, :] = jnp.zeros((8, 128), F32)
        return unused

    lax.fori_loop(0, SETS, one_set, 0)
    at_edges(me, [up_copy], [down_copy], "wait")

    def add_halo(x, at, weight):
        first[x] += (weight[None] * ext[at].reshape(BINS, LEV, GY)).reshape(ROWS, GY)

    pl.when(me > 0)(lambda: add_halo(0, 0, diff_s[0] + wind_s[0]))
    pl.when(me < N_XY - 1)(lambda: add_halo(GX - 1, GX + 1, diff_s[GX - 1]))


def deposit_kernel(starts_v, rows_u, hl_u, col_u, total, starts_s, sem):
    to_scalars = pltpu.make_async_copy(starts_v, starts_s, sem)
    to_scalars.start()
    to_scalars.wait()

    def place_of(k):
        return k // 2, pl.ds(pl.multiple_of((k % 2) * 16, 16), 16)

    def window(k, t):
        first_code = (k * 16 + 1).astype(F32)
        at = [jnp.minimum(starts_s[k, g] // 128 + WIN * t, UNITS) for g in range(SETS)]
        units = [(g, at[g] + i) for g in range(SETS) for i in range(WIN)]
        hl_row = lanes([hl_u[g, pl.ds(u, 1), :] for g, u in units])
        col_row = lanes([col_u[g, pl.ds(u, 1), :] for g, u in units])
        rows = lanes([rows_u[g, u] for g, u in units])
        width = 128 * WIN * SETS
        mine = jnp.broadcast_to(hl_row, (16, width)) == iota((16, width), 0) + first_code
        spread = [jnp.where(mine, jnp.broadcast_to(rows[q : q + 1, :], (16, width)), 0.0) for q in range(16)]
        spread.insert(8, jnp.where(mine, 1.0, 0.0))
        weighted = jnp.concatenate(spread, axis=0).astype(BF16)
        table = lax.dot_general(weighted, one_hot(col_row), NT, preferred_element_type=F32)
        table = table.reshape(17, 16, GY)
        return jnp.concatenate([table[:8] + table[9:], table[8:9]], axis=0)

    def one_bucket(k, unused):
        x, levels = place_of(k)
        total[x, :, levels, :] = window(k, 0)
        return unused

    lax.fori_loop(0, BUCKETS, one_bucket, 0, unroll=16)

    def rest(k, unused):
        x, levels = place_of(k)
        rounds = jnp.int32(1)
        for g in range(SETS):
            span = starts_s[k + 1, g] - starts_s[k, g] // 128 * 128
            rounds = jnp.maximum(rounds, (span + 128 * WIN - 1) // (128 * WIN))

        def again(t, unused):
            total[x, :, levels, :] += window(k, t)
            return unused

        lax.fori_loop(1, rounds, again, 0)
        return unused

    most = starts_s[BUCKETS + 1, 0]
    for g in range(1, SETS):
        most = jnp.maximum(most, starts_s[BUCKETS + 1, g])

    @pl.when(most > 128 * WIN)
    def _():
        lax.fori_loop(0, BUCKETS, rest, 0)


def correction(values, down, upward, p_col, e_col):
    shape = (BINS, LEV, GY)
    p_wide = lanes([p_col[...], p_col[...]]).reshape(shape)
    e_wide = lanes([e_col[...], e_col[...]]).reshape(shape)
    result = values.reshape(shape) + p_wide * down[:, None, :] + e_wide * upward[:, None, :]
    return result.reshape(ROWS, GY)


PARTS = (((0, 3), (3, 2), (5, 3)), ((0, 2), (2, 3), (5, 3)))
PLACE = (0, 2, 3, 4, 5, 6, 7, 1)


def solve_kernel(
    total, first, diffusivity, wind, triple, p_col, e_col, factors, kept, turned,
    second, down_out, up_out,
    ext, fixed, diff_s, wind_s, sum_s, beside, edge, seen, seen_halo, edge_w, edge2, seen2, edge3, seen_halo2, carry,
    load_sem, lev_send, lev_recv, diag_send, diag_recv, halo_send, halo_recv, side_send, side_recv,
):
    me, level = lax.axis_index("xy"), lax.axis_index("lev")
    above, below = lax.rem(me + 1, N_XY), lax.rem(me + N_XY - 1, N_XY)
    barrier = pltpu.get_barrier_semaphore()

    def greet(where, least):
        for k in range(least, N_LEV):
            device = {"xy": where, "lev": lax.rem(level + k, N_LEV)}
            pl.semaphore_signal(barrier, inc=1, device_id=device, device_id_type=MESH)

    greet(me, 1)
    pl.when(me < N_XY - 1)(lambda: greet(above, 0))
    pl.when(me > 0)(lambda: greet(below, 0))
    sides = jnp.where(me < N_XY - 1, 1, 0) + jnp.where(me > 0, 1, 0)
    loads = plane_copies(diffusivity, diff_s, load_sem.at[0]) + plane_copies(wind, wind_s, load_sem.at[1])
    for copy in loads:
        copy.start()
    def product(values):
        high = values.astype(BF16)
        low = (values - high.astype(F32)).astype(BF16)
        return jnp.dot(triple[...], jnp.concatenate([high, low, high], axis=0), preferred_element_type=F32)

    def both(i):
        return lanes([factors[i], factors[i]])

    def edges(values, target, place):
        blocks = values.reshape(BINS, LEV, GY)
        last, start = blocks[:, LEV - 1, :], blocks[:, 0, :]
        target[0, place] = last
        target[1, place] = start + both(10) * last

    def carries(tail, seen_at):
        down = jnp.zeros((BINS, GY), F32)
        upward = jnp.zeros((BINS, GY), F32)
        for f in range(N_LEV):
            here = jnp.where(level == f, 0.0, seen_at(f))
            down += both(f) * here
            upward += both(N_LEV + f) * here
        return down, upward + both(8) * tail + both(9) * down

    def tail_of(values):
        return values.reshape(BINS, LEV, GY)[:, LEV - 1, :]

    def peer_of(k):
        return lax.rem(level + k, N_LEV)

    def back(k):
        return lax.rem(level + N_LEV - k, N_LEV)

    def kind(k):
        return jnp.where(peer_of(k) > level, 0, 1)

    def lev_copies(turn, part, own):
        source, target = ((edge, seen), (edge2, seen2))[turn]
        span = pl.ds(*PARTS[turn][part])
        return [
            remote(
                source.at[kind(k), span], target.at[level if own else back(k), span],
                lev_send.at[turn, part, k], lev_recv.at[turn, part, k], {"xy": me, "lev": peer_of(k)},
            )
            for k in range(1, N_LEV)
        ]

    def diag_copies(turn, own):
        source, target = ((edge, seen_halo), (edge3, seen_halo2))[turn]
        return [
            remote(
                source.at[kind(k) if k else 0, ((GX - 1, 0), (1, 0))[turn][side]], target.at[side, level if own else back(k)],
                diag_send.at[turn, side, k], diag_recv.at[turn, side, k], {"xy": where, "lev": peer_of(k)},
            )
            for side, where in enumerate((above, below))
            for k in range(turn, N_LEV)
        ]

    def start(copies):
        for copy in copies:
            copy.start()

    def wait(copies):
        for copy in copies:
            copy.wait()

    def solve_plane(x, place):
        counts = total[x, BINS]
        share = counts / (counts + 2.0)
        old = first[x].reshape(BINS, LEV, GY)
        blended = (1.0 - share)[None] * old + share[None] * total[x, 0:BINS]
        solved = product(blended.reshape(ROWS, GY))
        ext[x + 1] = solved
        edges(solved, edge, place)

    def some(function, begin, count, shift):
        def one(i, unused):
            function(i, i + shift)
            return unused

        lax.fori_loop(begin, begin + count, one, 0, unroll=count)

    some(solve_plane, 0, 3, 0)
    some(solve_plane, 3, 2, 0)
    some(solve_plane, 5, 3, 0)
    wait(loads)
    sum_s[...] = diff_s[0] + wind_s[0]
    pl.semaphore_wait(barrier, N_LEV - 1 + N_LEV * sides)
    halos = [
        remote(ext.at[GX], ext.at[0], halo_send.at[0], halo_recv.at[0], {"xy": above, "lev": level}),
        remote(ext.at[1], ext.at[GX + 1], halo_send.at[1], halo_recv.at[1], {"xy": below, "lev": level}),
    ]
    weights = [
        remote(diff_s.at[GX - 1], beside.at[0], side_send.at[0], side_recv.at[0], {"xy": above, "lev": level}),
        remote(sum_s, beside.at[1], side_send.at[1], side_recv.at[1], {"xy": below, "lev": level}),
    ]
    sent, seen_in = diag_copies(0, True), diag_copies(0, False)
    sent2, seen_in2 = diag_copies(1, True), diag_copies(1, False)
    three = N_LEV - 1
    for part in range(3):
        start(lev_copies(0, part, True))
    at_edges(me, sent[:N_LEV], sent[N_LEV:], "start")
    at_edges(me, weights[:1], weights[1:], "start")
    at_edges(me, halos[:1], halos[1:], "start")

    def early_plane(x, before, after):
        edges(product(stencil(ext[x + 1], before, after, diff_s[x], wind_s[x])), edge_w, x)

    nothing = jnp.zeros((ROWS, GY), F32)
    early_plane(0, nothing, ext[2])
    some(lambda x, place: early_plane(x, ext[x], ext[x + 2]), 1, 3, 0)
    some(lambda x, place: early_plane(x, ext[x], ext[x + 2]), 4, 3, 0)
    early_plane(GX - 1, ext[GX - 1], nothing)

    def scaled(plane, values):
        return (plane[None] * values.reshape(BINS, LEV, GY)).reshape(ROWS, GY)

    def share_up():
        edges(product(scaled(beside[1], ext[GX])), edge3, 1)
        start(sent2[:three])

    def share_down():
        edges(product(scaled(beside[0], ext[1])), edge3, 0)
        start(sent2[three:])

    at_edges(me, weights[:1], weights[1:], "wait")
    pl.when(me < N_XY - 1)(share_up)
    pl.when(me > 0)(share_down)

    def keep_carries(at, found):
        carry[0, at] = found[0]
        carry[1, at] = found[1]

    def halo_carries(side):
        keep_carries(side * (GX + 1), carries(seen_halo[side, level], lambda f: seen_halo[side, f]))

    def no_carries(side):
        keep_carries(side * (GX + 1), (jnp.zeros((BINS, GY), F32),) * 2)

    def plane_carries(begin, end):
        for x in range(begin, end):
            keep_carries(x + 1, carries(edge[0, x], lambda f: seen[f, x]))

    lane = lax.broadcasted_iota(I32, (BINS, GY), 1)

    def late_edges(x):
        added = [jnp.zeros((BINS, GY), F32)] * 2
        for v in range(2):
            here, before = carry[v, x + 1], carry[v, x]
            left = jnp.where(lane == 0, 0.0, pltpu.roll(here, 1, 1))
            right = jnp.where(lane == GY - 1, 0.0, pltpu.roll(here, GY - 1, 1))
            laplace = carry[v, x + 2] + before + right + left - 4.0 * here
            drift = here - before
            for end in range(2):
                i = 2 * end + v
                keep = lanes([kept[i], kept[i]])
                added[end] += keep * here + turned[0, x, i] * laplace - turned[1, x, i] * drift
        edge2[0, PLACE[x]] = edge_w[0, x] + added[0]
        edge2[1, PLACE[x]] = edge_w[1, x] + added[1] + both(10) * added[0]

    wait(lev_copies(0, 0, False) + lev_copies(0, 1, False))
    plane_carries(0, 5)
    for x in range(1, 4):
        late_edges(x)
    start(lev_copies(1, 1, True))
    wait(lev_copies(0, 2, False))
    plane_carries(5, GX)
    for x in range(4, GX - 1):
        late_edges(x)
    start(lev_copies(1, 2, True))
    at_edges(me, seen_in[:N_LEV], seen_in[N_LEV:], "wait")
    pl.when(me > 0)(lambda: halo_carries(0))
    pl.when(me < N_XY - 1)(lambda: halo_carries(1))
    pl.when(me == 0)(lambda: no_carries(0))
    pl.when(me == N_XY - 1)(lambda: no_carries(1))
    late_edges(0)
    late_edges(GX - 1)
    start(lev_copies(1, 0, True))

    def correct_plane(at, unused):
        fixed[at] = correction(ext[at], carry[0, at], carry[1, at], p_col, e_col)

    def second_plane(x, unused):
        second[x] = product(stencil(fixed[x + 1], fixed[x], fixed[x + 2], diff_s[x], wind_s[x]))

    def no_plane(at):
        fixed[at] = nothing

    some(correct_plane, 1, 4, 0)
    some(correct_plane, 5, 4, 0)
    some(second_plane, 1, 3, 0)
    some(second_plane, 4, 3, 0)
    at_edges(me, halos[:1], halos[1:], "wait")
    pl.when(me > 0)(lambda: correct_plane(0, 0))
    pl.when(me < N_XY - 1)(lambda: correct_plane(GX + 1, 0))
    pl.when(me == 0)(lambda: no_plane(0))
    pl.when(me == N_XY - 1)(lambda: no_plane(GX + 1))
    second_plane(0, 0)
    second_plane(GX - 1, 0)
    at_edges(me, seen_in2[:three], seen_in2[three:], "wait")

    def no_share(side):
        seen_halo2[side] = jnp.zeros((N_LEV, BINS, GY), F32)

    pl.when(me == 0)(lambda: no_share(0))
    pl.when(me == N_XY - 1)(lambda: no_share(1))

    def seen_at(x):
        if x == 0:
            return lambda f: seen2[f, 0] + seen_halo2[0, f]
        if x == GX - 1:
            return lambda f: seen2[f, 1] + seen_halo2[1, f]
        return lambda f: seen2[f, PLACE[x]]

    wait(lev_copies(1, 1, False))
    for x in range(1, 4):
        down, upward = carries(tail_of(second[x]), seen_at(x))
        second[x] = correction(second[x], down, upward, p_col, e_col)
    wait(lev_copies(1, 2, False) + lev_copies(1, 0, False))
    for i, x in enumerate(LATE):
        down, upward = carries(tail_of(second[x]), seen_at(x))
        down_out[i] = down
        up_out[i] = upward


LATE = (4, 5, 6, 0, 7)


def finish_kernel(second, down, upward, p_col, e_col, out, outer, sem):
    inner = [pltpu.make_async_copy(second.at[x], out.at[:, x, :], sem.at[x]) for x in range(1, 4)]
    for copy in inner:
        copy.start()
    last = []
    for i, x in enumerate(LATE):
        outer[i] = correction(second[x], down[i], upward[i], p_col, e_col)
        last.append(pltpu.make_async_copy(outer.at[i], out.at[:, x, :], sem.at[x]))
        last[i].start()
    for copy in inner + last:
        copy.wait()


def vmem(*shape, dtype=F32):
    return pltpu.VMEM(shape, dtype)


def whole(count):
    return [pl.BlockSpec(memory_space=pltpu.VMEM)] * count


def somewhere(count):
    return [pl.BlockSpec(memory_space=pltpu.HBM)] * count


def shaped(*shape, dtype=F32):
    return jax.ShapeDtypeStruct(shape, dtype)


def shards(
    euler_field, parcel_mass, dest_device, dest_cell, diffusivity, wind_speed, inverses, lower_coupling, upper_coupling
):
    dma = pltpu.SemaphoreType.DMA
    euler, mass, dest, cell, diffusivity, wind, inv, low, up = [
        pltpu.with_memory_space_constraint(array, pltpu.HBM)
        for array in (
            euler_field.reshape(ROWS, GX, GY), parcel_mass, dest_device.reshape(32, 128), dest_cell.reshape(32, 128),
            diffusivity, wind_speed, inverses, lower_coupling, upper_coupling,
        )
    ]
    routed = pl.pallas_call(
        route_kernel,
        name="route",
        out_shape=[
            shaped(GX, ROWS, GY), shaped(SETS, UNITS + WIN, 16, 128), shaped(SETS, UNITS + 8, 128),
            shaped(SETS, UNITS + 8, 128), shaped(BUCKETS + 8, 128, dtype=I32), shaped(ROWS, 3 * ROWS, dtype=BF16),
            shaped(ROWS, 128), shaped(ROWS, 128), shaped(11, BINS, 128),
            shaped(4, BINS, 128), shaped(2, GX, 4, BINS, GY),
        ],
        in_specs=somewhere(9),
        out_specs=whole(11),
        scratch_shapes=[
            vmem(N_XY, BINS, CAP), vmem(N_XY, CAP), vmem(N_XY * (BUCKETS + 1), N_XY * BUCKETS, dtype=BF16),
            vmem(N_XY, BLK), vmem(N_XY, BLK), vmem(N_XY, BLK), vmem(N_XY, BLK),
            vmem(GX + 2, ROWS, GY), vmem(GX, LEV, GY), vmem(GX, LEV, GY),
            vmem(BINS, PARC), vmem(32, 128, dtype=I32), vmem(32, 128, dtype=I32),
            vmem(2, BINS, 16, 16), vmem(2, BINS), vmem(2, BINS),
            vmem(N_XY, BINS, CAP), vmem(N_XY, CAP), vmem(1, CAP), vmem(CAP, PARC, dtype=BF16), vmem(N_LEV, 3, BINS, 128),
            dma((3, GX)), dma((6,)), dma((2,)), dma((2,)), dma, dma, dma, dma,
            dma((N_LEV,)), dma((N_LEV,)),
        ],
        compiler_params=pltpu.CompilerParams(collective_id=0, has_side_effects=True, vmem_limit_bytes=LIMIT),
    )(euler, mass, dest, cell, diffusivity, wind, inv, low, up)
    first, rows_u, hl_u, col_u, starts, triple, p_col, e_col, factors, kept, turned = routed
    total = pl.pallas_call(
        deposit_kernel,
        name="deposit",
        out_shape=shaped(GX, BINS + 1, LEV, GY),
        in_specs=whole(4),
        out_specs=pl.BlockSpec(memory_space=pltpu.VMEM),
        scratch_shapes=[pltpu.SMEM((BUCKETS + 8, 128), I32), dma],
        compiler_params=pltpu.CompilerParams(vmem_limit_bytes=LIMIT),
    )(starts, rows_u, hl_u, col_u)
    second, down, upward = pl.pallas_call(
        solve_kernel,
        name="solve",
        out_shape=[shaped(GX, ROWS, GY), shaped(len(LATE), BINS, GY), shaped(len(LATE), BINS, GY)],
        in_specs=whole(2) + somewhere(2) + whole(6),
        out_specs=whole(3),
        scratch_shapes=[
            vmem(GX + 2, ROWS, GY), vmem(GX + 2, ROWS, GY),
            vmem(GX, LEV, GY), vmem(GX, LEV, GY), vmem(LEV, GY), vmem(2, LEV, GY),
            vmem(2, GX, BINS, GY), vmem(N_LEV, GX, BINS, GY), vmem(2, N_LEV, BINS, GY),
            vmem(2, GX, BINS, GY), vmem(2, GX, BINS, GY), vmem(N_LEV, GX, BINS, GY),
            vmem(2, 2, BINS, GY), vmem(2, N_LEV, BINS, GY), vmem(2, GX + 2, BINS, GY),
            dma((2, GX)), dma((2, 3, N_LEV)), dma((2, 3, N_LEV)), dma((2, 2, N_LEV)), dma((2, 2, N_LEV)),
            dma((2,)), dma((2,)), dma((2,)), dma((2,)),
        ],
        compiler_params=pltpu.CompilerParams(collective_id=1, has_side_effects=True, vmem_limit_bytes=LIMIT),
    )(total, first, diffusivity, wind, triple, p_col, e_col, factors, kept, turned)
    result = pl.pallas_call(
        finish_kernel,
        name="finish",
        out_shape=shaped(ROWS, GX, GY),
        in_specs=whole(5),
        out_specs=pl.BlockSpec(memory_space=pltpu.HBM),
        scratch_shapes=[vmem(len(LATE), ROWS, GY), dma((GX,))],
        compiler_params=pltpu.CompilerParams(vmem_limit_bytes=LIMIT),
    )(second, down, upward, p_col, e_col)
    return result.reshape(BINS, LEV, GX, GY)


def solution(mesh):
    placed = (
        P(None, "lev", "xy", None),
        P(None, ("xy", "lev")),
        P(("xy", "lev"), None),
        P(("xy", "lev")),
        P("lev", "xy", None),
        P("lev", "xy", None),
        P("lev", None, None, None),
        P("lev", None),
        P("lev", None),
    )
    return jax.shard_map(
        shards, mesh=mesh, in_specs=placed, out_specs=P(None, "lev", "xy", None), check_vma=False
    )
```

```python
import functools

import jax
import jax.numpy as jnp
from jax import lax
from jax.experimental import pallas as pl
from jax.experimental.pallas import tpu as pltpu
from jax.sharding import PartitionSpec as P

F32, BF16, I32 = jnp.float32, jnp.bfloat16, jnp.int32
MESH = pl.DeviceIdType.MESH
N_XY, N_LEV, BINS, LEV, GX, GY = 32, 4, 8, 32, 8, 256
ROWS = BINS * LEV
PARC, CAP, BLK = 4096, 256, 256
BUCKETS = 16
NT = (((1,), (1,)), ((), ()))
LIMIT = 24 << 20
SETS = 2
SRC = N_XY // SETS
SPAN = SRC * CAP
UNITS = SPAN // 128
WIN = 4


def iota(shape, dim, dtype=F32):
    return lax.broadcasted_iota(I32, shape, dim).astype(dtype)


def ranks(keys, count, lower):
    n = keys.shape[0]
    masks = [jnp.where(keys == k, 1.0, 0.0) for k in range(count)]
    stack = jnp.concatenate(masks, axis=0).astype(BF16)
    before = (iota((BLK, BLK), 0) < iota((BLK, BLK), 1)).astype(BF16)
    inside = jnp.dot(stack, before, preferred_element_type=F32)
    totals = jnp.dot(stack, jnp.ones((BLK, 128), BF16), preferred_element_type=F32)
    base = jnp.dot(lower, totals.astype(BF16), preferred_element_type=F32)
    wide = jnp.concatenate([base, base], axis=1)
    whole = inside + wide[: inside.shape[0]]
    position = jnp.zeros(keys.shape, F32)
    for k in range(count):
        position += masks[k] * whole[k * n : (k + 1) * n]
    return position, base


def lanes(pieces):
    return jnp.concatenate(pieces, axis=1)


def one_hot(row):
    width = row.shape[1]
    wide = jnp.broadcast_to(row, (BLK, width)).astype(BF16)
    ids = iota((BLK, width), 0, BF16)
    return jnp.where(ids == wide, jnp.ones((BLK, width), BF16), jnp.zeros((BLK, width), BF16))


def sort_slots(values16, high_low, column, target, spot, first, count):
    width = target.shape[1]
    chosen = jnp.broadcast_to(target, (16, width)).astype(BF16)
    zero = jnp.zeros((16, width), BF16)
    parts = [jnp.where(chosen == jnp.array(first + d, BF16), values16, zero) for d in range(count)]
    mine = iota((count, width), 0) + float(first) == target
    codes = jnp.concatenate([jnp.where(mine, high_low, 0.0), jnp.where(mine, column, 0.0)], axis=0)
    weighted = jnp.concatenate(parts + [codes.astype(BF16)], axis=0)
    return lax.dot_general(weighted, spot, NT, preferred_element_type=F32)


def two_parts(values):
    high = values.astype(BF16).astype(F32)
    return jnp.concatenate([high, values - high], axis=0).astype(BF16)


def stencil(centre, before, after, diffusivity, wind):
    shape = (BINS, LEV, GY)
    lane = lax.broadcasted_iota(I32, (ROWS, GY), 1)
    left = jnp.where(lane == 0, 0.0, pltpu.roll(centre, 1, 1))
    right = jnp.where(lane == GY - 1, 0.0, pltpu.roll(centre, GY - 1, 1))
    laplace = (after + before + right + left - 4.0 * centre).reshape(shape)
    drift = (centre - before).reshape(shape)
    result = centre.reshape(shape) + diffusivity[None] * laplace - wind[None] * drift
    return result.reshape(ROWS, GY)


def at_edges(me, upward, downward, action):
    @pl.when(me < N_XY - 1)
    def _():
        for copy in upward:
            copy.start() if action == "start" else copy.wait_send()
        for copy in downward if action == "wait" else []:
            copy.wait_recv()

    @pl.when(me > 0)
    def _():
        for copy in downward:
            copy.start() if action == "start" else copy.wait_send()
        for copy in upward if action == "wait" else []:
            copy.wait_recv()


def plane_copies(source, target, sems, at=0):
    return [pltpu.make_async_copy(source.at[:, x, :], target.at[at + x], sems.at[x]) for x in range(GX)]


def remote(src, dst, send, recv, device):
    return pltpu.make_async_remote_copy(
        src_ref=src, dst_ref=dst, send_sem=send, recv_sem=recv, device_id=device, device_id_type=MESH
    )


def compose(inv, low, up, triple, p_ref, e_ref):
    lane16 = lax.broadcasted_iota(I32, (16, ROWS), 1) % LEV
    row16 = lax.broadcasted_iota(I32, (16, ROWS), 0)
    own = lax.broadcasted_iota(I32, (BINS, 16, ROWS), 0) == (
        lax.broadcasted_iota(I32, (BINS, 16, ROWS), 2) // LEV
    )

    def spread(group):
        place = (lane16 == row16 + 16 * group).astype(F32)
        flat = inv[group].reshape(BINS * 16, 16)
        full = jnp.dot(flat, place, precision=lax.Precision.HIGHEST, preferred_element_type=F32)
        return jnp.where(own, full.reshape(BINS, 16, ROWS), 0.0)

    def per_bin(ref, group):
        wide = jnp.broadcast_to(ref[group : group + 1, :].reshape(1, 1, BINS), (BINS, 1, BINS))
        same = lax.broadcasted_iota(I32, (BINS, 1, BINS), 0) == lax.broadcasted_iota(
            I32, (BINS, 1, BINS), 2
        )
        return jnp.sum(jnp.where(same, wide, 0.0), axis=2, keepdims=True)

    t0, t1 = spread(0), spread(1)
    l0, l1, u0, u1 = per_bin(low, 0), per_bin(low, 1), per_bin(up, 0), per_bin(up, 1)
    m0, m1 = inv[0], inv[1]
    m0_first, m0_last = m0[:, :, 0:1], m0[:, :, 15:16]
    m1_first, m1_last = m1[:, :, 0:1], m1[:, :, 15:16]
    tail0 = t0[:, 15:16, :]
    link = (l1 * m1[:, 0:1, 0:1]) * tail0 + t1[:, 0:1, :]
    p0 = t0 + (u0 * m0_last) * link
    p1 = t1 + (l1 * m1_first) * tail0
    full = jnp.concatenate([p0, p1], axis=1).reshape(ROWS, ROWS)
    high = full.astype(BF16)
    triple[:, 0:ROWS] = high
    triple[:, ROWS : 2 * ROWS] = high
    triple[:, 2 * ROWS :] = (full - high.astype(F32)).astype(BF16)
    passed = l1 * l0 * m0[:, 15:16, 0:1]
    c0 = l0 * m0_first + (u0 * m0_last) * (passed * m1[:, 0:1, 0:1])
    c1 = passed * m1_first
    d0 = (u0 * u1 * m1[:, 0:1, 15:16]) * m0_last
    d1 = u1 * m1_last
    p_ref[...] = jnp.broadcast_to(jnp.concatenate([c0, c1], axis=1), (BINS, LEV, 128)).reshape(ROWS, 128)
    e_ref[...] = jnp.broadcast_to(jnp.concatenate([d0, d1], axis=1), (BINS, LEV, 128)).reshape(ROWS, 128)
    blocks = full.reshape(BINS, LEV, ROWS)
    eye = lax.broadcasted_iota(I32, (ROWS, ROWS), 0) == lax.broadcasted_iota(I32, (ROWS, ROWS), 1)
    across = [jnp.sum(jnp.where(eye, lanes([ref[...], ref[...]]), 0.0), axis=0, keepdims=True) for ref in (p_ref, e_ref)]
    rows = jnp.concatenate([blocks[:, at, :] * col for at in (LEV - 1, 0) for col in across], axis=0)
    fold = (
        lax.broadcasted_iota(I32, (ROWS, LEV), 0) % LEV == lax.broadcasted_iota(I32, (ROWS, LEV), 1)
    ).astype(F32)
    return jnp.dot(rows, fold, precision=lax.Precision.HIGHEST, preferred_element_type=F32)


def carry_factors(level, all_ref, out_ref):
    alpha = [all_ref[f, 0] for f in range(N_LEV)]
    beta = [all_ref[f, 1] for f in range(N_LEV)]
    gamma = [all_ref[f, 2] for f in range(N_LEV)]
    zero, one = jnp.zeros((BINS, 128), F32), jnp.ones((BINS, 128), F32)
    for f in range(N_LEV):
        down, product = zero, one
        for i in range(f + 1, N_LEV):
            down = jnp.where(level == i, product, down)
            product = product * alpha[i]
        upward, product = zero, one
        for i in range(f - 1, -1, -1):
            upward = jnp.where(level == i, product, upward)
            product = product * beta[i]
        out_ref[f] = down
        out_ref[N_LEV + f] = upward
    sigma = [zero] * N_LEV
    for f in range(N_LEV - 1, 0, -1):
        sigma[f - 1] = gamma[f] + beta[f] * alpha[f] * sigma[f]

    def own(values):
        result = values[0]
        for f in range(1, N_LEV):
            result = jnp.where(level == f, values[f], result)
        return result

    out_ref[8] = own(sigma)
    out_ref[9] = own([sigma[f] * alpha[f] for f in range(N_LEV)])
    out_ref[10] = own([sigma[f] * beta[f] for f in range(N_LEV)])


def route_kernel(
    euler, mass, dest, cell, diffusivity, wind, inv, low, up,
    first, rows_u, hl_u, col_u, starts_v, triple, p_col, e_col, factors, kept, turned,
    got_mass, got_code, order, hp_s, lp_s, hl_s, col_s, ext, diff_s, wind_s, mass_s, dest_in, cell_in, inv_s, low_s, up_s,
    send_mass, send_code, spare, spot_s, links,
    load_sem, small_sem, halo_send, halo_recv, mass_send, mass_recv, code_send, code_recv, link_send, link_recv,
):
    me, level = lax.axis_index("xy"), lax.axis_index("lev")
    barrier = pltpu.get_barrier_semaphore()

    def greet(k, unused):
        pl.semaphore_signal(
            barrier, inc=1, device_id={"xy": lax.rem(me + k, N_XY), "lev": level}, device_id_type=MESH
        )
        return unused

    lax.fori_loop(1, N_XY, greet, 0)
    for k in range(1, N_LEV):
        pl.semaphore_signal(
            barrier, inc=1, device_id={"xy": me, "lev": lax.rem(level + k, N_LEV)}, device_id_type=MESH
        )

    small = [
        pltpu.make_async_copy(source, target, small_sem.at[i])
        for i, (source, target) in enumerate(
            [(dest, dest_in), (cell, cell_in), (mass, mass_s), (inv, inv_s), (low, low_s), (up, up_s)]
        )
    ]
    field = plane_copies(euler, ext, load_sem.at[0], 1)
    coefficients = plane_copies(diffusivity, diff_s, load_sem.at[1]) + plane_copies(wind, wind_s, load_sem.at[2])
    for copy in small[:3]:
        copy.start()

    above, below = lax.rem(me + 1, N_XY), lax.rem(me + N_XY - 1, N_XY)
    up_copy = remote(euler.at[:, GX - 1, :], ext.at[0], halo_send.at[0], halo_recv.at[0], {"xy": above, "lev": level})
    down_copy = remote(euler.at[:, 0, :], ext.at[GX + 1], halo_send.at[1], halo_recv.at[1], {"xy": below, "lev": level})
    def wide(ref):
        return lanes([ref[pl.ds(0, 16, stride=2), :], ref[pl.ds(1, 16, stride=2), :]])

    def flat(rows):
        return lanes([rows[i : i + 1] for i in range(16)])

    for copy in small[:3]:
        copy.wait()
    target = wide(dest_in).astype(F32)
    cells = wide(cell_in)
    levels = cells // (GX * GY)
    bucket = (cells // GY) % GX * 2 + levels // 16
    high_low = flat((bucket * 16 + levels % 16 + 1).astype(F32))
    column = flat((cells % GY).astype(F32))
    r, c = (lax.broadcasted_iota(I32, (512, 512), d) for d in (0, 1))
    lower = jnp.where((c < r) & (c // 16 == r // 16), 1.0, 0.0).astype(BF16)
    slot, unused_base = ranks(target, N_XY, lower)
    for copy in small[3:] + field + coefficients:
        copy.start()
    spot_s[...] = one_hot(flat(slot))
    values = two_parts(mass_s[...])
    flat_target = flat(target)

    def mass_copy(other):
        device = {"xy": other, "lev": level}
        return remote(send_mass.at[other], got_mass.at[me], mass_send, mass_recv, device)

    def code_copy(other):
        source, target = send_code.at[pl.ds(other, 1)], got_code.at[pl.ds(me, 1)]
        return remote(source, target, code_send, code_recv, {"xy": other, "lev": level})

    table = sort_slots(values, high_low, column, flat_target, spot_s[...], 0, N_XY)
    masses = table[: 16 * N_XY].reshape(N_XY, 16, CAP)
    send_mass[...] = masses[:, :8] + masses[:, 8:]
    send_code[...] = table[16 * N_XY : 17 * N_XY] * 256.0 + table[17 * N_XY :]
    pl.semaphore_wait(barrier, N_XY - 1 + N_LEV - 1)

    def send(k, unused):
        mass_copy(lax.rem(me + k, N_XY)).start()
        return unused

    def send_codes(k, unused):
        code_copy(lax.rem(me + k, N_XY)).start()
        return unused

    lax.fori_loop(1, N_XY, send_codes, 0)
    lax.fori_loop(1, N_XY, send, 0)
    at_edges(me, [up_copy], [down_copy], "start")
    got_mass[me] = send_mass[me]
    pltpu.make_async_copy(send_code.at[pl.ds(me, 1)], got_code.at[pl.ds(me, 1)], code_recv).start()
    pltpu.make_async_copy(send_code.at[pl.ds(me, 1)], spare, code_send).start()

    for copy in small[3:]:
        copy.wait()
    edge_matrix = compose(inv_s, low_s, up_s, triple, p_col, e_col)
    r, c = (lax.broadcasted_iota(I32, (N_XY * (BUCKETS + 1), N_XY * BUCKETS), d) for d in (0, 1))
    order[...] = jnp.where((c < r) & (c % N_XY // SRC == r % N_XY // SRC), 1.0, 0.0).astype(BF16)
    links[level, 0] = p_col[pl.ds(LEV - 1, BINS, stride=LEV), :]
    links[level, 1] = e_col[pl.ds(0, BINS, stride=LEV), :]
    links[level, 2] = p_col[pl.ds(0, BINS, stride=LEV), :]

    def link_copy(k, owner):
        peer = lax.rem(level + k, N_LEV)
        return remote(
            links.at[owner], links.at[owner], link_send.at[k], link_recv.at[k], {"xy": me, "lev": peer}
        )

    for k in range(1, N_LEV):
        link_copy(k, level).start()

    for copy in field + coefficients:
        copy.wait()

    def step(x, unused):
        first[x] = stencil(ext[x + 1], ext[x], ext[x + 2], diff_s[x], wind_s[x])
        return unused

    lax.fori_loop(1, GX - 1, step, 0)
    nothing = jnp.zeros((ROWS, GY), F32)
    first[0] = stencil(ext[1], nothing, ext[2], diff_s[0], wind_s[0])
    first[GX - 1] = stencil(ext[GX], ext[GX - 1], nothing, diff_s[GX - 1], wind_s[GX - 1])

    kept[...] = jnp.broadcast_to(jnp.sum(edge_matrix, axis=1, keepdims=True), (4 * BINS, 128)).reshape(4, BINS, 128)
    high = edge_matrix.astype(BF16)
    low = (edge_matrix - high.astype(F32)).astype(BF16)
    three_parts = lanes([high, high, low])

    def turn(x, unused):
        for i, ref in enumerate((diff_s, wind_s)):
            top = ref[x].astype(BF16)
            rest = (ref[x] - top.astype(F32)).astype(BF16)
            result = jnp.dot(three_parts, jnp.concatenate([top, rest, top], axis=0), preferred_element_type=F32)
            turned[i, x] = result.reshape(4, BINS, GY)
        return unused

    lax.fori_loop(0, GX, turn, 0, unroll=2)
    for k in range(1, N_LEV):
        link_copy(k, lax.rem(level + N_LEV - k, N_LEV)).wait()
    carry_factors(level, links, factors)

    remote(send_code, got_code, code_send, code_recv, {"xy": above, "lev": level}).wait()
    code = got_code[...].astype(I32)
    hl = code // 256
    col = code % 256
    valid = hl > 0
    key = jnp.where(valid, (hl - 1) // 16, -1).astype(F32)
    hl_s[...] = hl.astype(F32)
    col_s[...] = col.astype(F32)
    position, base = ranks(key, BUCKETS, order[...])
    place = position.astype(I32)
    hp_s[...] = jnp.where(valid, place // BLK, -1).astype(F32)
    lp_s[...] = (place % BLK).astype(F32)
    lane = lax.broadcasted_iota(I32, (1, 128), 1)
    longest = jnp.zeros((1, 128), I32)
    before = None
    for k in range(BUCKETS + 1):
        start = jnp.zeros((1, 128), F32)
        for g in range(SETS):
            at = N_XY * k + SRC * g
            start = jnp.where(lane == g, base[at : at + 1, :], start)
        start = start.astype(I32)
        starts_v[k : k + 1, :] = start
        if k:
            longest = jnp.maximum(longest, start - before // 128 * 128)
        before = start
    starts_v[BUCKETS + 1 : BUCKETS + 2, :] = longest

    others = pl.ds(0, N_XY - 1)
    remote(send_mass.at[others], got_mass.at[others], mass_send, mass_recv, {"xy": above, "lev": level}).wait()

    def one_set(g, unused):
        take = lambda ref: lanes([ref[pl.ds(g * SRC + i, 1), :] for i in range(SRC)])
        values = lanes([two_parts(got_mass[g * SRC + i]) for i in range(SRC)])
        table = sort_slots(values, take(hl_s), take(col_s), take(hp_s), one_hot(take(lp_s)), 0, SRC)
        for half in range(2):
            side = slice(128 * half, 128 * half + 128)
            for d in range(SRC):
                rows_u[g, 2 * d + half] = table[16 * d : 16 * d + 16, side]
            hl_u[g, pl.ds(half, SRC, stride=2), :] = table[16 * SRC : 17 * SRC, side]
            col_u[g, pl.ds(half, SRC, stride=2), :] = table[17 * SRC : 18 * SRC, side]
        rows_u[g, UNITS:] = jnp.zeros((WIN, 16, 128), F32)
        hl_u[g, UNITS:, :] = jnp.zeros((8, 128), F32)
        col_u[g, UNITS:, :] = jnp.zeros((8, 128), F32)
        return unused

    lax.fori_loop(0, SETS, one_set, 0)
    at_edges(me, [up_copy], [down_copy], "wait")

    def add_halo(x, at, weight):
        first[x] += (weight[None] * ext[at].reshape(BINS, LEV, GY)).reshape(ROWS, GY)

    pl.when(me > 0)(lambda: add_halo(0, 0, diff_s[0] + wind_s[0]))
    pl.when(me < N_XY - 1)(lambda: add_halo(GX - 1, GX + 1, diff_s[GX - 1]))


def deposit_kernel(starts_v, rows_u, hl_u, col_u, total, starts_s, sem):
    to_scalars = pltpu.make_async_copy(starts_v, starts_s, sem)
    to_scalars.start()
    to_scalars.wait()

    def place_of(k):
        return k // 2, pl.ds(pl.multiple_of((k % 2) * 16, 16), 16)

    def window(k, t):
        first_code = (k * 16 + 1).astype(F32)
        at = [jnp.minimum(starts_s[k, g] // 128 + WIN * t, UNITS) for g in range(SETS)]
        units = [(g, at[g] + i) for g in range(SETS) for i in range(WIN)]
        hl_row = lanes([hl_u[g, pl.ds(u, 1), :] for g, u in units])
        col_row = lanes([col_u[g, pl.ds(u, 1), :] for g, u in units])
        rows = lanes([rows_u[g, u] for g, u in units])
        width = 128 * WIN * SETS
        mine = jnp.broadcast_to(hl_row, (16, width)) == iota((16, width), 0) + first_code
        spread = [jnp.where(mine, jnp.broadcast_to(rows[q : q + 1, :], (16, width)), 0.0) for q in range(16)]
        spread.insert(8, jnp.where(mine, 1.0, 0.0))
        weighted = jnp.concatenate(spread, axis=0).astype(BF16)
        table = lax.dot_general(weighted, one_hot(col_row), NT, preferred_element_type=F32)
        table = table.reshape(17, 16, GY)
        return jnp.concatenate([table[:8] + table[9:], table[8:9]], axis=0)

    def one_bucket(k, unused):
        x, levels = place_of(k)
        total[x, :, levels, :] = window(k, 0)
        return unused

    lax.fori_loop(0, BUCKETS, one_bucket, 0, unroll=16)

    def rest(k, unused):
        x, levels = place_of(k)
        rounds = jnp.int32(1)
        for g in range(SETS):
            span = starts_s[k + 1, g] - starts_s[k, g] // 128 * 128
            rounds = jnp.maximum(rounds, (span + 128 * WIN - 1) // (128 * WIN))

        def again(t, unused):
            total[x, :, levels, :] += window(k, t)
            return unused

        lax.fori_loop(1, rounds, again, 0)
        return unused

    most = starts_s[BUCKETS + 1, 0]
    for g in range(1, SETS):
        most = jnp.maximum(most, starts_s[BUCKETS + 1, g])

    @pl.when(most > 128 * WIN)
    def _():
        lax.fori_loop(0, BUCKETS, rest, 0)


def correction(values, down, upward, p_col, e_col):
    shape = (BINS, LEV, GY)
    p_wide = lanes([p_col[...], p_col[...]]).reshape(shape)
    e_wide = lanes([e_col[...], e_col[...]]).reshape(shape)
    result = values.reshape(shape) + p_wide * down[:, None, :] + e_wide * upward[:, None, :]
    return result.reshape(ROWS, GY)


PARTS = (((0, 3), (3, 2), (5, 3)), ((0, 2), (2, 3), (5, 3)))
PLACE = (0, 2, 3, 4, 5, 6, 7, 1)


def solve_kernel(
    total, first, diffusivity, wind, triple, p_col, e_col, factors, kept, turned,
    second, down_out, up_out,
    ext, fixed, diff_s, wind_s, sum_s, beside, edge, seen, seen_halo, edge_w, edge2, seen2, edge3, seen_halo2, carry,
    load_sem, lev_send, lev_recv, diag_send, diag_recv, halo_send, halo_recv, side_send, side_recv,
):
    me, level = lax.axis_index("xy"), lax.axis_index("lev")
    above, below = lax.rem(me + 1, N_XY), lax.rem(me + N_XY - 1, N_XY)
    barrier = pltpu.get_barrier_semaphore()

    def greet(where, least):
        for k in range(least, N_LEV):
            device = {"xy": where, "lev": lax.rem(level + k, N_LEV)}
            pl.semaphore_signal(barrier, inc=1, device_id=device, device_id_type=MESH)

    greet(me, 1)
    pl.when(me < N_XY - 1)(lambda: greet(above, 0))
    pl.when(me > 0)(lambda: greet(below, 0))
    sides = jnp.where(me < N_XY - 1, 1, 0) + jnp.where(me > 0, 1, 0)
    loads = plane_copies(diffusivity, diff_s, load_sem.at[0]) + plane_copies(wind, wind_s, load_sem.at[1])
    for copy in loads:
        copy.start()
    def product(values):
        high = values.astype(BF16)
        low = (values - high.astype(F32)).astype(BF16)
        return jnp.dot(triple[...], jnp.concatenate([high, low, high], axis=0), preferred_element_type=F32)

    def both(i):
        return lanes([factors[i], factors[i]])

    def edges(values, target, place):
        blocks = values.reshape(BINS, LEV, GY)
        last, start = blocks[:, LEV - 1, :], blocks[:, 0, :]
        target[0, place] = last
        target[1, place] = start + both(10) * last

    def carries(tail, seen_at):
        down = jnp.zeros((BINS, GY), F32)
        upward = jnp.zeros((BINS, GY), F32)
        for f in range(N_LEV):
            here = jnp.where(level == f, 0.0, seen_at(f))
            down += both(f) * here
            upward += both(N_LEV + f) * here
        return down, upward + both(8) * tail + both(9) * down

    def tail_of(values):
        return values.reshape(BINS, LEV, GY)[:, LEV - 1, :]

    def peer_of(k):
        return lax.rem(level + k, N_LEV)

    def back(k):
        return lax.rem(level + N_LEV - k, N_LEV)

    def kind(k):
        return jnp.where(peer_of(k) > level, 0, 1)

    def lev_copies(turn, part, own):
        source, target = ((edge, seen), (edge2, seen2))[turn]
        span = pl.ds(*PARTS[turn][part])
        return [
            remote(
                source.at[kind(k), span], target.at[level if own else back(k), span],
                lev_send.at[turn, part, k], lev_recv.at[turn, part, k], {"xy": me, "lev": peer_of(k)},
            )
            for k in range(1, N_LEV)
        ]

    def diag_copies(turn, own):
        source, target = ((edge, seen_halo), (edge3, seen_halo2))[turn]
        return [
            remote(
                source.at[kind(k) if k else 0, ((GX - 1, 0), (1, 0))[turn][side]], target.at[side, level if own else back(k)],
                diag_send.at[turn, side, k], diag_recv.at[turn, side, k], {"xy": where, "lev": peer_of(k)},
            )
            for side, where in enumerate((above, below))
            for k in range(turn, N_LEV)
        ]

    def start(copies):
        for copy in copies:
            copy.start()

    def wait(copies):
        for copy in copies:
            copy.wait()

    def solve_plane(x, place):
        counts = total[x, BINS]
        share = counts / (counts + 2.0)
        old = first[x].reshape(BINS, LEV, GY)
        blended = (1.0 - share)[None] * old + share[None] * total[x, 0:BINS]
        solved = product(blended.reshape(ROWS, GY))
        ext[x + 1] = solved
        edges(solved, edge, place)

    def some(function, begin, count, shift):
        def one(i, unused):
            function(i, i + shift)
            return unused

        lax.fori_loop(begin, begin + count, one, 0, unroll=count)

    some(solve_plane, 0, 3, 0)
    some(solve_plane, 3, 2, 0)
    some(solve_plane, 5, 3, 0)
    wait(loads)
    sum_s[...] = diff_s[0] + wind_s[0]
    pl.semaphore_wait(barrier, N_LEV - 1 + N_LEV * sides)
    halos = [
        remote(ext.at[GX], ext.at[0], halo_send.at[0], halo_recv.at[0], {"xy": above, "lev": level}),
        remote(ext.at[1], ext.at[GX + 1], halo_send.at[1], halo_recv.at[1], {"xy": below, "lev": level}),
    ]
    weights = [
        remote(diff_s.at[GX - 1], beside.at[0], side_send.at[0], side_recv.at[0], {"xy": above, "lev": level}),
        remote(sum_s, beside.at[1], side_send.at[1], side_recv.at[1], {"xy": below, "lev": level}),
    ]
    sent, seen_in = diag_copies(0, True), diag_copies(0, False)
    sent2, seen_in2 = diag_copies(1, True), diag_copies(1, False)
    three = N_LEV - 1
    for part in range(3):
        start(lev_copies(0, part, True))
    at_edges(me, sent[:N_LEV], sent[N_LEV:], "start")
    at_edges(me, weights[:1], weights[1:], "start")
    at_edges(me, halos[:1], halos[1:], "start")

    def early_plane(x, before, after):
        edges(product(stencil(ext[x + 1], before, after, diff_s[x], wind_s[x])), edge_w, x)

    nothing = jnp.zeros((ROWS, GY), F32)
    early_plane(0, nothing, ext[2])
    some(lambda x, place: early_plane(x, ext[x], ext[x + 2]), 1, 3, 0)
    some(lambda x, place: early_plane(x, ext[x], ext[x + 2]), 4, 3, 0)
    early_plane(GX - 1, ext[GX - 1], nothing)

    def scaled(plane, values):
        return (plane[None] * values.reshape(BINS, LEV, GY)).reshape(ROWS, GY)

    def share_up():
        edges(product(scaled(beside[1], ext[GX])), edge3, 1)
        start(sent2[:three])

    def share_down():
        edges(product(scaled(beside[0], ext[1])), edge3, 0)
        start(sent2[three:])

    at_edges(me, weights[:1], weights[1:], "wait")
    pl.when(me < N_XY - 1)(share_up)
    pl.when(me > 0)(share_down)

    def keep_carries(at, found):
        carry[0, at] = found[0]
        carry[1, at] = found[1]

    def halo_carries(side):
        keep_carries(side * (GX + 1), carries(seen_halo[side, level], lambda f: seen_halo[side, f]))

    def no_carries(side):
        keep_carries(side * (GX + 1), (jnp.zeros((BINS, GY), F32),) * 2)

    def plane_carries(begin, end):
        for x in range(begin, end):
            keep_carries(x + 1, carries(edge[0, x], lambda f: seen[f, x]))

    lane = lax.broadcasted_iota(I32, (BINS, GY), 1)

    def late_edges(x):
        added = [jnp.zeros((BINS, GY), F32)] * 2
        for v in range(2):
            here, before = carry[v, x + 1], carry[v, x]
            left = jnp.where(lane == 0, 0.0, pltpu.roll(here, 1, 1))
            right = jnp.where(lane == GY - 1, 0.0, pltpu.roll(here, GY - 1, 1))
            laplace = carry[v, x + 2] + before + right + left - 4.0 * here
            drift = here - before
            for end in range(2):
                i = 2 * end + v
                keep = lanes([kept[i], kept[i]])
                added[end] += keep * here + turned[0, x, i] * laplace - turned[1, x, i] * drift
        edge2[0, PLACE[x]] = edge_w[0, x] + added[0]
        edge2[1, PLACE[x]] = edge_w[1, x] + added[1] + both(10) * added[0]

    wait(lev_copies(0, 0, False) + lev_copies(0, 1, False))
    plane_carries(0, 5)
    for x in range(1, 4):
        late_edges(x)
    start(lev_copies(1, 1, True))
    wait(lev_copies(0, 2, False))
    plane_carries(5, GX)
    for x in range(4, GX - 1):
        late_edges(x)
    start(lev_copies(1, 2, True))
    at_edges(me, seen_in[:N_LEV], seen_in[N_LEV:], "wait")
    pl.when(me > 0)(lambda: halo_carries(0))
    pl.when(me < N_XY - 1)(lambda: halo_carries(1))
    pl.when(me == 0)(lambda: no_carries(0))
    pl.when(me == N_XY - 1)(lambda: no_carries(1))
    late_edges(0)
    late_edges(GX - 1)
    start(lev_copies(1, 0, True))

    def correct_plane(at, unused):
        fixed[at] = correction(ext[at], carry[0, at], carry[1, at], p_col, e_col)

    def second_plane(x, unused):
        second[x] = product(stencil(fixed[x + 1], fixed[x], fixed[x + 2], diff_s[x], wind_s[x]))

    def no_plane(at):
        fixed[at] = nothing

    some(correct_plane, 1, 4, 0)
    some(correct_plane, 5, 4, 0)
    some(second_plane, 1, 3, 0)
    some(second_plane, 4, 3, 0)
    at_edges(me, halos[:1], halos[1:], "wait")
    pl.when(me > 0)(lambda: correct_plane(0, 0))
    pl.when(me < N_XY - 1)(lambda: correct_plane(GX + 1, 0))
    pl.when(me == 0)(lambda: no_plane(0))
    pl.when(me == N_XY - 1)(lambda: no_plane(GX + 1))
    second_plane(0, 0)
    second_plane(GX - 1, 0)
    at_edges(me, seen_in2[:three], seen_in2[three:], "wait")

    def no_share(side):
        seen_halo2[side] = jnp.zeros((N_LEV, BINS, GY), F32)

    pl.when(me == 0)(lambda: no_share(0))
    pl.when(me == N_XY - 1)(lambda: no_share(1))

    def seen_at(x):
        if x == 0:
            return lambda f: seen2[f, 0] + seen_halo2[0, f]
        if x == GX - 1:
            return lambda f: seen2[f, 1] + seen_halo2[1, f]
        return lambda f: seen2[f, PLACE[x]]

    wait(lev_copies(1, 1, False))
    for x in range(1, 4):
        down, upward = carries(tail_of(second[x]), seen_at(x))
        second[x] = correction(second[x], down, upward, p_col, e_col)
    wait(lev_copies(1, 2, False) + lev_copies(1, 0, False))
    for i, x in enumerate(LATE):
        down, upward = carries(tail_of(second[x]), seen_at(x))
        down_out[i] = down
        up_out[i] = upward


LATE = (4, 5, 6, 0, 7)


def finish_kernel(second, down, upward, p_col, e_col, out, outer, sem):
    inner = [pltpu.make_async_copy(second.at[x], out.at[:, x, :], sem.at[x]) for x in range(1, 4)]
    for copy in inner:
        copy.start()
    last = []
    for i, x in enumerate(LATE):
        outer[i] = correction(second[x], down[i], upward[i], p_col, e_col)
        last.append(pltpu.make_async_copy(outer.at[i], out.at[:, x, :], sem.at[x]))
        last[i].start()
    for copy in inner + last:
        copy.wait()


def vmem(*shape, dtype=F32):
    return pltpu.VMEM(shape, dtype)


def whole(count):
    return [pl.BlockSpec(memory_space=pltpu.VMEM)] * count


def somewhere(count):
    return [pl.BlockSpec(memory_space=pltpu.HBM)] * count


def shaped(*shape, dtype=F32):
    return jax.ShapeDtypeStruct(shape, dtype)


def shards(
    euler_field, parcel_mass, dest_device, dest_cell, diffusivity, wind_speed, inverses, lower_coupling, upper_coupling
):
    dma = pltpu.SemaphoreType.DMA
    euler, mass, dest, cell, diffusivity, wind, inv, low, up = [
        pltpu.with_memory_space_constraint(array, pltpu.HBM)
        for array in (
            euler_field.reshape(ROWS, GX, GY), parcel_mass, dest_device.reshape(32, 128), dest_cell.reshape(32, 128),
            diffusivity, wind_speed, inverses, lower_coupling, upper_coupling,
        )
    ]
    routed = pl.pallas_call(
        route_kernel,
        name="route",
        out_shape=[
            shaped(GX, ROWS, GY), shaped(SETS, UNITS + WIN, 16, 128), shaped(SETS, UNITS + 8, 128),
            shaped(SETS, UNITS + 8, 128), shaped(BUCKETS + 8, 128, dtype=I32), shaped(ROWS, 3 * ROWS, dtype=BF16),
            shaped(ROWS, 128), shaped(ROWS, 128), shaped(11, BINS, 128),
            shaped(4, BINS, 128), shaped(2, GX, 4, BINS, GY),
        ],
        in_specs=somewhere(9),
        out_specs=whole(11),
        scratch_shapes=[
            vmem(N_XY, BINS, CAP), vmem(N_XY, CAP), vmem(N_XY * (BUCKETS + 1), N_XY * BUCKETS, dtype=BF16),
            vmem(N_XY, BLK), vmem(N_XY, BLK), vmem(N_XY, BLK), vmem(N_XY, BLK),
            vmem(GX + 2, ROWS, GY), vmem(GX, LEV, GY), vmem(GX, LEV, GY),
            vmem(BINS, PARC), vmem(32, 128, dtype=I32), vmem(32, 128, dtype=I32),
            vmem(2, BINS, 16, 16), vmem(2, BINS), vmem(2, BINS),
            vmem(N_XY, BINS, CAP), vmem(N_XY, CAP), vmem(1, CAP), vmem(CAP, PARC, dtype=BF16), vmem(N_LEV, 3, BINS, 128),
            dma((3, GX)), dma((6,)), dma((2,)), dma((2,)), dma, dma, dma, dma,
            dma((N_LEV,)), dma((N_LEV,)),
        ],
        compiler_params=pltpu.CompilerParams(collective_id=0, has_side_effects=True, vmem_limit_bytes=LIMIT),
    )(euler, mass, dest, cell, diffusivity, wind, inv, low, up)
    first, rows_u, hl_u, col_u, starts, triple, p_col, e_col, factors, kept, turned = routed
    total = pl.pallas_call(
        deposit_kernel,
        name="deposit",
        out_shape=shaped(GX, BINS + 1, LEV, GY),
        in_specs=whole(4),
        out_specs=pl.BlockSpec(memory_space=pltpu.VMEM),
        scratch_shapes=[pltpu.SMEM((BUCKETS + 8, 128), I32), dma],
        compiler_params=pltpu.CompilerParams(vmem_limit_bytes=LIMIT),
    )(starts, rows_u, hl_u, col_u)
    second, down, upward = pl.pallas_call(
        solve_kernel,
        name="solve",
        out_shape=[shaped(GX, ROWS, GY), shaped(len(LATE), BINS, GY), shaped(len(LATE), BINS, GY)],
        in_specs=whole(2) + somewhere(2) + whole(6),
        out_specs=whole(3),
        scratch_shapes=[
            vmem(GX + 2, ROWS, GY), vmem(GX + 2, ROWS, GY),
            vmem(GX, LEV, GY), vmem(GX, LEV, GY), vmem(LEV, GY), vmem(2, LEV, GY),
            vmem(2, GX, BINS, GY), vmem(N_LEV, GX, BINS, GY), vmem(2, N_LEV, BINS, GY),
            vmem(2, GX, BINS, GY), vmem(2, GX, BINS, GY), vmem(N_LEV, GX, BINS, GY),
            vmem(2, 2, BINS, GY), vmem(2, N_LEV, BINS, GY), vmem(2, GX + 2, BINS, GY),
            dma((2, GX)), dma((2, 3, N_LEV)), dma((2, 3, N_LEV)), dma((2, 2, N_LEV)), dma((2, 2, N_LEV)),
            dma((2,)), dma((2,)), dma((2,)), dma((2,)),
        ],
        compiler_params=pltpu.CompilerParams(collective_id=1, has_side_effects=True, vmem_limit_bytes=LIMIT),
    )(total, first, diffusivity, wind, triple, p_col, e_col, factors, kept, turned)
    result = pl.pallas_call(
        finish_kernel,
        name="finish",
        out_shape=shaped(ROWS, GX, GY),
        in_specs=whole(5),
        out_specs=pl.BlockSpec(memory_space=pltpu.HBM),
        scratch_shapes=[vmem(len(LATE), ROWS, GY), dma((GX,))],
        compiler_params=pltpu.CompilerParams(vmem_limit_bytes=LIMIT),
    )(second, down, upward, p_col, e_col)
    return result.reshape(BINS, LEV, GX, GY)


def solution(mesh):
    placed = (
        P(None, "lev", "xy", None),
        P(None, ("xy", "lev")),
        P(("xy", "lev"), None),
        P(("xy", "lev")),
        P("lev", "xy", None),
        P("lev", "xy", None),
        P("lev", None, None, None),
        P("lev", None),
        P("lev", None),
    )
    return jax.shard_map(
        shards, mesh=mesh, in_specs=placed, out_specs=P(None, "lev", "xy", None), check_vma=False
    )
```
